128 devices in a mesh: wide: 32 (over z, x, y_lo), rep: 4 (over y_hi, core).
Axes of the slice: x: 4, y: 4 (y_hi: 2, y_lo: 2; y = y_hi * 2 + y_lo), z: 4, core: 2. Of those that a mesh axis runs over, the one named last changes fastest.
Arguments:
- samples: bfloat16 [16384, 49152], P(('wide', 'rep')), may hold values from -6 to 6
- out_grad: bfloat16 [16384, 24576], P(('wide', 'rep')), may hold values from -0.046875 to 0.046875
- row_ids: int32 [16384, 256], P(('wide', 'rep')), may hold values from 0 to 255
- table_owner: int32 [256], replicated, may hold values from 0 to 255, each once
- slot_map: int32 [256, 256], P('wide'), may hold values from 0 to 2047, as said below
- proj: bfloat16 [256, 16], P('wide'), may hold values from -0.375 to 0.375
- gain_flat: bfloat16 [4096], P('wide'), may hold values from 0.25 to 1.75
- w_in: bfloat16 [4096, 128], P('wide'), may hold values from -0.09375 to 0.09375
- w_out: bfloat16 [12288, 128], P('wide'), may hold values from -0.5 to 0.5
- w_lcb: bfloat16 [256, 64], P('wide'), may hold values from -0.375 to 0.375
- table_rows: float32 [65536, 192], P('wide'), may hold values from -0.6 to 0.6
- row_accum: float32 [65536], P('wide'), may hold values from 0.0001 to 0.01
Outputs:
- proj_grad: float32 [256, 16], P('wide')
- gain_grad: float32 [4096], P('wide')
- w_in_grad: float32 [4096, 128], P('wide')
- w_out_grad: float32 [12288, 128], P('wide')
- w_lcb_grad: float32 [256, 64], P('wide')
- new_rows: float32 [65536, 192], P('wide')
- new_accum: float32 [65536], P('wide')
The draws below stay inside these ranges and needn't reach their ends.
Inputs may be any that keep to these rules, and one draw needn't show every extreme that they name: `table_owner`: each position 0 to 255 once. `slot_map`: within each aligned block of 8 rows every value 0 to 2047 appears once.
All inputs are finite; a program needn't handle non-finite values.
Results may differ from the reference program's by a relative error of at most 0.0065.
Values may be sent and summed in bfloat16 or wider, within the bound.
No kernel may reach another device: no remote copies, remote signals or barrier semaphores. Data moves between devices by JAX's collectives and lax.ppermute only.
A program may use at most 256 MiB of HBM per device.

```python
import math
import jax
import jax.numpy as jnp
from jax import lax

N = 256
D = 192
K = 16
FMH = 128
NF = 64
NL = 64
ROWS = 256
BATCH = 16384
NK = 4096
TABLES_DEV = 8
STATE = 2048


def draw_slot_map(key, part):
    key = jax.random.fold_in(key, 7)
    owners = N // TABLES_DEV
    keys = jax.random.split(key, owners)
    perms = jax.vmap(lambda k: jax.random.permutation(k, STATE))(keys)
    return perms.reshape(N, ROWS).astype(jnp.int32)


def plant(entries, rng, low, high):
    index_at = [jax.random.randint(jax.random.fold_in(rng, axis), (), 0, length) for axis, length in enumerate(entries.shape)]
    longest = entries.shape.index(max(entries.shape))
    beside = index_at[:longest] + [(index_at[longest] + 1) % entries.shape[longest]] + index_at[longest + 1:]
    return entries.at[tuple(index_at)].set(low).at[tuple(beside)].set(high)


def block_scale(key, shape, pieces, low, largest):
    def one(dim, shards_of):
        heights = jax.random.uniform(jax.random.fold_in(jax.random.fold_in(key, 6), dim), (shards_of,), jnp.float32, low / len(pieces), largest / len(pieces))
        return jnp.repeat(jnp.exp(heights), shape[dim] // shards_of).reshape((-1,) + (1,) * (len(shape) - dim - 1))

    loudness = one(*pieces[0])
    for cut in pieces[1:]:
        loudness = loudness * one(*cut)
    return loudness


def noise(rng, dims, scale, limit, cuts=(), kind=jnp.bfloat16):
    gain = block_scale(rng, dims, cuts, -0.22, 0.18) if cuts else 1.0
    array = jax.random.normal(rng, dims, jnp.float32) * scale * gain
    return jnp.minimum(jnp.maximum(array, -limit), limit).astype(kind)


def setup_inputs(seed: int = 0) -> dict:
    splits = jax.random.split(jax.random.key(seed), 13)
    samples = noise(splits[0], (BATCH, N * D), 1.0, 6.0, ((0, 128),))
    out_grad = noise(splits[1], (BATCH, (NF + NL) * D), (BATCH ** -0.5), 0.046875, ((0, 128),))
    row_ids = plant(jax.random.randint(splits[2], (BATCH, N), 0, ROWS), jax.random.fold_in(splits[2], 1), 0, ROWS - 1).astype(jnp.int32)
    table_owner = jax.random.permutation(splits[3], N).astype(jnp.int32)
    slot_map = draw_slot_map(jax.random.fold_in(splits[12], 71), 0)
    proj = noise(splits[5], (N, K), N ** -0.5, 0.375, ((0, 32),))
    gain_flat = jnp.clip(1.0 + 0.15 * jax.random.normal(splits[6], (NK,), jnp.float32), 0.25, 1.75).astype(jnp.bfloat16)
    w_in = noise(splits[7], (NK, FMH), NK ** -0.5, 0.09375, ((0, 32),))
    w_out = noise(splits[8], (NF * D, FMH), FMH ** -0.5, 0.5, ((0, 32),))
    w_lcb = noise(splits[9], (N, NL), N ** -0.5, 0.375, ((0, 32),))
    table_rows = noise(splits[10], (N * ROWS, D), 0.1, 0.6, ((0, 32),), jnp.float32)
    row_accum = jnp.clip(jnp.exp(math.log(0.01) - 4.6051702 * jax.random.uniform(splits[11], (N * ROWS,), jnp.float32) ** block_scale(splits[11], (N * ROWS,), ((0, 32),), -0.2, 0.2)), 0.0001, 0.01)
    return dict(samples=samples, out_grad=out_grad, row_ids=row_ids, table_owner=table_owner, slot_map=slot_map, proj=proj, gain_flat=gain_flat, w_in=w_in, w_out=w_out, w_lcb=w_lcb, table_rows=table_rows, row_accum=row_accum)


LEARN = 0.1
EPS = 1e-05
HIGH = lax.Precision.HIGHEST

def rounded_values(value):
    return lax.optimization_barrier(value.astype(jnp.bfloat16)).astype(jnp.float32)

def layer_grads(x3, grad3, proj, norm_gain, w_in, w_out, w_lcb):
    count = x3.shape[0]
    score = jnp.einsum('bnd,nk->bdk', x3, proj, precision=HIGH)
    flat = jnp.einsum('bnd,bdk->bnk', x3, score, precision=HIGH).reshape(count, NK)
    centered_input = flat - lax.optimization_barrier(jnp.mean(flat, axis=1, keepdims=True))
    inverse_deviation = 1.0 / jnp.sqrt(lax.optimization_barrier(jnp.mean(centered_input * centered_input, axis=1, keepdims=True)) + EPS)
    standardized_input = centered_input * inverse_deviation
    normalized_rows = rounded_values(standardized_input * norm_gain)
    pre = jnp.einsum('bi,ih->bh', normalized_rows, w_in)
    hidden = rounded_values(jax.nn.silu(pre))
    fout = jnp.einsum('bh,jh->bj', hidden, w_out).reshape(count, NF, D)
    lout = jnp.einsum('bnd,nl->bld', x3, w_lcb)
    joined = jnp.concatenate([fout, lout], axis=1)
    mid = joined - lax.optimization_barrier(jnp.mean(joined, axis=2, keepdims=True))
    out_inv = 1.0 / jnp.sqrt(lax.optimization_barrier(jnp.mean(mid * mid, axis=2, keepdims=True)) + EPS)
    chat = mid * out_inv
    dcat = out_inv * (grad3 - lax.optimization_barrier(jnp.mean(grad3, axis=2, keepdims=True)) - chat * lax.optimization_barrier(jnp.mean(grad3 * chat, axis=2, keepdims=True)))
    dfeat = rounded_values(dcat[:, :NF].reshape(count, NF * D))
    dlin = rounded_values(dcat[:, NF:])
    g_out = jnp.einsum('bj,bh->jh', dfeat, hidden)
    g_lcb = jnp.einsum('bnd,bld->nl', x3, dlin)
    sig = jax.nn.sigmoid(pre)
    dpre = rounded_values(jnp.einsum('bj,jh->bh', dfeat, w_out) * sig * (1.0 + pre * (1.0 - sig)))
    g_in = jnp.einsum('bi,bh->ih', normalized_rows, dpre)
    norm_gradient = jnp.einsum('bh,ih->bi', dpre, w_in)
    gain_gradient = lax.optimization_barrier(jnp.sum(norm_gradient * standardized_input, axis=0))
    boundary_value = norm_gradient * norm_gain
    flat_gradient = inverse_deviation * (boundary_value - lax.optimization_barrier(jnp.mean(boundary_value, axis=1, keepdims=True)) - standardized_input * lax.optimization_barrier(jnp.mean(boundary_value * standardized_input, axis=1, keepdims=True)))
    dfm = rounded_values(flat_gradient.reshape(count, N, K))
    dscore = jnp.einsum('bnd,bnk->bdk', x3, dfm, precision=HIGH)
    g_proj = jnp.einsum('bnd,bdk->nk', x3, dscore, precision=HIGH)
    dx3 = jnp.einsum('bnk,bdk->bnd', dfm, score, precision=HIGH) + jnp.einsum('nk,bdk->bnd', proj, dscore, precision=HIGH) + jnp.einsum('nl,bld->bnd', w_lcb, dlin)
    return ((g_proj, gain_gradient, g_in, g_out, g_lcb), rounded_values(dx3))

def reference(samples, out_grad, row_ids, table_owner, slot_map, proj, gain_flat, w_in, w_out, w_lcb, table_rows, row_accum):
    block = math.gcd(BATCH, 512)
    steps = BATCH // block
    xs = samples.astype(jnp.float32).reshape(steps, block, N, D)
    gs = out_grad.astype(jnp.float32).reshape(steps, block, NF + NL, D)
    idx = row_ids.reshape(steps, block, N)
    weights = (proj.astype(jnp.float32), gain_flat.astype(jnp.float32), w_in.astype(jnp.float32), w_out.astype(jnp.float32), w_lcb.astype(jnp.float32))
    start = tuple((jnp.zeros(w.shape, jnp.float32) for w in weights)) + (jnp.zeros((N, ROWS, D), jnp.float32),)
    tables = jnp.arange(N, dtype=jnp.int32)[None, :]

    def step(carry, item):
        x3, grad3, ids = item
        grads, dx3 = layer_grads(x3, grad3, *weights)
        summed = tuple((c + g for c, g in zip(carry[:5], grads)))
        table_sum = carry[5].at[tables, ids].add(dx3)
        return (summed + (table_sum,), None)
    final, _ = lax.scan(step, start, (xs, gs, idx))
    grow = final[5]
    placed = jnp.zeros((N, ROWS, D), jnp.float32).at[table_owner].set(grow)
    owners = jnp.arange(N, dtype=jnp.int32) // TABLES_DEV * STATE
    where = (owners[:, None] + slot_map).reshape(N * ROWS)
    gstate = jnp.zeros((N * ROWS, D), jnp.float32).at[where].set(placed.reshape(N * ROWS, D))
    new_accum = row_accum + lax.optimization_barrier(jnp.mean(gstate * gstate, axis=1))
    new_rows = table_rows - LEARN * gstate / jnp.sqrt(new_accum)[:, None]
    return (final[0], final[1], final[2], final[3], final[4], new_rows, new_accum)
```

```python
import functools

import jax
import jax.numpy as jnp
from jax import lax
from jax.experimental import pallas as pl
from jax.experimental.pallas import tpu as pltpu
from jax.sharding import Mesh, PartitionSpec as P

LEARN = 0.1
EPS = 1e-05
F32 = jnp.float32
BF16 = jnp.bfloat16
D = 192
DP = 256
K = 16
NN = (((1,), (0,)), ((), ()))
NT = (((1,), (1,)), ((), ()))
TN = (((0,), (0,)), ((), ()))


def dot(a, b, dims=NN):
    return lax.dot_general(a, b, dims, preferred_element_type=F32)


def params(mib=56):
    return pltpu.CompilerParams(vmem_limit_bytes=mib * 1024 * 1024)


def cost(flops, nbytes):
    return pl.CostEstimate(flops=int(flops), bytes_accessed=int(nbytes), transcendentals=0)


def split(v):
    hi = v.astype(BF16)
    return hi, (v - hi.astype(F32)).astype(BF16)


def unfold_kernel(x_ref, o_ref, lo, hi):
    rows, tables = o_ref.shape[0], o_ref.shape[1]

    def pair(j, _):
        v = x_ref[:, pl.ds(pl.multiple_of(j * 384, 128), 384)].astype(F32)
        w = pltpu.roll(v, 192, 1)
        lo[pl.ds(2 * j, rows, stride=tables), :] = v[:, :128]
        hi[pl.ds(2 * j, rows, stride=tables), :] = v[:, 128:256]
        lo[pl.ds(2 * j + 1, rows, stride=tables), :] = w[:, :128]
        hi[pl.ds(2 * j + 1, rows, stride=tables), :] = w[:, 128:256]
        return 0

    lax.fori_loop(0, tables // 2, pair, 0, unroll=4)
    keep = lax.broadcasted_iota(jnp.int32, (tables, 128), 1) < 64
    for b in range(rows):
        o_ref[b, :, :128] = lo[b * tables : (b + 1) * tables, :].astype(BF16)
        o_ref[b, :, 128:] = jnp.where(keep, hi[b * tables : (b + 1) * tables, :], 0.0).astype(BF16)


def unfold(x, tables, first, rows=16):
    count = x.shape[0]
    return pl.pallas_call(
        unfold_kernel,
        grid=(count // rows,),
        in_specs=[pl.BlockSpec((rows, tables * D), lambda i: (i, first))],
        out_specs=pl.BlockSpec((rows, tables, DP), lambda i: (i, 0, 0)),
        out_shape=jax.ShapeDtypeStruct((count, tables, DP), BF16),
        scratch_shapes=[pltpu.VMEM((rows * tables, 128), F32)] * 2,
        compiler_params=params(),
        cost_estimate=cost(1e9, count * tables * 900),
        name="unfold",
    )(x)


def first_kernel(x_ref, g_ref, w_ref, s_ref, dl_ref, xh_ref, inv_ref, lo, hi):
    rows = x_ref.shape[0]
    n = x_ref.shape[1]
    w = w_ref[...]
    keep = lax.broadcasted_iota(jnp.int32, (1, DP), 1) < D
    for b in range(rows):
        xb = x_ref[b]
        r = dot(w, xb)
        shi, slo = split(r[:K])
        s_ref[b, :K, :] = shi
        s_ref[b, K:, :] = slo
        f2 = dot(jnp.concatenate([shi, slo], axis=0), xb, NT)
        fm = f2[:K] + f2[K:]
        mean = jnp.sum(fm) * (1.0 / (K * n))
        c = fm - mean
        inv = 1.0 / jnp.sqrt(jnp.full((1, 128), jnp.sum(c * c), F32) * (1.0 / (K * n)) + EPS)
        inv_ref[b : b + 1, :] = inv
        xh = c * inv[:, :1]
        lo[pl.ds(b, K, stride=rows), :] = xh[:, :128]
        hi[pl.ds(b, K, stride=rows), :] = xh[:, 128:]
        lout = r[K:]
        grad = g_ref[b].astype(F32)
        mid = jnp.where(keep, lout - jnp.sum(lout, axis=1, keepdims=True) * (1.0 / D), 0.0)
        oinv = 1.0 / jnp.sqrt(jnp.sum(mid * mid, axis=1, keepdims=True) * (1.0 / D) + EPS)
        chat = mid * oinv
        gm = jnp.sum(grad, axis=1, keepdims=True) * (1.0 / D)
        gc = jnp.sum(grad * chat, axis=1, keepdims=True) * (1.0 / D)
        dl_ref[b] = jnp.where(keep, oinv * (grad - gm - chat * gc), 0.0).astype(BF16)
    xh_ref[:, :, :128] = lo[...].reshape(K, rows, 128)
    xh_ref[:, :, 128:] = hi[...].reshape(K, rows, 128)


def first(x3, g2, wt, rows=8):
    count, n, _ = x3.shape
    nl = g2.shape[1]
    return pl.pallas_call(
        first_kernel,
        grid=(count // rows,),
        in_specs=[
            pl.BlockSpec((rows, n, DP), lambda i: (i, 0, 0)),
            pl.BlockSpec((rows, nl, DP), lambda i: (i, 0, 0)),
            pl.BlockSpec(wt.shape, lambda i: (0, 0)),
        ],
        out_specs=[
            pl.BlockSpec((rows, 2 * K, DP), lambda i: (i, 0, 0)),
            pl.BlockSpec((rows, nl, DP), lambda i: (i, 0, 0)),
            pl.BlockSpec((K, rows, n), lambda i: (0, i, 0)),
            pl.BlockSpec((rows, 128), lambda i: (i, 0)),
        ],
        out_shape=[
            jax.ShapeDtypeStruct((count, 2 * K, DP), BF16),
            jax.ShapeDtypeStruct((count, nl, DP), BF16),
            jax.ShapeDtypeStruct((K, count, n), F32),
            jax.ShapeDtypeStruct((count, 128), F32),
        ],
        scratch_shapes=[pltpu.VMEM((K * rows, 128), F32)] * 2,
        compiler_params=params(),
        cost_estimate=cost(2e10, count * n * DP * 2),
        name="first",
    )(x3, g2, wt)


def batch_kernel(
    xh_ref, inv_ref, gain_ref, win_ref, wout_ref, g_ref,
    gout_ref, gin_ref, ggain_ref, dfm_ref, pre_s, hid_s, dhid_s, norm_s, e_s,
):
    step = pl.program_id(0)
    count, n = xh_ref.shape[1], xh_ref.shape[2]

    @pl.when(step == 0)
    def _():
        pre = jnp.zeros((count, 128), F32)
        for k in range(K):
            normed = (xh_ref[k] * gain_ref[k : k + 1, :]).astype(BF16)
            norm_s[k] = normed
            pre = pre + dot(normed, win_ref[k])
        pre_s[...] = pre
        hid_s[...] = (pre / (1.0 + jnp.exp(-pre))).astype(BF16)
        dhid_s[...] = jnp.zeros_like(dhid_s)

    hid = hid_s[...]
    w = wout_ref[...]
    rows = w.shape[0]
    fout = dot(w, hid, NT).reshape(rows // D, D, count)
    grad = g_ref[...].astype(F32).T.reshape(rows // D, D, count)
    mid = fout - jnp.sum(fout, axis=1, keepdims=True) * (1.0 / D)
    oinv = 1.0 / jnp.sqrt(jnp.sum(mid * mid, axis=1, keepdims=True) * (1.0 / D) + EPS)
    chat = mid * oinv
    gm = jnp.sum(grad, axis=1, keepdims=True) * (1.0 / D)
    gc = jnp.sum(grad * chat, axis=1, keepdims=True) * (1.0 / D)
    df = (oinv * (grad - gm - chat * gc)).reshape(rows, count).astype(BF16)
    gout_ref[...] = dot(df, hid).astype(BF16)
    dhid_s[...] += dot(w, df, TN)

    @pl.when(step == pl.num_programs(0) - 1)
    def _():
        pre = pre_s[...]
        sig = 1.0 / (1.0 + jnp.exp(-pre))
        dpre = (dhid_s[...].T * sig * (1.0 + pre * (1.0 - sig))).astype(BF16)
        m1 = jnp.zeros((count, n), F32)
        m2 = jnp.zeros((count, n), F32)
        for k in range(K):
            gin_ref[k] = dot(norm_s[k], dpre, TN)
            dn = dot(dpre, win_ref[k], NT)
            xh = xh_ref[k]
            ggain_ref[k : k + 1, :] = jnp.sum(dn * xh, axis=0, keepdims=True)
            e = dn * gain_ref[k : k + 1, :]
            e_s[k] = e
            m1 = m1 + e
            m2 = m2 + e * xh
        a1 = jnp.sum(m1, axis=1, keepdims=True) * (1.0 / (K * n))
        a2 = jnp.sum(m2, axis=1, keepdims=True) * (1.0 / (K * n))
        inv = inv_ref[:, :1]
        for k in range(K):
            dfm_ref[k] = inv * (e_s[k] - a1 - xh_ref[k] * a2)


def batch(xh, inv, gain, win, wout, out_grad, feats=4):
    k, count, n = xh.shape
    total = wout.shape[0]
    rows = feats * D
    whole = lambda shape: pl.BlockSpec(shape, lambda i: (0,) * len(shape))
    return pl.pallas_call(
        batch_kernel,
        grid=(total // rows,),
        in_specs=[
            whole((k, count, n)),
            whole((count, 128)),
            whole((k, n)),
            whole((k, n, 128)),
            pl.BlockSpec((rows, 128), lambda i: (i, 0)),
            pl.BlockSpec((count, rows), lambda i: (0, i)),
        ],
        out_specs=[
            pl.BlockSpec((rows, 128), lambda i: (i, 0)),
            whole((k, n, 128)),
            whole((k, n)),
            whole((k, count, n)),
        ],
        out_shape=[
            jax.ShapeDtypeStruct((total, 128), BF16),
            jax.ShapeDtypeStruct((k, n, 128), F32),
            jax.ShapeDtypeStruct((k, n), F32),
            jax.ShapeDtypeStruct((k, count, n), F32),
        ],
        scratch_shapes=[
            pltpu.VMEM((count, 128), F32),
            pltpu.VMEM((count, 128), BF16),
            pltpu.VMEM((128, count), F32),
            pltpu.VMEM((k, count, n), BF16),
            pltpu.VMEM((k, count, n), F32),
        ],
        compiler_params=params(),
        cost_estimate=cost(2e10, 2e7),
        name="batch",
    )(xh, inv, gain, win, wout, out_grad)


def last_kernel(order_ref, x_ref, s_ref, dl_ref, dfm_ref, wt_ref, out_ref, acc_ref, flo, fhi, lo, hi):
    rows, n = x_ref.shape[0], x_ref.shape[1]
    owners = out_ref.shape[0]

    @pl.when(pl.program_id(0) == 0)
    def _():
        acc_ref[...] = jnp.zeros_like(acc_ref)

    flo[...] = dfm_ref[:, :, :128].reshape(K * rows, 128)
    fhi[...] = dfm_ref[:, :, 128:].reshape(K * rows, 128)
    proj = wt_ref[:K, :]
    shared = wt_ref[...]

    def sample(b, _):
        dfm = jnp.concatenate(
            [flo[pl.ds(b, K, stride=rows), :], fhi[pl.ds(b, K, stride=rows), :]], axis=1
        ).astype(BF16)
        xb = x_ref[b]
        dhi, dlo = split(dot(dfm, xb))
        dl = dl_ref[b]
        low = jnp.concatenate([dhi, dlo, dl], axis=0)
        acc_ref[...] += dot(low, xb, NT)
        left = jnp.concatenate([dfm, dfm, proj, shared], axis=0)
        right = jnp.concatenate([s_ref[b], dlo, dhi, dl], axis=0)
        dx = dot(left, right, TN)
        lo[pl.ds(b, n, stride=rows), :] = dx[:, :128]
        hi[pl.ds(b, n, stride=rows), :] = dx[:, 128:]
        return 0

    lax.fori_loop(0, rows, sample, 0, unroll=2)
    keep = lax.broadcasted_iota(jnp.int32, (rows, 128), 1) < 64

    def owner(o, _):
        for q in range(n // owners // 2):
            t0 = order_ref[o * (n // owners) + 2 * q]
            t1 = order_ref[o * (n // owners) + 2 * q + 1]
            p0 = pl.ds(pl.multiple_of(t0 * rows, rows), rows)
            p1 = pl.ds(pl.multiple_of(t1 * rows, rows), rows)
            a1 = pltpu.roll(lo[p1, :], 64, 1)
            b1 = pltpu.roll(hi[p1, :], 64, 1)
            v = jnp.concatenate(
                [lo[p0, :], jnp.where(keep, hi[p0, :], a1), jnp.where(keep, a1, b1)], axis=1
            )
            out_ref[o, :, 384 * q : 384 * (q + 1)] = v.astype(BF16)
        return 0

    lax.fori_loop(0, owners, owner, 0, unroll=2)


def last(order, x3, s, dl, dfm, wt, owners, rows=16):
    count, n, _ = x3.shape
    nl = dl.shape[1]
    per = n // owners * D
    grid = pltpu.PrefetchScalarGridSpec(
        num_scalar_prefetch=1,
        grid=(count // rows,),
        in_specs=[
            pl.BlockSpec((rows, n, DP), lambda i, o: (i, 0, 0)),
            pl.BlockSpec((rows, 2 * K, DP), lambda i, o: (i, 0, 0)),
            pl.BlockSpec((rows, nl, DP), lambda i, o: (i, 0, 0)),
            pl.BlockSpec((K, rows, n), lambda i, o: (0, i, 0)),
            pl.BlockSpec(wt.shape, lambda i, o: (0, 0)),
        ],
        out_specs=[
            pl.BlockSpec((owners, rows, per), lambda i, o: (0, i, 0)),
            pl.BlockSpec((2 * K + nl, n), lambda i, o: (0, 0)),
        ],
        scratch_shapes=[pltpu.VMEM((K * rows, 128), F32)] * 2
        + [pltpu.VMEM((n * rows, 128), F32)] * 2,
    )
    return pl.pallas_call(
        last_kernel,
        grid_spec=grid,
        out_shape=[
            jax.ShapeDtypeStruct((owners, count, per), BF16),
            jax.ShapeDtypeStruct((2 * K + nl, n), F32),
        ],
        compiler_params=params(),
        cost_estimate=cost(2e10, count * n * DP * 4),
        name="last",
    )(order, x3, s, dl, dfm, wt)


def rows_kernel(slot_ref, dx_ref, ids_ref, out_ref, acc, turn):
    step = pl.program_id(0)
    srcs, tables, count = ids_ref.shape
    state = out_ref.shape[0]
    rows = state // tables

    @pl.when(step == 0)
    def _():
        acc[...] = jnp.zeros_like(acc)

    iota = lax.broadcasted_iota(jnp.int32, (rows, count), 0)
    for j in range(tables):
        start = 384 * (j // 2) + 128 * (j % 2)
        total = jnp.zeros((rows, DP), F32)
        for s in range(0, srcs, 2):
            hot = [
                jnp.where(iota == ids_ref[s + i, j : j + 1, :], 1.0, 0.0).astype(BF16)
                for i in range(2)
            ]
            block = dx_ref[s : s + 2, :, start : start + DP].reshape(2 * count, DP)
            total = total + dot(jnp.concatenate(hot, axis=1), block)
        acc[j * rows : (j + 1) * rows, :] += total

    @pl.when(step == pl.num_programs(0) - 1)
    def _():
        for j in range(1, tables, 2):
            part = slice(j * rows, (j + 1) * rows)
            acc[part, :] = pltpu.roll(acc[part, :], DP - 64, 1)

        def place(i, _):
            turn[pl.ds(slot_ref[i], 1), :] = acc[pl.ds(i, 1), :]
            return 0

        lax.fori_loop(0, state, place, 0, unroll=8)
        out_ref[...] = turn[:, :D].astype(BF16)


def row_sums(slots, dx, ids, state, srcs=8):
    total, count, per = dx.shape
    tables = ids.shape[1]
    grid = pltpu.PrefetchScalarGridSpec(
        num_scalar_prefetch=1,
        grid=(total // srcs,),
        in_specs=[
            pl.BlockSpec((srcs, count, per), lambda i, s: (i, 0, 0)),
            pl.BlockSpec((srcs, tables, count), lambda i, s: (i, 0, 0)),
        ],
        out_specs=pl.BlockSpec((state, D), lambda i, s: (0, 0)),
        scratch_shapes=[pltpu.VMEM((state, DP), F32)] * 2,
    )
    return pl.pallas_call(
        rows_kernel,
        grid_spec=grid,
        out_shape=jax.ShapeDtypeStruct((state, D), BF16),
        compiler_params=params(),
        cost_estimate=cost(1e10, dx.size * 2),
        name="row_sums",
    )(slots, dx, ids)


def layer(samples, out_grad, order, proj, gain, w_in, w_out, w_lcb, owners):
    n = proj.shape[0]
    nl = w_lcb.shape[1]
    x3 = unfold(samples, n, 0)
    g2 = unfold(out_grad, nl, out_grad.shape[1] // D // nl - 1)
    wt = jnp.concatenate([proj.T, w_lcb.T], axis=0)
    gain_t = gain.reshape(n, K).T.astype(F32)
    win_t = w_in.reshape(n, K, 128).transpose(1, 0, 2)
    s, dl, xh, inv = first(x3, g2, wt)
    g_out, g_in, g_gain, dfm = batch(xh, inv, gain_t, win_t, w_out, out_grad)
    dx, acc = last(order, x3, s, dl, dfm, wt, owners)
    g_proj = acc[:K] + acc[K : 2 * K]
    return g_proj, g_gain, g_in, g_out, acc[2 * K :], dx


WIDE = ("z", "x", "yl")


def gather(a):
    n = 32
    return lax.all_to_all(jnp.broadcast_to(a[None], (n,) + a.shape), WIDE, 0, 0, tiled=True)


def rep_sum(v):
    swap = [(0, 1), (1, 0)]
    for axis in ("c", "yh"):
        v = v.astype(BF16)
        v = v.astype(F32) + lax.ppermute(v, axis, swap).astype(F32)
    return v


def body(
    samples, out_grad, row_ids, table_owner, slot_map, proj, gain_flat, w_in, w_out, w_lcb,
    table_rows, row_accum,
):
    owners = 32
    count = samples.shape[0]
    per = proj.shape[0]
    n = per * owners
    nl = w_lcb.shape[1]
    small = jnp.concatenate([proj, gain_flat.reshape(per, K), w_lcb], axis=1)
    small = jnp.pad(small, ((0, 8), (0, 128 - small.shape[1])))
    packed = gather(jnp.concatenate([w_in, small], axis=0))
    w_in_f = packed[:, : w_in.shape[0]].reshape(-1, 128)
    small_f = packed[:, w_in.shape[0] : w_in.shape[0] + per].reshape(n, 128)
    proj_f = small_f[:, :K]
    gain_f = small_f[:, K : 2 * K].reshape(-1)
    w_lcb_f = small_f[:, 2 * K : 2 * K + nl]
    w_out_f = gather(w_out).reshape(-1, 128)

    order = jnp.zeros((n,), jnp.int32).at[table_owner].set(jnp.arange(n, dtype=jnp.int32))
    ids = jnp.take(row_ids.T, order, axis=0).reshape(owners, per, count)
    ids = lax.all_to_all(ids, WIDE, 0, 0, tiled=True)

    g_proj, g_gain, g_in, g_out, g_lcb, dx = layer(
        samples, out_grad, order, proj_f, gain_f, w_in_f, w_out_f, w_lcb_f, owners
    )
    big = jnp.concatenate(
        [
            g_out.reshape(owners, -1, 128),
            g_in.astype(BF16).transpose(1, 0, 2).reshape(owners, -1, 128),
        ],
        axis=1,
    )
    big = lax.all_to_all(big, WIDE, 0, 0, tiled=True)
    little = jnp.concatenate([g_proj, g_gain, g_lcb], axis=0).T.reshape(owners, per, -1)
    little = lax.all_to_all(little, WIDE, 0, 0, tiled=True)
    recv = lax.all_to_all(dx, WIDE, 0, 0, tiled=True)
    part = row_sums(slot_map.reshape(-1), recv, ids, table_rows.shape[0])
    total = rep_sum(part)
    big = rep_sum(jnp.sum(big.astype(F32), axis=0))
    little = rep_sum(jnp.sum(little, axis=0))
    split_at = w_out.shape[0]
    new_accum = row_accum + jnp.mean(total * total, axis=1)
    new_rows = table_rows - LEARN * total / jnp.sqrt(new_accum)[:, None]
    return (
        little[:, :K],
        little[:, K : 2 * K].reshape(-1),
        big[split_at:],
        big[:split_at],
        little[:, 2 * K :],
        new_rows,
        new_accum,
    )


def solution(mesh):
    cube = Mesh(mesh.devices.reshape(4, 4, 2, 2, 2), ("z", "x", "yl", "yh", "c"))
    batch_spec = P(("z", "x", "yl", "yh", "c"), None)
    two, one = P(WIDE, None), P(WIDE)
    in_specs = (batch_spec,) * 3 + (P(), two, two, one, two, two, two, two, one)
    out_specs = (two, one, two, two, two, two, one)
    return jax.shard_map(body, mesh=cube, in_specs=in_specs, out_specs=out_specs, check_vma=False)
```

```python
import functools

import jax
import jax.numpy as jnp
from jax import lax
from jax.experimental import pallas as pl
from jax.experimental.pallas import tpu as pltpu
from jax.sharding import Mesh, PartitionSpec as P

LEARN = 0.1
EPS = 1e-05
F32 = jnp.float32
BF16 = jnp.bfloat16
D = 192
DP = 256
K = 16
NN = (((1,), (0,)), ((), ()))
NT = (((1,), (1,)), ((), ()))
TN = (((0,), (0,)), ((), ()))


def dot(a, b, dims=NN):
    return lax.dot_general(a, b, dims, preferred_element_type=F32)


def params(mib=56):
    return pltpu.CompilerParams(vmem_limit_bytes=mib * 1024 * 1024)


def cost(flops, nbytes):
    return pl.CostEstimate(flops=int(flops), bytes_accessed=int(nbytes), transcendentals=0)


def split(v):
    hi = v.astype(BF16)
    return hi, (v - hi.astype(F32)).astype(BF16)


def unfold_kernel(x_ref, o_ref):
    tables = o_ref.shape[1]
    keep = lax.broadcasted_iota(jnp.int32, (1, 1, 128), 2) < 64

    def group(j, _):
        lo, hi = [], []
        for p in range(8):
            v = x_ref[:, pl.ds(pl.multiple_of(j * 3072 + 384 * p, 128), 384)].astype(F32)
            w = pltpu.roll(v, 192, 1)
            lo += [v[:, :128], w[:, :128]]
            hi += [v[:, 128:256], w[:, 128:256]]
        at = pl.ds(pl.multiple_of(j * 16, 16), 16)
        o_ref[:, at, :128] = jnp.swapaxes(jnp.stack(lo), 0, 1).astype(BF16)
        o_ref[:, at, 128:] = jnp.where(keep, jnp.swapaxes(jnp.stack(hi), 0, 1), 0.0).astype(BF16)
        return 0

    lax.fori_loop(0, tables // 16, group, 0)


def unfold(x, tables, first, rows=16):
    count = x.shape[0]
    return pl.pallas_call(
        unfold_kernel,
        grid=(count // rows,),
        in_specs=[pl.BlockSpec((rows, tables * D), lambda i: (i, first))],
        out_specs=pl.BlockSpec((rows, tables, DP), lambda i: (i, 0, 0)),
        out_shape=jax.ShapeDtypeStruct((count, tables, DP), BF16),
        compiler_params=params(),
        cost_estimate=cost(1e9, count * tables * 900),
        name="unfold",
    )(x)


def first_kernel(x_ref, g_ref, w_ref, s_ref, dl_ref, xh_ref, inv_ref, lo, hi):
    rows = x_ref.shape[0]
    n = x_ref.shape[1]
    w = w_ref[...]
    keep = lax.broadcasted_iota(jnp.int32, (1, DP), 1) < D
    for b in range(rows):
        xb = x_ref[b]
        r = dot(w, xb)
        shi, slo = split(r[:K])
        s_ref[b, :K, :] = shi
        s_ref[b, K:, :] = slo
        f2 = dot(jnp.concatenate([shi, slo], axis=0), xb, NT)
        fm = f2[:K] + f2[K:]
        mean = jnp.sum(fm) * (1.0 / (K * n))
        c = fm - mean
        inv = 1.0 / jnp.sqrt(jnp.full((1, 128), jnp.sum(c * c), F32) * (1.0 / (K * n)) + EPS)
        inv_ref[b : b + 1, :] = inv
        xh = c * inv[:, :1]
        lo[pl.ds(b, K, stride=rows), :] = xh[:, :128]
        hi[pl.ds(b, K, stride=rows), :] = xh[:, 128:]
        lout = r[K:]
        grad = g_ref[b].astype(F32)
        mid = jnp.where(keep, lout - jnp.sum(lout, axis=1, keepdims=True) * (1.0 / D), 0.0)
        oinv = 1.0 / jnp.sqrt(jnp.sum(mid * mid, axis=1, keepdims=True) * (1.0 / D) + EPS)
        chat = mid * oinv
        gm = jnp.sum(grad, axis=1, keepdims=True) * (1.0 / D)
        gc = jnp.sum(grad * chat, axis=1, keepdims=True) * (1.0 / D)
        dl_ref[b] = jnp.where(keep, oinv * (grad - gm - chat * gc), 0.0).astype(BF16)
    xh_ref[:, :, :128] = lo[...].reshape(K, rows, 128)
    xh_ref[:, :, 128:] = hi[...].reshape(K, rows, 128)


def first(x3, g2, wt, rows=8):
    count, n, _ = x3.shape
    nl = g2.shape[1]
    return pl.pallas_call(
        first_kernel,
        grid=(count // rows,),
        in_specs=[
            pl.BlockSpec((rows, n, DP), lambda i: (i, 0, 0)),
            pl.BlockSpec((rows, nl, DP), lambda i: (i, 0, 0)),
            pl.BlockSpec(wt.shape, lambda i: (0, 0)),
        ],
        out_specs=[
            pl.BlockSpec((rows, 2 * K, DP), lambda i: (i, 0, 0)),
            pl.BlockSpec((rows, nl, DP), lambda i: (i, 0, 0)),
            pl.BlockSpec((K, rows, n), lambda i: (0, i, 0)),
            pl.BlockSpec((rows, 128), lambda i: (i, 0)),
        ],
        out_shape=[
            jax.ShapeDtypeStruct((count, 2 * K, DP), BF16),
            jax.ShapeDtypeStruct((count, nl, DP), BF16),
            jax.ShapeDtypeStruct((K, count, n), F32),
            jax.ShapeDtypeStruct((count, 128), F32),
        ],
        scratch_shapes=[pltpu.VMEM((K * rows, 128), F32)] * 2,
        compiler_params=params(),
        cost_estimate=cost(2e10, count * n * DP * 2),
        name="first",
    )(x3, g2, wt)


def batch_kernel(
    xh_ref, inv_ref, gain_ref, win_ref, wout_ref, g_ref,
    gout_ref, gin_ref, ggain_ref, dfm_ref, pre_s, hid_s, dhid_s, norm_s, e_s,
):
    step = pl.program_id(0)
    count, n = xh_ref.shape[1], xh_ref.shape[2]

    @pl.when(step == 0)
    def _():
        pre = jnp.zeros((count, 128), F32)
        for k in range(K):
            normed = (xh_ref[k] * gain_ref[k : k + 1, :]).astype(BF16)
            norm_s[k] = normed
            pre = pre + dot(normed, win_ref[k])
        pre_s[...] = pre
        hid_s[...] = (pre / (1.0 + jnp.exp(-pre))).astype(BF16)
        dhid_s[...] = jnp.zeros_like(dhid_s)

    hid = hid_s[...]
    w = wout_ref[...]
    rows = w.shape[0]
    fout = dot(w, hid, NT).reshape(rows // D, D, count)
    grad = g_ref[...].astype(F32).T.reshape(rows // D, D, count)
    mid = fout - jnp.sum(fout, axis=1, keepdims=True) * (1.0 / D)
    oinv = 1.0 / jnp.sqrt(jnp.sum(mid * mid, axis=1, keepdims=True) * (1.0 / D) + EPS)
    chat = mid * oinv
    gm = jnp.sum(grad, axis=1, keepdims=True) * (1.0 / D)
    gc = jnp.sum(grad * chat, axis=1, keepdims=True) * (1.0 / D)
    df = (oinv * (grad - gm - chat * gc)).reshape(rows, count).astype(BF16)
    gout_ref[...] = dot(df, hid).astype(BF16)
    dhid_s[...] += dot(w, df, TN)

    @pl.when(step == pl.num_programs(0) - 1)
    def _():
        pre = pre_s[...]
        sig = 1.0 / (1.0 + jnp.exp(-pre))
        dpre = (dhid_s[...].T * sig * (1.0 + pre * (1.0 - sig))).astype(BF16)
        m1 = jnp.zeros((count, n), F32)
        m2 = jnp.zeros((count, n), F32)
        for k in range(K):
            gin_ref[k] = dot(norm_s[k], dpre, TN)
            dn = dot(dpre, win_ref[k], NT)
            xh = xh_ref[k]
            ggain_ref[k : k + 1, :] = jnp.sum(dn * xh, axis=0, keepdims=True)
            e = dn * gain_ref[k : k + 1, :]
            e_s[k] = e
            m1 = m1 + e
            m2 = m2 + e * xh
        a1 = jnp.sum(m1, axis=1, keepdims=True) * (1.0 / (K * n))
        a2 = jnp.sum(m2, axis=1, keepdims=True) * (1.0 / (K * n))
        inv = inv_ref[:, :1]
        for k in range(K):
            dfm_ref[k] = inv * (e_s[k] - a1 - xh_ref[k] * a2)


def batch(xh, inv, gain, win, wout, out_grad, feats=4):
    k, count, n = xh.shape
    total = wout.shape[0]
    rows = feats * D
    whole = lambda shape: pl.BlockSpec(shape, lambda i: (0,) * len(shape))
    return pl.pallas_call(
        batch_kernel,
        grid=(total // rows,),
        in_specs=[
            whole((k, count, n)),
            whole((count, 128)),
            whole((k, n)),
            whole((k, n, 128)),
            pl.BlockSpec((rows, 128), lambda i: (i, 0)),
            pl.BlockSpec((count, rows), lambda i: (0, i)),
        ],
        out_specs=[
            pl.BlockSpec((rows, 128), lambda i: (i, 0)),
            whole((k, n, 128)),
            whole((k, n)),
            whole((k, count, n)),
        ],
        out_shape=[
            jax.ShapeDtypeStruct((total, 128), BF16),
            jax.ShapeDtypeStruct((k, n, 128), F32),
            jax.ShapeDtypeStruct((k, n), F32),
            jax.ShapeDtypeStruct((k, count, n), F32),
        ],
        scratch_shapes=[
            pltpu.VMEM((count, 128), F32),
            pltpu.VMEM((count, 128), BF16),
            pltpu.VMEM((128, count), F32),
            pltpu.VMEM((k, count, n), BF16),
            pltpu.VMEM((k, count, n), F32),
        ],
        compiler_params=params(),
        cost_estimate=cost(2e10, 2e7),
        name="batch",
    )(xh, inv, gain, win, wout, out_grad)


def last_kernel(
    order_ref, x_ref, s_ref, dl_ref, dfm_ref, wt_ref, keep_ref, send_ref, acc_ref, flo, fhi, lo, hi
):
    rows, n = x_ref.shape[0], x_ref.shape[1]
    pairs = keep_ref.shape[0]

    @pl.when(pl.program_id(0) == 0)
    def _():
        acc_ref[...] = jnp.zeros_like(acc_ref)

    flo[...] = dfm_ref[:, :, :128].reshape(K * rows, 128)
    fhi[...] = dfm_ref[:, :, 128:].reshape(K * rows, 128)
    proj = wt_ref[:K, :]
    shared = wt_ref[...]

    def sample(b, _):
        dfm = jnp.concatenate(
            [flo[pl.ds(b, K, stride=rows), :], fhi[pl.ds(b, K, stride=rows), :]], axis=1
        ).astype(BF16)
        xb = x_ref[b]
        dhi, dlo = split(dot(dfm, xb))
        dl = dl_ref[b]
        low = jnp.concatenate([dhi, dlo, dl], axis=0)
        acc_ref[...] += dot(low, xb, NT)
        left = jnp.concatenate([dfm, dfm, proj, shared], axis=0)
        right = jnp.concatenate([s_ref[b], dlo, dhi, dl], axis=0)
        dx = dot(left, right, TN)
        lo[pl.ds(b, n, stride=rows), :] = dx[:, :128]
        hi[pl.ds(b, n, stride=rows), :] = dx[:, 128:]
        return 0

    lax.fori_loop(0, rows, sample, 0, unroll=2)
    keep = lax.broadcasted_iota(jnp.int32, (rows, 128), 1) < 64

    def pair(i, _):
        for part, ref in enumerate((keep_ref, send_ref)):
            t0 = order_ref[part * 2 * pairs + 2 * i]
            t1 = order_ref[part * 2 * pairs + 2 * i + 1]
            p0 = pl.ds(pl.multiple_of(t0 * rows, rows), rows)
            p1 = pl.ds(pl.multiple_of(t1 * rows, rows), rows)
            a1 = pltpu.roll(lo[p1, :], 64, 1)
            b1 = pltpu.roll(hi[p1, :], 64, 1)
            v = jnp.concatenate(
                [lo[p0, :], jnp.where(keep, hi[p0, :], a1), jnp.where(keep, a1, b1)], axis=1
            )
            ref[i] = v.astype(BF16)
        return 0

    lax.fori_loop(0, pairs, pair, 0, unroll=4)


def last(order, x3, s, dl, dfm, wt, rows=16):
    count, n, _ = x3.shape
    nl = dl.shape[1]
    pairs = n // 4
    grid = pltpu.PrefetchScalarGridSpec(
        num_scalar_prefetch=1,
        grid=(count // rows,),
        in_specs=[
            pl.BlockSpec((rows, n, DP), lambda i, o: (i, 0, 0)),
            pl.BlockSpec((rows, 2 * K, DP), lambda i, o: (i, 0, 0)),
            pl.BlockSpec((rows, nl, DP), lambda i, o: (i, 0, 0)),
            pl.BlockSpec((K, rows, n), lambda i, o: (0, i, 0)),
            pl.BlockSpec(wt.shape, lambda i, o: (0, 0)),
        ],
        out_specs=[
            pl.BlockSpec((pairs, rows, 2 * D), lambda i, o: (0, i, 0)),
            pl.BlockSpec((pairs, rows, 2 * D), lambda i, o: (0, i, 0)),
            pl.BlockSpec((2 * K + nl, n), lambda i, o: (0, 0)),
        ],
        scratch_shapes=[pltpu.VMEM((K * rows, 128), F32)] * 2
        + [pltpu.VMEM((n * rows, 128), F32)] * 2,
    )
    return pl.pallas_call(
        last_kernel,
        grid_spec=grid,
        out_shape=[
            jax.ShapeDtypeStruct((pairs, count, 2 * D), BF16),
            jax.ShapeDtypeStruct((pairs, count, 2 * D), BF16),
            jax.ShapeDtypeStruct((2 * K + nl, n), F32),
        ],
        compiler_params=params(),
        cost_estimate=cost(2e10, count * n * DP * 4),
        name="last",
    )(order, x3, s, dl, dfm, wt)


def fold(v, even):
    half = v.shape[0] // 2
    main, tail = (v[:, :128], v[:, 128:]) if even else (v[:, 128:], v[:, :128])
    keep = lax.broadcasted_iota(jnp.int32, (half, 128), 1) < 64
    if even:
        tail = jnp.where(keep, tail[:half], pltpu.roll(tail[half:], 64, 1))
    else:
        tail = jnp.where(keep, pltpu.roll(tail[:half], 64, 1), tail[half:])
    return main.astype(BF16), tail.astype(BF16)


def sums_kernel(at_ref, mine_ref, other_ref, ids_ref, oid_ref, even_ref, odd_ref):
    pairs, count, _ = mine_ref.shape
    rows = 2 * count
    iota = lax.broadcasted_iota(jnp.int32, (rows, count), 0)
    for i in range(pairs):
        for t, ref in enumerate((even_ref, odd_ref)):
            hot = jnp.concatenate(
                [
                    jnp.where(iota == r[i, t : t + 1, :], 1.0, 0.0).astype(BF16)
                    for r in (ids_ref, oid_ref)
                ],
                axis=1,
            )
            cols = slice(128 * t, 128 * t + DP)
            block = jnp.concatenate([mine_ref[i, :, cols], other_ref[i, :, cols]], axis=0)
            main, tail = fold(dot(hot, block), t == 0)
            ref[0, 0, i, :rows, :] = main
            ref[0, 0, i, rows:, :] = tail


def sums(at, mine, other, ids, oids, nz, nx):
    total, count, wide = mine.shape
    ny = total // (nz * nx)
    grid = pltpu.PrefetchScalarGridSpec(
        num_scalar_prefetch=1,
        grid=(nz, nx),
        in_specs=[
            pl.BlockSpec((ny, count, wide), lambda z, x, at: (z * nx + x, 0, 0)),
            pl.BlockSpec((ny, count, wide), lambda z, x, at: (z * nx + x, 0, 0)),
            pl.BlockSpec((ny, 2, count), lambda z, x, at: (z * nx + x, 0, 0)),
            pl.BlockSpec((ny, 2, count), lambda z, x, at: (z * nx + x, 0, 0)),
        ],
        out_specs=[
            pl.BlockSpec(
                (1, 1, ny, 384, 128),
                lambda z, x, at: ((z + nz - at[0]) % nz, (x + nx - at[1]) % nx, 0, 0, 0),
            ),
            pl.BlockSpec(
                (1, 1, ny, 384, 128),
                lambda z, x, at: ((x + nx - at[1]) % nx, (z + nz - at[0]) % nz, 0, 0, 0),
            ),
        ],
    )
    return pl.pallas_call(
        sums_kernel,
        grid_spec=grid,
        out_shape=[
            jax.ShapeDtypeStruct((nz, nx, ny, 384, 128), BF16),
            jax.ShapeDtypeStruct((nx, nz, ny, 384, 128), BF16),
        ],
        compiler_params=params(),
        cost_estimate=cost(1e10, mine.size * 8),
        name="sums",
    )(at, mine, other, ids, oids)


def place_kernel(slot_ref, sum_ref, out_ref, acc, turn):
    tables = sum_ref.shape[0]
    state = out_ref.shape[0]
    rows = state // tables
    half = rows // 2
    keep = lax.broadcasted_iota(jnp.int32, (half, 128), 1) < 64
    for t in range(tables):
        main = sum_ref[t, :rows, :].astype(F32)
        tail = sum_ref[t, rows:, :].astype(F32)
        first, second = slice(t * rows, t * rows + half), slice(t * rows + half, (t + 1) * rows)
        flip = pltpu.roll(tail, 64, 1)
        if t % 2 == 0:
            acc[t * rows : (t + 1) * rows, :128] = main
            acc[first, 128:] = tail
            acc[second, 128:] = flip
        else:
            turned = pltpu.roll(main, 64, 1)
            acc[first, :128] = jnp.where(keep, tail, turned[:half])
            acc[second, :128] = jnp.where(keep, flip, turned[half:])
            acc[t * rows : (t + 1) * rows, 128:] = turned

    def place(i, _):
        turn[pl.ds(slot_ref[i], 1), :] = acc[pl.ds(i, 1), :]
        return 0

    lax.fori_loop(0, state, place, 0, unroll=8)
    out_ref[...] = turn[:, :D]


def place(slots, sums):
    state = slots.shape[0]
    grid = pltpu.PrefetchScalarGridSpec(
        num_scalar_prefetch=1,
        grid=(1,),
        in_specs=[pl.BlockSpec(sums.shape, lambda i, s: (0, 0, 0))],
        out_specs=pl.BlockSpec((state, D), lambda i, s: (0, 0)),
        scratch_shapes=[pltpu.VMEM((state, DP), F32)] * 2,
    )
    return pl.pallas_call(
        place_kernel,
        grid_spec=grid,
        out_shape=jax.ShapeDtypeStruct((state, D), F32),
        compiler_params=params(),
        cost_estimate=cost(1e8, state * D * 8),
        name="place",
    )(slots, sums)


def layer(samples, out_grad, order, proj, gain, w_in, w_out, w_lcb):
    n = proj.shape[0]
    nl = w_lcb.shape[1]
    x3 = unfold(samples, n, 0)
    g2 = unfold(out_grad, nl, out_grad.shape[1] // D // nl - 1)
    wt = jnp.concatenate([proj.T, w_lcb.T], axis=0)
    gain_t = gain.reshape(n, K).T.astype(F32)
    win_t = w_in.reshape(n, K, 128).transpose(1, 0, 2)
    s, dl, xh, inv = first(x3, g2, wt)
    g_out, g_in, g_gain, dfm = batch(xh, inv, gain_t, win_t, w_out, out_grad)
    keep, send, acc = last(order, x3, s, dl, dfm, wt)
    g_proj = acc[:K] + acc[K : 2 * K]
    return g_proj, g_gain, g_in, g_out, acc[2 * K :], keep, send


WIDE = ("z", "x", "yl")


def gather(a):
    n = 32
    return lax.all_to_all(jnp.broadcast_to(a[None], (n,) + a.shape), WIDE, 0, 0, tiled=True)


def ring_step(axis, by, v):
    n = 4
    return lax.ppermute(v, axis, [(i, (i + by) % n) for i in range(n)])


def add(*terms):
    total = terms[0].astype(F32)
    for term in terms[1:]:
        total = total + term.astype(F32)
    return total.astype(BF16)


def ring_sums(parts):
    fore = [ring_step(axis, 1, v[2, :2]) for axis, v in parts]
    back = [ring_step(axis, -1, v[2, 2:]) for axis, v in parts]
    fore = [
        ring_step(axis, 1, jnp.concatenate([add(v[1, :2], f), v[1, 2:]], axis=0))
        for (axis, v), f in zip(parts, fore)
    ]
    back = [
        ring_step(axis, -1, jnp.concatenate([v[3, :2], add(v[3, 2:], b)], axis=0))
        for (axis, v), b in zip(parts, back)
    ]
    return [add(v[0], f, b) for (_, v), f, b in zip(parts, fore, back)]


SWAP = [(0, 1), (1, 0)]


def rep_sum(v):
    swap = SWAP
    for axis in ("c", "yh"):
        v = v.astype(BF16)
        v = v.astype(F32) + lax.ppermute(v, axis, swap).astype(F32)
    return v


def body(
    samples, out_grad, row_ids, table_owner, slot_map, proj, gain_flat, w_in, w_out, w_lcb,
    table_rows, row_accum,
):
    owners = 32
    count = samples.shape[0]
    per = proj.shape[0]
    n = per * owners
    nl = w_lcb.shape[1]
    small = jnp.concatenate([proj, gain_flat.reshape(per, K), w_lcb], axis=1)
    small = jnp.pad(small, ((0, 8), (0, 128 - small.shape[1])))
    packed = gather(jnp.concatenate([w_in, small], axis=0))
    w_in_f = packed[:, : w_in.shape[0]].reshape(-1, 128)
    small_f = packed[:, w_in.shape[0] : w_in.shape[0] + per].reshape(n, 128)
    proj_f = small_f[:, :K]
    gain_f = small_f[:, K : 2 * K].reshape(-1)
    w_lcb_f = small_f[:, 2 * K : 2 * K + nl]
    w_out_f = gather(w_out).reshape(-1, 128)

    core = lax.axis_index("c")
    order = jnp.zeros((n,), jnp.int32).at[table_owner].set(jnp.arange(n, dtype=jnp.int32))
    order = order.reshape(owners, 2, per // 2).transpose(1, 0, 2)
    order = jnp.where(core == 0, order, order[::-1]).reshape(-1)
    ids = jnp.take(row_ids.T, order, axis=0).reshape(2, n // 4, 2, count)
    other_ids = lax.ppermute(ids[1], "c", SWAP)

    g_proj, g_gain, g_in, g_out, g_lcb, keep, send = layer(
        samples, out_grad, order, proj_f, gain_f, w_in_f, w_out_f, w_lcb_f
    )
    big = jnp.concatenate(
        [
            g_out.reshape(owners, -1, 128),
            g_in.astype(BF16).transpose(1, 0, 2).reshape(owners, -1, 128),
        ],
        axis=1,
    )
    big = lax.all_to_all(big, WIDE, 0, 0, tiled=True)
    big = rep_sum(jnp.sum(big.astype(F32), axis=0))
    little = jnp.concatenate([g_proj, g_gain, g_lcb], axis=0).T.reshape(owners, per, -1)
    little = lax.all_to_all(little, WIDE, 0, 0, tiled=True)
    little = rep_sum(jnp.sum(little, axis=0))

    other = lax.ppermute(send, "c", SWAP)
    at = jnp.stack([lax.axis_index("z"), lax.axis_index("x")]).astype(jnp.int32)
    even, odd = sums(at, keep, other, ids[0], other_ids, 4, 4)
    even, odd = ring_sums([("z", even), ("x", odd)])
    even, odd = ring_sums([("x", even), ("z", odd)])
    both = jnp.stack([even, odd], axis=1).reshape(2, 1, 2, 2, 384, 128)
    both = jnp.broadcast_to(both, (2, 2, 2, 2, 384, 128)).reshape(4, 4, 384, 128)
    both = lax.all_to_all(both, ("yl", "yh"), 0, 0, tiled=True)
    mine = jnp.sum(both.astype(F32), axis=0).astype(BF16)
    others = lax.ppermute(mine, "c", SWAP)
    owned = jnp.where(
        core == 0, jnp.concatenate([mine, others], axis=0), jnp.concatenate([others, mine], axis=0)
    )
    total = place(slot_map.reshape(-1), owned)
    split_at = w_out.shape[0]
    new_accum = row_accum + jnp.mean(total * total, axis=1)
    new_rows = table_rows - LEARN * total / jnp.sqrt(new_accum)[:, None]
    return (
        little[:, :K],
        little[:, K : 2 * K].reshape(-1),
        big[split_at:],
        big[:split_at],
        little[:, 2 * K :],
        new_rows,
        new_accum,
    )


def solution(mesh):
    cube = Mesh(mesh.devices.reshape(4, 4, 2, 2, 2), ("z", "x", "yl", "yh", "c"))
    batch_spec = P(("z", "x", "yl", "yh", "c"), None)
    two, one = P(WIDE, None), P(WIDE)
    in_specs = (batch_spec,) * 3 + (P(), two, two, one, two, two, two, two, one)
    out_specs = (two, one, two, two, two, two, one)
    return jax.shard_map(body, mesh=cube, in_specs=in_specs, out_specs=out_specs, check_vma=False)
```

```python
import functools

import jax
import jax.numpy as jnp
from jax import lax
from jax.experimental import pallas as pl
from jax.experimental.pallas import tpu as pltpu
from jax.sharding import Mesh, PartitionSpec as P

LEARN = 0.1
EPS = 1e-05
F32 = jnp.float32
BF16 = jnp.bfloat16
D = 192
DP = 256
K = 16
NN = (((1,), (0,)), ((), ()))
NT = (((1,), (1,)), ((), ()))
TN = (((0,), (0,)), ((), ()))


def dot(a, b, dims=NN):
    return lax.dot_general(a, b, dims, preferred_element_type=F32)


def params(mib=56):
    return pltpu.CompilerParams(vmem_limit_bytes=mib * 1024 * 1024)


def cost(flops, nbytes):
    return pl.CostEstimate(flops=int(flops), bytes_accessed=int(nbytes), transcendentals=0)


def split(v):
    hi = v.astype(BF16)
    return hi, (v - hi.astype(F32)).astype(BF16)


def unfold_kernel(x_ref, o_ref):
    tables = o_ref.shape[1]
    low = lax.broadcasted_iota(jnp.int32, (1, 1, 128), 2) < 64

    def group(j, _):
        at = pl.ds(pl.multiple_of(j * 16, 16), 16)
        for h in range(2):
            lo, hi = [], []
            part = slice(16 * h, 16 * h + 16)
            for p in range(8):
                v = x_ref[part, pl.ds(pl.multiple_of(j * 3072 + 384 * p, 128), 384)].astype(F32)
                w = pltpu.roll(v, 192, 1)
                lo += [v[:, :128], w[:, :128]]
                if h == 0:
                    hi += [v[:, 128:256], w[:, 128:256]]
                else:
                    hi += [pltpu.roll(v[:, 128:256], 64, 1), v[:, 256:]]
            hi = jnp.swapaxes(jnp.stack(hi), 0, 1)
            hi = jnp.where(low, hi, 0.0) if h == 0 else jnp.where(low, 0.0, hi)
            o_ref[part, at, :128] = jnp.swapaxes(jnp.stack(lo), 0, 1).astype(BF16)
            o_ref[part, at, 128:] = hi.astype(BF16)
        return 0

    lax.fori_loop(0, tables // 16, group, 0)


def unfold(x, tables, first, rows=32):
    count = x.shape[0]
    return pl.pallas_call(
        unfold_kernel,
        grid=(count // rows,),
        in_specs=[pl.BlockSpec((rows, tables * D), lambda i: (i, first))],
        out_specs=pl.BlockSpec((rows, tables, DP), lambda i: (i, 0, 0)),
        out_shape=jax.ShapeDtypeStruct((count, tables, DP), BF16),
        compiler_params=params(),
        cost_estimate=cost(1e9, count * tables * 900),
        name="unfold",
    )(x)


def first_kernel(x_ref, g_ref, w_ref, s_ref, dl_ref, xh_ref, inv_ref, lo, hi):
    rows = x_ref.shape[0]
    n = x_ref.shape[1]
    w = w_ref[...]
    lane = lax.broadcasted_iota(jnp.int32, (1, DP), 1)
    half = (pl.program_id(0) * rows // 16) % 2
    keep = (lane < 128) | ((lane >= 128 + 64 * half) & (lane < 192 + 64 * half))
    total = lambda v: jnp.sum(jnp.sum(v, axis=0, keepdims=True), axis=1, keepdims=True)
    for b in range(rows):
        xb = x_ref[b]
        r = dot(w, xb)
        shi, slo = split(r[:K])
        s_ref[b, :K, :] = shi
        s_ref[b, K:, :] = slo
        f2 = dot(jnp.concatenate([shi, slo], axis=0), xb, NT)
        fm = f2[:K] + f2[K:]
        c = fm - total(fm) * (1.0 / (K * n))
        inv = 1.0 / jnp.sqrt(total(c * c) * (1.0 / (K * n)) + EPS)
        inv_ref[b : b + 1, :] = jnp.broadcast_to(inv, (1, 128))
        xh = c * inv
        lo[pl.ds(b, K, stride=rows), :] = xh[:, :128]
        hi[pl.ds(b, K, stride=rows), :] = xh[:, 128:]
        lout = r[K:]
        grad = g_ref[b].astype(F32)
        mid = jnp.where(keep, lout - jnp.sum(lout, axis=1, keepdims=True) * (1.0 / D), 0.0)
        oinv = 1.0 / jnp.sqrt(jnp.sum(mid * mid, axis=1, keepdims=True) * (1.0 / D) + EPS)
        chat = mid * oinv
        gm = jnp.sum(grad, axis=1, keepdims=True) * (1.0 / D)
        gc = jnp.sum(grad * chat, axis=1, keepdims=True) * (1.0 / D)
        dl_ref[b] = jnp.where(keep, oinv * (grad - gm - chat * gc), 0.0).astype(BF16)
    xh_ref[:, :, :128] = lo[...].reshape(K, rows, 128)
    xh_ref[:, :, 128:] = hi[...].reshape(K, rows, 128)


def first(x3, g2, wt, rows=8):
    count, n, _ = x3.shape
    nl = g2.shape[1]
    return pl.pallas_call(
        first_kernel,
        grid=(count // rows,),
        in_specs=[
            pl.BlockSpec((rows, n, DP), lambda i: (i, 0, 0)),
            pl.BlockSpec((rows, nl, DP), lambda i: (i, 0, 0)),
            pl.BlockSpec(wt.shape, lambda i: (0, 0)),
        ],
        out_specs=[
            pl.BlockSpec((rows, 2 * K, DP), lambda i: (i, 0, 0)),
            pl.BlockSpec((rows, nl, DP), lambda i: (i, 0, 0)),
            pl.BlockSpec((K, rows, n), lambda i: (0, i, 0)),
            pl.BlockSpec((rows, 128), lambda i: (i, 0)),
        ],
        out_shape=[
            jax.ShapeDtypeStruct((count, 2 * K, DP), BF16),
            jax.ShapeDtypeStruct((count, nl, DP), BF16),
            jax.ShapeDtypeStruct((K, count, n), F32),
            jax.ShapeDtypeStruct((count, 128), F32),
        ],
        scratch_shapes=[pltpu.VMEM((K * rows, 128), F32)] * 2,
        compiler_params=params(),
        cost_estimate=cost(2e10, count * n * DP * 2),
        name="first",
    )(x3, g2, wt)


def batch_kernel(
    xh_ref, inv_ref, gain_ref, win_ref, wout_ref, g_ref,
    gout_ref, gin_ref, ggain_ref, dfm_ref, pre_s, hid_s, dhid_s, norm_s, e_s,
):
    step = pl.program_id(0)
    count, n = xh_ref.shape[1], xh_ref.shape[2]

    @pl.when(step == 0)
    def _():
        pre = jnp.zeros((count, 128), F32)
        for k in range(K):
            normed = (xh_ref[k] * gain_ref[k : k + 1, :]).astype(BF16)
            norm_s[k] = normed
            pre = pre + dot(normed, win_ref[k])
        pre_s[...] = pre
        hid_s[...] = (pre / (1.0 + jnp.exp(-pre))).astype(BF16)
        dhid_s[...] = jnp.zeros_like(dhid_s)

    hid = hid_s[...]
    w = wout_ref[...]
    rows = w.shape[0]
    fout = dot(w, hid, NT).reshape(rows // D, D, count)
    grad = g_ref[...].astype(F32).T.reshape(rows // D, D, count)
    mid = fout - jnp.sum(fout, axis=1, keepdims=True) * (1.0 / D)
    oinv = 1.0 / jnp.sqrt(jnp.sum(mid * mid, axis=1, keepdims=True) * (1.0 / D) + EPS)
    chat = mid * oinv
    gm = jnp.sum(grad, axis=1, keepdims=True) * (1.0 / D)
    gc = jnp.sum(grad * chat, axis=1, keepdims=True) * (1.0 / D)
    df = (oinv * (grad - gm - chat * gc)).reshape(rows, count).astype(BF16)
    gout_ref[...] = dot(df, hid).astype(BF16)
    dhid_s[...] += dot(w, df, TN)

    @pl.when(step == pl.num_programs(0) - 1)
    def _():
        pre = pre_s[...]
        sig = 1.0 / (1.0 + jnp.exp(-pre))
        dpre = (dhid_s[...].T * sig * (1.0 + pre * (1.0 - sig))).astype(BF16)
        m1 = jnp.zeros((count, n), F32)
        m2 = jnp.zeros((count, n), F32)
        for k in range(K):
            gin_ref[k] = dot(norm_s[k], dpre, TN)
            dn = dot(dpre, win_ref[k], NT)
            xh = xh_ref[k]
            ggain_ref[k : k + 1, :] = jnp.sum(dn * xh, axis=0, keepdims=True)
            e = dn * gain_ref[k : k + 1, :]
            e_s[k] = e
            m1 = m1 + e
            m2 = m2 + e * xh
        a1 = jnp.sum(m1, axis=1, keepdims=True) * (1.0 / (K * n))
        a2 = jnp.sum(m2, axis=1, keepdims=True) * (1.0 / (K * n))
        inv = inv_ref[:, :1]
        for k in range(K):
            dfm_ref[k] = inv * (e_s[k] - a1 - xh_ref[k] * a2)


def batch(xh, inv, gain, win, wout, out_grad, feats=4):
    k, count, n = xh.shape
    total = wout.shape[0]
    rows = feats * D
    whole = lambda shape: pl.BlockSpec(shape, lambda i: (0,) * len(shape))
    return pl.pallas_call(
        batch_kernel,
        grid=(total // rows,),
        in_specs=[
            whole((k, count, n)),
            whole((count, 128)),
            whole((k, n)),
            whole((k, n, 128)),
            pl.BlockSpec((rows, 128), lambda i: (i, 0)),
            pl.BlockSpec((count, rows), lambda i: (0, i)),
        ],
        out_specs=[
            pl.BlockSpec((rows, 128), lambda i: (i, 0)),
            whole((k, n, 128)),
            whole((k, n)),
            whole((k, count, n)),
        ],
        out_shape=[
            jax.ShapeDtypeStruct((total, 128), BF16),
            jax.ShapeDtypeStruct((k, n, 128), F32),
            jax.ShapeDtypeStruct((k, n), F32),
            jax.ShapeDtypeStruct((k, count, n), F32),
        ],
        scratch_shapes=[
            pltpu.VMEM((count, 128), F32),
            pltpu.VMEM((count, 128), BF16),
            pltpu.VMEM((128, count), F32),
            pltpu.VMEM((k, count, n), BF16),
            pltpu.VMEM((k, count, n), F32),
        ],
        compiler_params=params(),
        cost_estimate=cost(2e10, 2e7),
        name="batch",
    )(xh, inv, gain, win, wout, out_grad)


def last_kernel(
    at_ref, x_ref, s_ref, dl_ref, dfm_ref, wt_ref, keep_ref, send_ref, acc_ref, flo, fhi, dx, both
):
    rows, n = x_ref.shape[0], x_ref.shape[1]

    @pl.when(pl.program_id(0) == 0)
    def _():
        acc_ref[...] = jnp.zeros_like(acc_ref)

    flo[...] = dfm_ref[:, :, :128].reshape(K * rows, 128)
    fhi[...] = dfm_ref[:, :, 128:].reshape(K * rows, 128)
    proj = wt_ref[:K, :]
    shared = wt_ref[...]

    def sample(b, _):
        dfm = jnp.concatenate(
            [flo[pl.ds(b, K, stride=rows), :], fhi[pl.ds(b, K, stride=rows), :]], axis=1
        ).astype(BF16)
        xb = x_ref[b]
        dhi, dlo = split(dot(dfm, xb))
        dl = dl_ref[b]
        low = jnp.concatenate([dhi, dlo, dl], axis=0)
        acc_ref[...] += dot(low, xb, NT)
        left = jnp.concatenate([dfm, dfm, proj, shared], axis=0)
        right = jnp.concatenate([s_ref[b], dlo, dhi, dl], axis=0)
        dx[b] = dot(left, right, TN)
        return 0

    lax.fori_loop(0, rows, sample, 0, unroll=8)

    def turn(j, _):
        at = pl.ds(pl.multiple_of(j * 16, 16), 16)
        lo = jnp.swapaxes(dx[:, at, :128], 0, 1).astype(BF16)
        hi = jnp.swapaxes(dx[:16, at, 128:] + dx[16:, at, 128:], 0, 1).astype(BF16)
        for i in range(16):
            p = at_ref[j * 16 + i]
            both[p, :rows, :] = lo[i]
            both[p, rows:, :] = hi[i]
        return 0

    lax.fori_loop(0, n // 16, turn, 0)
    keep_ref[:, 0] = both[: n // 2]
    send_ref[:, 0] = both[n // 2 :]


def last(at, x3, s, dl, dfm, wt, rows=32):
    count, n, _ = x3.shape
    nl = dl.shape[1]
    out = pl.BlockSpec((n // 2, 1, rows + rows // 2, 128), lambda i, o: (0, i, 0, 0))
    grid = pltpu.PrefetchScalarGridSpec(
        num_scalar_prefetch=1,
        grid=(count // rows,),
        in_specs=[
            pl.BlockSpec((rows, n, DP), lambda i, o: (i, 0, 0)),
            pl.BlockSpec((rows, 2 * K, DP), lambda i, o: (i, 0, 0)),
            pl.BlockSpec((rows, nl, DP), lambda i, o: (i, 0, 0)),
            pl.BlockSpec((K, rows, n), lambda i, o: (0, i, 0)),
            pl.BlockSpec(wt.shape, lambda i, o: (0, 0)),
        ],
        out_specs=[out, out, pl.BlockSpec((2 * K + nl, n), lambda i, o: (0, 0))],
        scratch_shapes=[pltpu.VMEM((K * rows, 128), F32)] * 2
        + [pltpu.VMEM((rows, n, DP), F32), pltpu.VMEM((n, rows + rows // 2, 128), BF16)],
    )
    half = jax.ShapeDtypeStruct((n // 2, count // rows, rows + rows // 2, 128), BF16)
    return pl.pallas_call(
        last_kernel,
        grid_spec=grid,
        out_shape=[half, half, jax.ShapeDtypeStruct((2 * K + nl, n), F32)],
        compiler_params=params(),
        cost_estimate=cost(2e10, count * n * DP * 4),
        name="last",
    )(at, x3, s, dl, dfm, wt)


def sums_kernel(at_ref, mine_ref, other_ref, ids_ref, oid_ref, even_ref, odd_ref):
    tables, steps, height, _ = mine_ref.shape
    part = height // 3
    count = ids_ref.shape[2]
    rows = 2 * count
    iota = lax.broadcasted_iota(jnp.int32, (rows, count), 0)
    low = lax.broadcasted_iota(jnp.int32, (1, 128), 1) < 64
    zero = jnp.zeros((part, 128), BF16)
    for i in range(tables // 2):
        for t, ref in enumerate((even_ref, odd_ref)):
            hot = jnp.concatenate(
                [
                    jnp.where(iota == r[i, t : t + 1, :], 1.0, 0.0).astype(BF16)
                    for r in (ids_ref, oid_ref)
                ],
                axis=1,
            )
            main, rest = [], []
            for r in (mine_ref, other_ref):
                for s in range(steps):
                    tail = r[2 * i + t, s, 2 * part :, :]
                    main.append(r[2 * i + t, s, : 2 * part, :])
                    rest += [jnp.where(low, tail, zero), jnp.where(low, zero, tail)]
            block = jnp.concatenate(
                [jnp.concatenate(main, axis=0), jnp.concatenate(rest, axis=0)], axis=1
            )
            out = dot(hot, block)
            tail = out[:, 128:] + pltpu.roll(out[:, 128:], 64, 1)
            ref[0, 0, i, :rows, :] = out[:, :128].astype(BF16)
            ref[0, 0, i, rows:, :] = jnp.where(low, tail[:count], tail[count:]).astype(BF16)


def sums(at, mine, other, ids, oids, nz, nx):
    tables, steps, height, _ = mine.shape
    count = ids.shape[2]
    ny = tables // (2 * nz * nx)
    data = pl.BlockSpec((2 * ny, steps, height, 128), lambda z, x, at: (z * nx + x, 0, 0, 0))
    index = pl.BlockSpec((ny, 2, count), lambda z, x, at: (z * nx + x, 0, 0))
    grid = pltpu.PrefetchScalarGridSpec(
        num_scalar_prefetch=1,
        grid=(nz, nx),
        in_specs=[data, data, index, index],
        out_specs=[
            pl.BlockSpec(
                (1, 1, ny, 384, 128),
                lambda z, x, at: ((z + nz - at[0]) % nz, (x + nx - at[1]) % nx, 0, 0, 0),
            ),
            pl.BlockSpec(
                (1, 1, ny, 384, 128),
                lambda z, x, at: ((x + nx - at[1]) % nx, (z + nz - at[0]) % nz, 0, 0, 0),
            ),
        ],
    )
    return pl.pallas_call(
        sums_kernel,
        grid_spec=grid,
        out_shape=[
            jax.ShapeDtypeStruct((nz, nx, ny, 384, 128), BF16),
            jax.ShapeDtypeStruct((nx, nz, ny, 384, 128), BF16),
        ],
        compiler_params=params(),
        cost_estimate=cost(1e10, mine.size * 8),
        name="sums",
    )(at, mine, other, ids, oids)


def update_kernel(slot_ref, sum_ref, rows_ref, accum_ref, new_rows_ref, new_accum_ref, acc):
    tables = sum_ref.shape[0]
    state = rows_ref.shape[1]
    rows = state // tables
    half = rows // 2
    for t in range(tables):
        first = slice(t * rows, t * rows + half)
        second = slice(t * rows + half, (t + 1) * rows)
        main = sum_ref[t, :rows, :].astype(F32).T.astype(BF16)
        tail = sum_ref[t, rows:, :].astype(F32).T.astype(BF16)
        acc[:128, t * rows : (t + 1) * rows] = main
        acc[128:, first] = tail[:64]
        acc[128:, second] = tail[64:]
    size = 256
    iota = lax.broadcasted_iota(jnp.int32, (size, state), 0)
    slots = slot_ref[...]
    for i in range(state // size):
        at = slice(i * size, (i + 1) * size)
        hot = jnp.where(iota == slots - i * size, 1.0, 0.0).astype(BF16)
        total = dot(acc[...], hot, NT)
        accum = accum_ref[:, at] + jnp.sum(total * total, axis=0, keepdims=True) * (1.0 / D)
        new_accum_ref[:, at] = accum
        new_rows_ref[:, at] = rows_ref[:, at] - LEARN * total / jnp.sqrt(accum)


def update(slots, sums, table_rows, row_accum):
    state = slots.shape[1]
    return pl.pallas_call(
        update_kernel,
        out_shape=[
            jax.ShapeDtypeStruct((D, state), F32),
            jax.ShapeDtypeStruct((1, state), F32),
        ],
        scratch_shapes=[pltpu.VMEM((D, state), BF16)],
        compiler_params=params(),
        cost_estimate=cost(4e9, state * D * 12),
        name="update",
    )(slots, sums, table_rows, row_accum)


def forward(x3, g2, proj, w_lcb):
    wt = jnp.concatenate([proj.T, w_lcb.T], axis=0)
    return (wt,) + tuple(first(x3, g2, wt))


def layer(samples, out_grad, spot, proj, gain, w_in, w_out, w_lcb):
    n = proj.shape[0]
    nl = w_lcb.shape[1]
    x3 = unfold(samples, n, 0)
    g2 = unfold(out_grad, nl, out_grad.shape[1] // D // nl - 1)
    wt, s, dl, xh, inv = forward(x3, g2, proj, w_lcb)
    gain_t = gain.reshape(n, K).T.astype(F32)
    win_t = w_in.reshape(n, K, 128).transpose(1, 0, 2)
    g_out, g_in, g_gain, dfm = batch(xh, inv, gain_t, win_t, w_out, out_grad)
    keep, send, acc = last(spot, x3, s, dl, dfm, wt)
    return acc[:K] + acc[K : 2 * K], g_gain, g_in, g_out, acc[2 * K :], keep, send


SWAP = [(0, 1), (1, 0)]
WIDE = ("z", "x", "yl")


def gather(a):
    n = 32
    return lax.all_to_all(jnp.broadcast_to(a[None], (n,) + a.shape), WIDE, 0, 0, tiled=True)


def ring_step(axis, by, v):
    n = 4
    return lax.ppermute(v, axis, [(i, (i + by) % n) for i in range(n)])


def add(*terms):
    total = terms[0].astype(F32)
    for term in terms[1:]:
        total = total + term.astype(F32)
    return total.astype(BF16)


def ring_sums(parts):
    fore = [ring_step(axis, 1, v[2, :2]) for axis, v in parts]
    back = [ring_step(axis, -1, v[2, 2:]) for axis, v in parts]
    fore = [
        ring_step(axis, 1, jnp.concatenate([add(v[1, :2], f), v[1, 2:]], axis=0))
        for (axis, v), f in zip(parts, fore)
    ]
    back = [
        ring_step(axis, -1, jnp.concatenate([v[3, :2], add(v[3, 2:], b)], axis=0))
        for (axis, v), b in zip(parts, back)
    ]
    return [add(v[0], f, b) for (_, v), f, b in zip(parts, fore, back)]


def rep_sum(v):
    swap = SWAP
    for axis in ("c", "yh"):
        v = v.astype(BF16)
        v = v.astype(F32) + lax.ppermute(v, axis, swap).astype(F32)
    return v


def body(
    samples, out_grad, row_ids, table_owner, slot_map, proj, gain_flat, w_in, w_out, w_lcb,
    table_rows, row_accum,
):
    owners = 32
    count = samples.shape[0]
    per = proj.shape[0]
    n = per * owners
    nl = w_lcb.shape[1]
    core = lax.axis_index("c")
    small = jnp.concatenate([proj, gain_flat.reshape(per, K), w_lcb], axis=1)
    small = gather(jnp.pad(small, ((0, 8), (0, 128 - small.shape[1]))))[:, :per].reshape(n, 128)
    proj_f = small[:, :K]
    gain_t = small[:, K : 2 * K].T.astype(F32)
    w_lcb_f = small[:, 2 * K : 2 * K + nl]
    shard = jnp.concatenate([w_in, w_out], axis=0)
    rows = shard.shape[0] // 2
    near = gather(lax.dynamic_slice_in_dim(shard, core * rows, rows, 0))
    far = lax.ppermute(near, "c", SWAP)
    lower, upper = jnp.where(core == 0, near, far), jnp.where(core == 0, far, near)
    w_in_t = lower[:, : w_in.shape[0]].reshape(n, K, 128).transpose(1, 0, 2)
    w_out_f = jnp.concatenate([lower[:, w_in.shape[0] :], upper], axis=1).reshape(-1, 128)

    quad = per // 2
    spot = table_owner // per * quad + table_owner % quad
    spot = jnp.where((table_owner % per) // quad == core, spot, spot + n // 2)
    order = jnp.zeros((n,), jnp.int32).at[spot].set(jnp.arange(n, dtype=jnp.int32))
    ids = jnp.take(row_ids.T, order, axis=0).reshape(2, n // 4, 2, count)
    other_ids = lax.ppermute(ids[1], "c", SWAP)

    x3 = unfold(samples, n, 0)
    g2 = unfold(out_grad, nl, out_grad.shape[1] // D // nl - 1)
    wt, score, dl, xh, inv = forward(x3, g2, proj_f, w_lcb_f)
    g_out, g_in, g_gain, dfm = batch(xh, inv, gain_t, w_in_t, w_out_f, out_grad)
    keep, send, acc = last(spot, x3, score, dl, dfm, wt)
    g_proj, g_lcb = acc[:K] + acc[K : 2 * K], acc[2 * K :]
    big = jnp.concatenate(
        [
            g_out.reshape(owners, -1, 128),
            g_in.astype(BF16).transpose(1, 0, 2).reshape(owners, -1, 128),
        ],
        axis=1,
    )
    big = lax.all_to_all(big, WIDE, 0, 0, tiled=True)
    big, send = lax.optimization_barrier((big, send))
    big = rep_sum(jnp.sum(big.astype(F32), axis=0))
    little = jnp.concatenate([g_proj, g_gain, g_lcb], axis=0).T.reshape(owners, per, -1)
    little = lax.all_to_all(little, WIDE, 0, 0, tiled=True)
    little = rep_sum(jnp.sum(little, axis=0))

    other = lax.ppermute(send, "c", SWAP)
    at = jnp.stack([lax.axis_index("z"), lax.axis_index("x")]).astype(jnp.int32)
    even, odd = sums(at, keep, other, ids[0], other_ids, 4, 4)
    even, odd = ring_sums([("z", even), ("x", odd)])
    even, odd = ring_sums([("x", even), ("z", odd)])
    both = jnp.stack([even, odd], axis=1).reshape(2, 1, 2, 2, 384, 128)
    both = jnp.broadcast_to(both, (2, 2, 2, 2, 384, 128)).reshape(4, 4, 384, 128)
    both = lax.all_to_all(both, ("yl", "yh"), 0, 0, tiled=True)
    mine = jnp.sum(both.astype(F32), axis=0).astype(BF16)
    others = lax.ppermute(mine, "c", SWAP)
    owned = jnp.where(
        core == 0, jnp.concatenate([mine, others], axis=0), jnp.concatenate([others, mine], axis=0)
    )
    new_rows, new_accum = update(
        slot_map.reshape(1, -1), owned, table_rows.T, row_accum.reshape(1, -1)
    )
    split_at = w_out.shape[0]
    return (
        little[:, :K],
        little[:, K : 2 * K].reshape(-1),
        big[split_at:],
        big[:split_at],
        little[:, 2 * K :],
        new_rows.T,
        new_accum.reshape(-1),
    )


def solution(mesh):
    cube = Mesh(mesh.devices.reshape(4, 4, 2, 2, 2), ("z", "x", "yl", "yh", "c"))
    batch_spec = P(("z", "x", "yl", "yh", "c"), None)
    two, one = P(WIDE, None), P(WIDE)
    in_specs = (batch_spec,) * 3 + (P(), two, two, one, two, two, two, two, one)
    out_specs = (two, one, two, two, two, two, one)
    return jax.shard_map(body, mesh=cube, in_specs=in_specs, out_specs=out_specs, check_vma=False)
```

```python
import functools

import jax
import jax.numpy as jnp
from jax import lax
from jax.experimental import pallas as pl
from jax.experimental.pallas import tpu as pltpu
from jax.sharding import Mesh, PartitionSpec as P

LEARN = 0.1
EPS = 1e-05
F32 = jnp.float32
BF16 = jnp.bfloat16
D = 192
DP = 256
K = 16
NN = (((1,), (0,)), ((), ()))
NT = (((1,), (1,)), ((), ()))
TN = (((0,), (0,)), ((), ()))


def dot(a, b, dims=NN):
    return lax.dot_general(a, b, dims, preferred_element_type=F32)


def params(mib=56):
    return pltpu.CompilerParams(vmem_limit_bytes=mib * 1024 * 1024)


def cost(flops, nbytes):
    return pl.CostEstimate(flops=int(flops), bytes_accessed=int(nbytes), transcendentals=0)


def split(v):
    hi = v.astype(BF16)
    return hi, (v - hi.astype(F32)).astype(BF16)


def unfold_kernel(x_ref, o_ref):
    tables = o_ref.shape[1]
    low = lax.broadcasted_iota(jnp.int32, (1, 1, 128), 2) < 64

    def group(j, _):
        at = pl.ds(pl.multiple_of(j * 16, 16), 16)
        for h in range(2):
            lo, hi = [], []
            part = slice(16 * h, 16 * h + 16)
            for p in range(8):
                v = x_ref[part, pl.ds(pl.multiple_of(j * 3072 + 384 * p, 128), 384)].astype(F32)
                w = pltpu.roll(v, 192, 1)
                lo += [v[:, :128], w[:, :128]]
                if h == 0:
                    hi += [v[:, 128:256], w[:, 128:256]]
                else:
                    hi += [pltpu.roll(v[:, 128:256], 64, 1), v[:, 256:]]
            hi = jnp.swapaxes(jnp.stack(hi), 0, 1)
            hi = jnp.where(low, hi, 0.0) if h == 0 else jnp.where(low, 0.0, hi)
            o_ref[part, at, :128] = jnp.swapaxes(jnp.stack(lo), 0, 1).astype(BF16)
            o_ref[part, at, 128:] = hi.astype(BF16)
        return 0

    lax.fori_loop(0, tables // 16, group, 0)


def unfold(x, tables, first, rows=32):
    count = x.shape[0]
    return pl.pallas_call(
        unfold_kernel,
        grid=(count // rows,),
        in_specs=[pl.BlockSpec((rows, tables * D), lambda i: (i, first))],
        out_specs=pl.BlockSpec((rows, tables, DP), lambda i: (i, 0, 0)),
        out_shape=jax.ShapeDtypeStruct((count, tables, DP), BF16),
        compiler_params=params(),
        cost_estimate=cost(1e9, count * tables * 900),
        name="unfold",
    )(x)


def first_kernel(x_ref, g_ref, w_ref, s_ref, dl_ref, xh_ref, inv_ref, lo, hi):
    rows = x_ref.shape[0]
    n = x_ref.shape[1]
    w = w_ref[...]
    lane = lax.broadcasted_iota(jnp.int32, (1, DP), 1)
    half = (pl.program_id(0) * rows // 16) % 2
    keep = (lane < 128) | ((lane >= 128 + 64 * half) & (lane < 192 + 64 * half))
    total = lambda v: jnp.sum(jnp.sum(v, axis=0, keepdims=True), axis=1, keepdims=True)
    for b in range(rows):
        xb = x_ref[b]
        r = dot(w, xb)
        shi, slo = split(r[:K])
        s_ref[b, :K, :] = shi
        s_ref[b, K:, :] = slo
        f2 = dot(jnp.concatenate([shi, slo], axis=0), xb, NT)
        fm = f2[:K] + f2[K:]
        c = fm - total(fm) * (1.0 / (K * n))
        inv = 1.0 / jnp.sqrt(total(c * c) * (1.0 / (K * n)) + EPS)
        inv_ref[b : b + 1, :] = jnp.broadcast_to(inv, (1, 128))
        xh = c * inv
        lo[pl.ds(b, K, stride=rows), :] = xh[:, :128]
        hi[pl.ds(b, K, stride=rows), :] = xh[:, 128:]
        lout = r[K:]
        grad = g_ref[b].astype(F32)
        mid = jnp.where(keep, lout - jnp.sum(lout, axis=1, keepdims=True) * (1.0 / D), 0.0)
        oinv = 1.0 / jnp.sqrt(jnp.sum(mid * mid, axis=1, keepdims=True) * (1.0 / D) + EPS)
        chat = mid * oinv
        gm = jnp.sum(grad, axis=1, keepdims=True) * (1.0 / D)
        gc = jnp.sum(grad * chat, axis=1, keepdims=True) * (1.0 / D)
        dl_ref[b] = jnp.where(keep, oinv * (grad - gm - chat * gc), 0.0).astype(BF16)
    xh_ref[:, :, :128] = lo[...].reshape(K, rows, 128)
    xh_ref[:, :, 128:] = hi[...].reshape(K, rows, 128)


def first(x3, g2, wt, rows=8):
    count, n, _ = x3.shape
    nl = g2.shape[1]
    return pl.pallas_call(
        first_kernel,
        grid=(count // rows,),
        in_specs=[
            pl.BlockSpec((rows, n, DP), lambda i: (i, 0, 0)),
            pl.BlockSpec((rows, nl, DP), lambda i: (i, 0, 0)),
            pl.BlockSpec(wt.shape, lambda i: (0, 0)),
        ],
        out_specs=[
            pl.BlockSpec((rows, 2 * K, DP), lambda i: (i, 0, 0)),
            pl.BlockSpec((rows, nl, DP), lambda i: (i, 0, 0)),
            pl.BlockSpec((K, rows, n), lambda i: (0, i, 0)),
            pl.BlockSpec((rows, 128), lambda i: (i, 0)),
        ],
        out_shape=[
            jax.ShapeDtypeStruct((count, 2 * K, DP), BF16),
            jax.ShapeDtypeStruct((count, nl, DP), BF16),
            jax.ShapeDtypeStruct((K, count, n), F32),
            jax.ShapeDtypeStruct((count, 128), F32),
        ],
        scratch_shapes=[pltpu.VMEM((K * rows, 128), F32)] * 2,
        compiler_params=params(),
        cost_estimate=cost(2e10, count * n * DP * 2),
        name="first",
    )(x3, g2, wt)


def batch_kernel(
    xh_ref, inv_ref, gain_ref, win_ref, wout_ref, g_ref,
    gout_ref, gin_ref, ggain_ref, dfm_ref, pre_s, hid_s, dhid_s, norm_s, e_s,
):
    step = pl.program_id(0)
    count, n = xh_ref.shape[1], xh_ref.shape[2]

    @pl.when(step == 0)
    def _():
        pre = jnp.zeros((count, 128), F32)
        for k in range(K):
            normed = (xh_ref[k] * gain_ref[k : k + 1, :]).astype(BF16)
            norm_s[k] = normed
            pre = pre + dot(normed, win_ref[k])
        pre_s[...] = pre
        hid_s[...] = (pre / (1.0 + jnp.exp(-pre))).astype(BF16)
        dhid_s[...] = jnp.zeros_like(dhid_s)

    hid = hid_s[...]
    w = wout_ref[...]
    rows = w.shape[0]
    fout = dot(w, hid, NT).reshape(rows // D, D, count)
    grad = g_ref[...].astype(F32).T.reshape(rows // D, D, count)
    mid = fout - jnp.sum(fout, axis=1, keepdims=True) * (1.0 / D)
    oinv = 1.0 / jnp.sqrt(jnp.sum(mid * mid, axis=1, keepdims=True) * (1.0 / D) + EPS)
    chat = mid * oinv
    gm = jnp.sum(grad, axis=1, keepdims=True) * (1.0 / D)
    gc = jnp.sum(grad * chat, axis=1, keepdims=True) * (1.0 / D)
    df = (oinv * (grad - gm - chat * gc)).reshape(rows, count).astype(BF16)
    gout_ref[...] = dot(df, hid).astype(BF16)
    dhid_s[...] += dot(w, df, TN)

    @pl.when(step == pl.num_programs(0) - 1)
    def _():
        pre = pre_s[...]
        sig = 1.0 / (1.0 + jnp.exp(-pre))
        dpre = (dhid_s[...].T * sig * (1.0 + pre * (1.0 - sig))).astype(BF16)
        m1 = jnp.zeros((count, n), F32)
        m2 = jnp.zeros((count, n), F32)
        for k in range(K):
            gin_ref[k] = dot(norm_s[k], dpre, TN)
            dn = dot(dpre, win_ref[k], NT)
            xh = xh_ref[k]
            ggain_ref[k : k + 1, :] = jnp.sum(dn * xh, axis=0, keepdims=True)
            e = dn * gain_ref[k : k + 1, :]
            e_s[k] = e
            m1 = m1 + e
            m2 = m2 + e * xh
        a1 = jnp.sum(m1, axis=1, keepdims=True) * (1.0 / (K * n))
        a2 = jnp.sum(m2, axis=1, keepdims=True) * (1.0 / (K * n))
        inv = inv_ref[:, :1]
        for k in range(K):
            dfm_ref[k] = inv * (e_s[k] - a1 - xh_ref[k] * a2)


def batch(xh, inv, gain, win, wout, out_grad, feats=4):
    k, count, n = xh.shape
    total = wout.shape[0]
    rows = feats * D
    whole = lambda shape: pl.BlockSpec(shape, lambda i: (0,) * len(shape))
    return pl.pallas_call(
        batch_kernel,
        grid=(total // rows,),
        in_specs=[
            whole((k, count, n)),
            whole((count, 128)),
            whole((k, n)),
            whole((k, n, 128)),
            pl.BlockSpec((rows, 128), lambda i: (i, 0)),
            pl.BlockSpec((count, rows), lambda i: (0, i)),
        ],
        out_specs=[
            pl.BlockSpec((rows, 128), lambda i: (i, 0)),
            whole((k, n, 128)),
            whole((k, n)),
            whole((k, count, n)),
        ],
        out_shape=[
            jax.ShapeDtypeStruct((total, 128), BF16),
            jax.ShapeDtypeStruct((k, n, 128), F32),
            jax.ShapeDtypeStruct((k, n), F32),
            jax.ShapeDtypeStruct((k, count, n), F32),
        ],
        scratch_shapes=[
            pltpu.VMEM((count, 128), F32),
            pltpu.VMEM((count, 128), BF16),
            pltpu.VMEM((128, count), F32),
            pltpu.VMEM((k, count, n), BF16),
            pltpu.VMEM((k, count, n), F32),
        ],
        compiler_params=params(),
        cost_estimate=cost(2e10, 2e7),
        name="batch",
    )(xh, inv, gain, win, wout, out_grad)


def last_kernel(
    at_ref, x_ref, s_ref, dl_ref, dfm_ref, wt_ref, keep_ref, send_ref, acc_ref, flo, fhi, dx, both
):
    rows, n = x_ref.shape[0], x_ref.shape[1]

    @pl.when(pl.program_id(0) == 0)
    def _():
        acc_ref[...] = jnp.zeros_like(acc_ref)

    flo[...] = dfm_ref[:, :, :128].reshape(K * rows, 128)
    fhi[...] = dfm_ref[:, :, 128:].reshape(K * rows, 128)
    proj = wt_ref[:K, :]
    shared = wt_ref[...]

    def sample(b, _):
        dfm = jnp.concatenate(
            [flo[pl.ds(b, K, stride=rows), :], fhi[pl.ds(b, K, stride=rows), :]], axis=1
        ).astype(BF16)
        xb = x_ref[b]
        dhi, dlo = split(dot(dfm, xb))
        dl = dl_ref[b]
        low = jnp.concatenate([dhi, dlo, dl], axis=0)
        acc_ref[...] += dot(low, xb, NT)
        left = jnp.concatenate([dfm, dfm, proj, shared], axis=0)
        right = jnp.concatenate([s_ref[b], dlo, dhi, dl], axis=0)
        dx[b] = dot(left, right, TN)
        return 0

    lax.fori_loop(0, rows, sample, 0, unroll=8)

    def turn(j, _):
        at = pl.ds(pl.multiple_of(j * 16, 16), 16)
        lo = jnp.swapaxes(dx[:, at, :128], 0, 1).astype(BF16)
        hi = jnp.swapaxes(dx[:16, at, 128:] + dx[16:, at, 128:], 0, 1).astype(BF16)
        for i in range(16):
            p = at_ref[j * 16 + i]
            both[p, :rows, :] = lo[i]
            both[p, rows:, :] = hi[i]
        return 0

    lax.fori_loop(0, n // 16, turn, 0)
    keep_ref[:, 0] = both[: n // 2]
    send_ref[:, 0] = both[n // 2 :]


def last(at, x3, s, dl, dfm, wt, rows=32):
    count, n, _ = x3.shape
    nl = dl.shape[1]
    out = pl.BlockSpec((n // 2, 1, rows + rows // 2, 128), lambda i, o: (0, i, 0, 0))
    grid = pltpu.PrefetchScalarGridSpec(
        num_scalar_prefetch=1,
        grid=(count // rows,),
        in_specs=[
            pl.BlockSpec((rows, n, DP), lambda i, o: (i, 0, 0)),
            pl.BlockSpec((rows, 2 * K, DP), lambda i, o: (i, 0, 0)),
            pl.BlockSpec((rows, nl, DP), lambda i, o: (i, 0, 0)),
            pl.BlockSpec((K, rows, n), lambda i, o: (0, i, 0)),
            pl.BlockSpec(wt.shape, lambda i, o: (0, 0)),
        ],
        out_specs=[out, out, pl.BlockSpec((2 * K + nl, n), lambda i, o: (0, 0))],
        scratch_shapes=[pltpu.VMEM((K * rows, 128), F32)] * 2
        + [pltpu.VMEM((rows, n, DP), F32), pltpu.VMEM((n, rows + rows // 2, 128), BF16)],
    )
    half = jax.ShapeDtypeStruct((n // 2, count // rows, rows + rows // 2, 128), BF16)
    return pl.pallas_call(
        last_kernel,
        grid_spec=grid,
        out_shape=[half, half, jax.ShapeDtypeStruct((2 * K + nl, n), F32)],
        compiler_params=params(),
        cost_estimate=cost(2e10, count * n * DP * 4),
        name="last",
    )(at, x3, s, dl, dfm, wt)


def sums_kernel(at_ref, mine_ref, other_ref, ids_ref, oid_ref, small_ref, a_ref, b_ref, c_ref):
    tables, steps, height, _ = mine_ref.shape
    part = height // 3
    count = ids_ref.shape[2]
    rows = 2 * count
    iota = lax.broadcasted_iota(jnp.int32, (rows, count), 0).astype(F32).astype(BF16)
    one, none = jnp.ones((rows, count), BF16), jnp.zeros((rows, count), BF16)
    low = lax.broadcasted_iota(jnp.int32, (1, 128), 1) < 64
    zero = jnp.zeros((part, 128), BF16)
    b_ref[0, 0, :, 96:112, :] = small_ref[0, 0]
    for i in range(tables // 2):
        for t in range(2):
            hot = jnp.concatenate(
                [
                    jnp.where(iota == r[i, t : t + 1, :].astype(F32).astype(BF16), one, none)
                    for r in (ids_ref, oid_ref)
                ],
                axis=1,
            )
            main, rest = [], []
            for r in (mine_ref, other_ref):
                for s in range(steps):
                    tail = r[2 * i + t, s, 2 * part :, :]
                    main.append(r[2 * i + t, s, : 2 * part, :])
                    rest += [jnp.where(low, tail, zero), jnp.where(low, zero, tail)]
            block = jnp.concatenate(
                [jnp.concatenate(main, axis=0), jnp.concatenate(rest, axis=0)], axis=1
            )
            out = dot(hot, block)
            tail = out[:, 128:] + pltpu.roll(out[:, 128:], 64, 1)
            main = out[:, :128].astype(BF16)
            tail = jnp.where(low, tail[:count], tail[count:]).astype(BF16)
            if t == 0:
                a_ref[0, 0, i, :256, :] = main
                a_ref[0, 0, i, 256:, :] = tail[:32]
                b_ref[0, 0, i, :96, :] = tail[32:]
            else:
                b_ref[0, 0, i, 112:, :] = main[:160]
                c_ref[i, 0, 0, :96, :] = main[160:]
                c_ref[i, 0, 0, 96:, :] = tail


def sums(at, mine, other, ids, oids, small):
    tables, steps, height, _ = mine.shape
    count = ids.shape[2]
    nz, nx, ny = small.shape[:3]
    extra = small.shape[3]
    data = pl.BlockSpec((2 * ny, steps, height, 128), lambda z, x, at: (z * nx + x, 0, 0, 0))
    index = pl.BlockSpec((ny, 2, count), lambda z, x, at: (z * nx + x, 0, 0))
    grid = pltpu.PrefetchScalarGridSpec(
        num_scalar_prefetch=1,
        grid=(nz, nx),
        in_specs=[
            data, data, index, index,
            pl.BlockSpec((1, 1, ny, extra, 128), lambda z, x, at: (z, x, 0, 0, 0)),
        ],
        out_specs=[
            pl.BlockSpec(
                (1, 1, ny, 288, 128),
                lambda z, x, at: ((z + nz - at[0]) % nz, (x + nx - at[1]) % nx, 0, 0, 0),
            ),
            pl.BlockSpec(
                (1, 1, ny, 272, 128),
                lambda z, x, at: ((x + nx - at[1]) % nx, (z + nz - at[0]) % nz, 0, 0, 0),
            ),
            pl.BlockSpec((ny, 1, 1, 224, 128), lambda z, x, at: (0, z, x, 0, 0)),
        ],
    )
    return pl.pallas_call(
        sums_kernel,
        grid_spec=grid,
        out_shape=[
            jax.ShapeDtypeStruct((nz, nx, ny, 288, 128), BF16),
            jax.ShapeDtypeStruct((nx, nz, ny, 272, 128), BF16),
            jax.ShapeDtypeStruct((ny, nz, nx, 224, 128), BF16),
        ],
        compiler_params=params(),
        cost_estimate=cost(1e10, mine.size * 8),
        name="sums",
    )(at, mine, other, ids, oids, small)


def update_kernel(slot_ref, sum_ref, rows_ref, accum_ref, new_rows_ref, new_accum_ref, acc):
    cores, runs, height, _ = sum_ref.shape
    tables = 2 * cores * runs
    state = rows_ref.shape[1]
    rows = state // tables
    half = rows // 2
    for t in range(tables):
        where = t // 2 // runs, t // 2 % runs
        base = (t % 2) * (height - 384)
        first = slice(t * rows, t * rows + half)
        second = slice(t * rows + half, (t + 1) * rows)
        main = sum_ref[where + (slice(base, base + rows),)].astype(F32).T.astype(BF16)
        tail = sum_ref[where + (slice(base + rows, base + 384),)].astype(F32).T.astype(BF16)
        acc[:128, t * rows : (t + 1) * rows] = main
        acc[128:, first] = tail[:64]
        acc[128:, second] = tail[64:]
    size = 256
    iota = lax.broadcasted_iota(jnp.int32, (size, state), 0)
    slots = slot_ref[...]
    for i in range(state // size):
        at = slice(i * size, (i + 1) * size)
        hot = jnp.where(iota == slots - i * size, 1.0, 0.0).astype(BF16)
        total = dot(acc[...], hot, NT)
        accum = accum_ref[:, at] + jnp.sum(total * total, axis=0, keepdims=True) * (1.0 / D)
        new_accum_ref[:, at] = accum
        new_rows_ref[:, at] = rows_ref[:, at] - LEARN * total / jnp.sqrt(accum)


def update(slots, sums, table_rows, row_accum):
    state = slots.shape[1]
    return pl.pallas_call(
        update_kernel,
        out_shape=[
            jax.ShapeDtypeStruct((D, state), F32),
            jax.ShapeDtypeStruct((1, state), F32),
        ],
        scratch_shapes=[pltpu.VMEM((D, state), BF16)],
        compiler_params=params(),
        cost_estimate=cost(4e9, state * D * 12),
        name="update",
    )(slots, sums, table_rows, row_accum)


def forward(x3, g2, proj, w_lcb):
    wt = jnp.concatenate([proj.T, w_lcb.T], axis=0)
    return (wt,) + tuple(first(x3, g2, wt))


def layer(samples, out_grad, spot, proj, gain, w_in, w_out, w_lcb):
    n = proj.shape[0]
    nl = w_lcb.shape[1]
    x3 = unfold(samples, n, 0)
    g2 = unfold(out_grad, nl, out_grad.shape[1] // D // nl - 1)
    wt, s, dl, xh, inv = forward(x3, g2, proj, w_lcb)
    gain_t = gain.reshape(n, K).T.astype(F32)
    win_t = w_in.reshape(n, K, 128).transpose(1, 0, 2)
    g_out, g_in, g_gain, dfm = batch(xh, inv, gain_t, win_t, w_out, out_grad)
    keep, send, acc = last(spot, x3, s, dl, dfm, wt)
    return acc[:K] + acc[K : 2 * K], g_gain, g_in, g_out, acc[2 * K :], keep, send


SWAP = [(0, 1), (1, 0)]
WIDE = ("z", "x", "yl")


def gather(a):
    n = 32
    return lax.all_to_all(jnp.broadcast_to(a[None], (n,) + a.shape), WIDE, 0, 0, tiled=True)


def ring_step(axis, by, v):
    n = 4
    return lax.ppermute(v, axis, [(i, (i + by) % n) for i in range(n)])


def add(*terms):
    total = terms[0].astype(F32)
    for term in terms[1:]:
        total = total + term.astype(F32)
    return total.astype(BF16)


def ring_sums(parts):
    fore = [ring_step(axis, 1, v[2, :2]) for axis, v in parts]
    back = [ring_step(axis, -1, v[2, 2:]) for axis, v in parts]
    fore = [
        ring_step(axis, 1, jnp.concatenate([add(v[1, :2], f), v[1, 2:]], axis=0))
        for (axis, v), f in zip(parts, fore)
    ]
    back = [
        ring_step(axis, -1, jnp.concatenate([v[3, :2], add(v[3, 2:], b)], axis=0))
        for (axis, v), b in zip(parts, back)
    ]
    return [add(v[0], f, b) for (_, v), f, b in zip(parts, fore, back)]


def body(
    samples, out_grad, row_ids, table_owner, slot_map, proj, gain_flat, w_in, w_out, w_lcb,
    table_rows, row_accum,
):
    owners = 32
    count = samples.shape[0]
    per = proj.shape[0]
    n = per * owners
    nl = w_lcb.shape[1]
    core = lax.axis_index("c")
    small = jnp.concatenate([proj, gain_flat.reshape(per, K), w_lcb], axis=1)
    small = jnp.pad(small, ((0, 8), (0, 128 - small.shape[1])))
    shard = jnp.concatenate([w_in, w_out], axis=0)
    rows = shard.shape[0] // 2
    near = jnp.concatenate([lax.dynamic_slice_in_dim(shard, core * rows, rows, 0), small], axis=0)
    x3 = unfold(samples, n, 0)
    g2 = unfold(out_grad, nl, out_grad.shape[1] // D // nl - 1)
    near, x3, g2 = lax.optimization_barrier((gather(near), x3, g2))
    small = near[:, rows : rows + per].reshape(n, 128)
    proj_f = small[:, :K]
    gain_t = small[:, K : 2 * K].T.astype(F32)
    w_lcb_f = small[:, 2 * K : 2 * K + nl]
    near = near[:, :rows]
    far = lax.ppermute(near, "c", SWAP)
    lower, upper = jnp.where(core == 0, near, far), jnp.where(core == 0, far, near)
    w_in_t = lower[:, : w_in.shape[0]].reshape(n, K, 128).transpose(1, 0, 2)
    w_out_f = jnp.concatenate([lower[:, w_in.shape[0] :], upper], axis=1).reshape(-1, 128)

    quad = per // 2
    spot = table_owner // per * quad + table_owner % quad
    spot = jnp.where((table_owner % per) // quad == core, spot, spot + n // 2)
    order = jnp.zeros((n,), jnp.int32).at[spot].set(jnp.arange(n, dtype=jnp.int32))
    ids = jnp.take(row_ids.T, order, axis=0).reshape(2, n // 4, 2, count)
    other_ids = lax.ppermute(ids[1], "c", SWAP)

    wt, score, dl, xh, inv = forward(x3, g2, proj_f, w_lcb_f)
    g_out, g_in, g_gain, dfm = batch(xh, inv, gain_t, w_in_t, w_out_f, out_grad)
    w_grads = jnp.concatenate(
        [
            g_out.reshape(owners, -1, 128),
            g_in.astype(BF16).transpose(1, 0, 2).reshape(owners, -1, 128),
        ],
        axis=1,
    )
    top, bottom = w_grads[:, :rows], w_grads[:, rows:]
    theirs = lax.ppermute(jnp.where(core == 0, bottom, top), "c", SWAP)
    w_grads = add(jnp.where(core == 0, top, bottom), theirs)
    w_grads, dfm = lax.optimization_barrier((w_grads, dfm))
    w_grads = lax.all_to_all(w_grads, WIDE, 0, 0, tiled=True)
    keep, send, acc = last(spot, x3, score, dl, dfm, wt)
    w_grads, send = lax.optimization_barrier((w_grads, send))
    g_proj, g_lcb = acc[:K] + acc[K : 2 * K], acc[2 * K :]
    little = jnp.concatenate([g_proj, g_gain, g_lcb], axis=0).T.reshape(4, 4, 2, 1, per, -1)
    pad = ((0, 0),) * 3 + ((0, 1), (0, 8), (0, 128 - little.shape[-1]))
    little = jnp.pad(little.astype(BF16), pad).reshape(4, 4, 4, 16, 128)

    other = lax.ppermute(send, "c", SWAP)
    at = jnp.stack([lax.axis_index("z"), lax.axis_index("x")]).astype(jnp.int32)
    a, b, c = sums(at, keep, other, ids[0], other_ids, little)
    c = lax.all_to_all(c, ("yl", "yh"), 0, 0, tiled=True)
    a, b = ring_sums([("z", a), ("x", b)])
    c = jnp.sum(c.astype(F32), axis=0).astype(BF16)
    a, b, c = lax.optimization_barrier((a, b, c))
    c = lax.all_to_all(c.reshape((16,) + c.shape[2:]), ("z", "x"), 0, 0, tiled=True)
    a, b = ring_sums([("x", a), ("z", b)])
    c = jnp.sum(c.astype(F32), axis=0).astype(BF16)
    w_grads = jnp.sum(w_grads.astype(F32), axis=0).astype(BF16)
    w_grads = w_grads.astype(F32) + lax.ppermute(w_grads, "yh", SWAP).astype(F32)
    w_theirs = lax.ppermute(w_grads, "c", SWAP)
    low, high = jnp.where(core == 0, w_grads, w_theirs), jnp.where(core == 0, w_theirs, w_grads)
    big = jnp.concatenate([low, high], axis=0)
    a, b, c, big = lax.optimization_barrier((a, b, c, big))
    ab = jnp.concatenate([a, b], axis=1)
    ab = ab.reshape((2, 1, 2) + ab.shape[1:])
    here = (jnp.arange(2)[:, None] == lax.axis_index("yl")) & (
        jnp.arange(2)[None, :] == lax.axis_index("yh")
    )
    c = jnp.where(here.reshape(2, 1, 2, 1, 1), c, jnp.zeros_like(c))
    both = jnp.concatenate(
        [jnp.broadcast_to(v, (2, 2, 2) + v.shape[3:]) for v in (ab, c)], axis=3
    )
    both = both.reshape((4, 2) + both.shape[3:])
    both = lax.all_to_all(both, ("yl", "yh"), 0, 0, tiled=True)
    mine = jnp.sum(both.astype(F32), axis=0).astype(BF16)
    others = lax.ppermute(mine, "c", SWAP)
    owned = jnp.where(core == 0, jnp.stack([mine, others]), jnp.stack([others, mine]))
    little = (mine[0, 384:392].astype(F32) + others[0, 384:392].astype(F32))[:, : 2 * K + nl]
    new_rows, new_accum = update(
        slot_map.reshape(1, -1), owned, table_rows.T, row_accum.reshape(1, -1)
    )
    split_at = w_out.shape[0]
    return (
        little[:, :K],
        little[:, K : 2 * K].reshape(-1),
        big[split_at:],
        big[:split_at],
        little[:, 2 * K :],
        new_rows.T,
        new_accum.reshape(-1),
    )


def solution(mesh):
    cube = Mesh(mesh.devices.reshape(4, 4, 2, 2, 2), ("z", "x", "yl", "yh", "c"))
    batch_spec = P(("z", "x", "yl", "yh", "c"), None)
    two, one = P(WIDE, None), P(WIDE)
    in_specs = (batch_spec,) * 3 + (P(), two, two, one, two, two, two, two, one)
    out_specs = (two, one, two, two, two, two, one)
    return jax.shard_map(body, mesh=cube, in_specs=in_specs, out_specs=out_specs, check_vma=False)
```

```python
import functools

import jax
import jax.numpy as jnp
from jax import lax
from jax.experimental import pallas as pl
from jax.experimental.pallas import tpu as pltpu
from jax.sharding import Mesh, PartitionSpec as P

LEARN = 0.1
EPS = 1e-05
F32 = jnp.float32
BF16 = jnp.bfloat16
D = 192
DP = 256
K = 16
NN = (((1,), (0,)), ((), ()))
NT = (((1,), (1,)), ((), ()))
TN = (((0,), (0,)), ((), ()))


def dot(a, b, dims=NN):
    return lax.dot_general(a, b, dims, preferred_element_type=F32)


def params(mib=56):
    return pltpu.CompilerParams(vmem_limit_bytes=mib * 1024 * 1024)


def cost(flops, nbytes):
    return pl.CostEstimate(flops=int(flops), bytes_accessed=int(nbytes), transcendentals=0)


def split(v):
    hi = v.astype(BF16)
    return hi, (v - hi.astype(F32)).astype(BF16)


def unfold_kernel(x_ref, o_ref):
    tables = o_ref.shape[1]
    low = lax.broadcasted_iota(jnp.int32, (1, 1, 128), 2) < 64

    def group(j, _):
        at = pl.ds(pl.multiple_of(j * 16, 16), 16)
        for h in range(2):
            lo, hi = [], []
            part = slice(16 * h, 16 * h + 16)
            for p in range(8):
                v = x_ref[part, pl.ds(pl.multiple_of(j * 3072 + 384 * p, 128), 384)].astype(F32)
                w = pltpu.roll(v, 192, 1)
                lo += [v[:, :128], w[:, :128]]
                if h == 0:
                    hi += [v[:, 128:256], w[:, 128:256]]
                else:
                    hi += [pltpu.roll(v[:, 128:256], 64, 1), v[:, 256:]]
            hi = jnp.swapaxes(jnp.stack(hi), 0, 1)
            hi = jnp.where(low, hi, 0.0) if h == 0 else jnp.where(low, 0.0, hi)
            o_ref[part, at, :128] = jnp.swapaxes(jnp.stack(lo), 0, 1).astype(BF16)
            o_ref[part, at, 128:] = hi.astype(BF16)
        return 0

    lax.fori_loop(0, tables // 16, group, 0)


def unfold(x, tables, first, rows=32):
    count = x.shape[0]
    return pl.pallas_call(
        unfold_kernel,
        grid=(count // rows,),
        in_specs=[pl.BlockSpec((rows, tables * D), lambda i: (i, first))],
        out_specs=pl.BlockSpec((rows, tables, DP), lambda i: (i, 0, 0)),
        out_shape=jax.ShapeDtypeStruct((count, tables, DP), BF16),
        compiler_params=params(),
        cost_estimate=cost(1e9, count * tables * 900),
        name="unfold",
    )(x)


def first_kernel(x_ref, g_ref, w_ref, s_ref, dl_ref, xh_ref, inv_ref, lo, hi):
    rows = x_ref.shape[0]
    n = x_ref.shape[1]
    w = w_ref[...]
    lane = lax.broadcasted_iota(jnp.int32, (1, DP), 1)
    half = (pl.program_id(0) * rows // 16) % 2
    keep = (lane < 128) | ((lane >= 128 + 64 * half) & (lane < 192 + 64 * half))
    total = lambda v: jnp.sum(jnp.sum(v, axis=0, keepdims=True), axis=1, keepdims=True)
    for b in range(rows):
        xb = x_ref[b]
        r = dot(w, xb)
        shi, slo = split(r[:K])
        s_ref[b, :K, :] = shi
        s_ref[b, K:, :] = slo
        f2 = dot(jnp.concatenate([shi, slo], axis=0), xb, NT)
        fm = f2[:K] + f2[K:]
        c = fm - total(fm) * (1.0 / (K * n))
        inv = 1.0 / jnp.sqrt(total(c * c) * (1.0 / (K * n)) + EPS)
        inv_ref[b : b + 1, :] = jnp.broadcast_to(inv, (1, 128))
        xh = c * inv
        lo[pl.ds(b, K, stride=rows), :] = xh[:, :128]
        hi[pl.ds(b, K, stride=rows), :] = xh[:, 128:]
        lout = r[K:]
        grad = g_ref[b].astype(F32)
        mid = jnp.where(keep, lout - jnp.sum(lout, axis=1, keepdims=True) * (1.0 / D), 0.0)
        oinv = 1.0 / jnp.sqrt(jnp.sum(mid * mid, axis=1, keepdims=True) * (1.0 / D) + EPS)
        chat = mid * oinv
        gm = jnp.sum(grad, axis=1, keepdims=True) * (1.0 / D)
        gc = jnp.sum(grad * chat, axis=1, keepdims=True) * (1.0 / D)
        dl_ref[b] = jnp.where(keep, oinv * (grad - gm - chat * gc), 0.0).astype(BF16)
    xh_ref[:, :, :128] = lo[...].reshape(K, rows, 128)
    xh_ref[:, :, 128:] = hi[...].reshape(K, rows, 128)


def first(x3, g2, wt, rows=16):
    count, n, _ = x3.shape
    nl = g2.shape[1]
    return pl.pallas_call(
        first_kernel,
        grid=(count // rows,),
        in_specs=[
            pl.BlockSpec((rows, n, DP), lambda i: (i, 0, 0)),
            pl.BlockSpec((rows, nl, DP), lambda i: (i, 0, 0)),
            pl.BlockSpec(wt.shape, lambda i: (0, 0)),
        ],
        out_specs=[
            pl.BlockSpec((rows, 2 * K, DP), lambda i: (i, 0, 0)),
            pl.BlockSpec((rows, nl, DP), lambda i: (i, 0, 0)),
            pl.BlockSpec((K, rows, n), lambda i: (0, i, 0)),
            pl.BlockSpec((rows, 128), lambda i: (i, 0)),
        ],
        out_shape=[
            jax.ShapeDtypeStruct((count, 2 * K, DP), BF16),
            jax.ShapeDtypeStruct((count, nl, DP), BF16),
            jax.ShapeDtypeStruct((K, count, n), F32),
            jax.ShapeDtypeStruct((count, 128), F32),
        ],
        scratch_shapes=[pltpu.VMEM((K * rows, 128), F32)] * 2,
        compiler_params=params(),
        cost_estimate=cost(2e10, count * n * DP * 2),
        name="first",
    )(x3, g2, wt)


def batch_kernel(
    core_ref, xh_ref, inv_ref, gain_ref, nraw_ref, fraw_ref, near_ref, far_ref, g_ref,
    gout_ref, gin_ref, ggain_ref, dfm_ref, pre_s, hid_s, dhid_s, norm_s, e_s, win_ref, gin_s,
):
    step = pl.program_id(0)
    count, n = xh_ref.shape[1], xh_ref.shape[2]
    owners = nraw_ref.shape[0]
    per = n // owners
    first_core = core_ref[0] == 0

    @pl.when(step == 0)
    def _():
        for o in range(owners):
            v = jnp.where(first_core, nraw_ref[o], fraw_ref[o]).astype(F32)
            v = jnp.swapaxes(v.reshape(per, K, 128), 0, 1)
            win_ref[:, o * per : (o + 1) * per, :] = v
        pre = jnp.zeros((count, 128), F32)
        for k in range(K):
            normed = (xh_ref[k] * gain_ref[k : k + 1, :]).astype(BF16)
            norm_s[k] = normed
            pre = pre + dot(normed, win_ref[k].astype(BF16))
        pre_s[...] = pre
        hid_s[...] = (pre / (1.0 + jnp.exp(-pre))).astype(BF16)
        dhid_s[...] = jnp.zeros_like(dhid_s)

    hid = hid_s[...]
    near, far = near_ref[...], far_ref[...]
    lower = jnp.where(first_core, near[:, per * K :], far[:, per * K :])
    w = jnp.concatenate([lower, jnp.where(first_core, far, near)], axis=1).reshape(-1, 128)
    rows = w.shape[0]
    fout = dot(w, hid, NT).reshape(rows // D, D, count)
    grad = g_ref[...].astype(F32).T.reshape(rows // D, D, count)
    mid = fout - jnp.sum(fout, axis=1, keepdims=True) * (1.0 / D)
    oinv = 1.0 / jnp.sqrt(jnp.sum(mid * mid, axis=1, keepdims=True) * (1.0 / D) + EPS)
    chat = mid * oinv
    gm = jnp.sum(grad, axis=1, keepdims=True) * (1.0 / D)
    gc = jnp.sum(grad * chat, axis=1, keepdims=True) * (1.0 / D)
    df = (oinv * (grad - gm - chat * gc)).reshape(rows, count).astype(BF16)
    gout_ref[...] = dot(df, hid).astype(BF16)
    dhid_s[...] += dot(w, df, TN)

    @pl.when(step == pl.num_programs(0) - 1)
    def _():
        pre = pre_s[...]
        sig = 1.0 / (1.0 + jnp.exp(-pre))
        dpre = (dhid_s[...].T * sig * (1.0 + pre * (1.0 - sig))).astype(BF16)
        m1 = jnp.zeros((count, n), F32)
        m2 = jnp.zeros((count, n), F32)
        for k in range(K):
            gin_s[k] = dot(norm_s[k], dpre, TN)
            dn = dot(dpre, win_ref[k].astype(BF16), NT)
            xh = xh_ref[k]
            ggain_ref[k : k + 1, :] = jnp.sum(dn * xh, axis=0, keepdims=True)
            e = dn * gain_ref[k : k + 1, :]
            e_s[k] = e
            m1 = m1 + e
            m2 = m2 + e * xh
        a1 = jnp.sum(m1, axis=1, keepdims=True) * (1.0 / (K * n))
        a2 = jnp.sum(m2, axis=1, keepdims=True) * (1.0 / (K * n))
        inv = inv_ref[:, :1]
        for k in range(K):
            dfm_ref[k] = inv * (e_s[k] - a1 - xh_ref[k] * a2)
        for o in range(owners):
            v = jnp.swapaxes(gin_s[:, o * per : (o + 1) * per, :], 0, 1)
            gin_ref[o] = v.reshape(per * K, 128).astype(BF16)


def batch(core, xh, inv, gain, near, far, half, out_grad, feats=16):
    k, count, n = xh.shape
    owners = near.shape[0]
    per = n // owners * k
    total = owners * (2 * half - per)
    rows = feats * D
    some = rows * owners // total
    whole = lambda shape: pl.BlockSpec(shape, lambda i: (0,) * len(shape))
    return pl.pallas_call(
        batch_kernel,
        grid=(total // rows,),
        in_specs=[
            pl.BlockSpec(memory_space=pltpu.SMEM),
            whole((k, count, n)),
            whole((count, 128)),
            whole((k, n)),
            pl.BlockSpec((owners, per, 128), lambda i: (0, 0, 0)),
            pl.BlockSpec((owners, per, 128), lambda i: (0, 0, 0)),
            pl.BlockSpec((some, half, 128), lambda i: (i, 0, 0)),
            pl.BlockSpec((some, half, 128), lambda i: (i, 0, 0)),
            pl.BlockSpec((count, rows), lambda i: (0, i)),
        ],
        out_specs=[
            pl.BlockSpec((rows, 128), lambda i: (i, 0)),
            whole((owners, per, 128)),
            whole((k, n)),
            whole((k, count, n)),
        ],
        out_shape=[
            jax.ShapeDtypeStruct((total, 128), BF16),
            jax.ShapeDtypeStruct((owners, per, 128), BF16),
            jax.ShapeDtypeStruct((k, n), F32),
            jax.ShapeDtypeStruct((k, count, n), F32),
        ],
        scratch_shapes=[
            pltpu.VMEM((count, 128), F32),
            pltpu.VMEM((count, 128), BF16),
            pltpu.VMEM((128, count), F32),
            pltpu.VMEM((k, count, n), BF16),
            pltpu.VMEM((k, count, n), F32),
            pltpu.VMEM((k, n, 128), F32),
            pltpu.VMEM((k, n, 128), F32),
        ],
        compiler_params=params(),
        cost_estimate=cost(2e10, 2e7),
        name="batch",
    )(core, xh, inv, gain, near, far, near, far, out_grad)


def last_kernel(
    at_ref, x_ref, s_ref, dl_ref, dfm_ref, wt_ref, keep_ref, send_ref, acc_ref, flo, fhi, dx, both
):
    rows, n = x_ref.shape[0], x_ref.shape[1]

    @pl.when(pl.program_id(0) == 0)
    def _():
        acc_ref[...] = jnp.zeros_like(acc_ref)

    flo[...] = dfm_ref[:, :, :128].reshape(K * rows, 128)
    fhi[...] = dfm_ref[:, :, 128:].reshape(K * rows, 128)
    proj = wt_ref[:K, :]
    shared = wt_ref[...]

    def sample(b, _):
        dfm = jnp.concatenate(
            [flo[pl.ds(b, K, stride=rows), :], fhi[pl.ds(b, K, stride=rows), :]], axis=1
        ).astype(BF16)
        xb = x_ref[b]
        dhi, dlo = split(dot(dfm, xb))
        dl = dl_ref[b]
        low = jnp.concatenate([dhi, dlo, dl], axis=0)
        acc_ref[...] += dot(low, xb, NT)
        left = jnp.concatenate([dfm, dfm, proj, shared], axis=0)
        right = jnp.concatenate([s_ref[b], dlo, dhi, dl], axis=0)
        dx[b] = dot(left, right, TN)
        return 0

    lax.fori_loop(0, rows, sample, 0, unroll=8)

    def turn(j, _):
        at = pl.ds(pl.multiple_of(j * 16, 16), 16)
        lo = jnp.swapaxes(dx[:, at, :128], 0, 1).astype(BF16)
        hi = jnp.swapaxes(dx[:16, at, 128:] + dx[16:, at, 128:], 0, 1).astype(BF16)
        for i in range(16):
            p = at_ref[j * 16 + i]
            both[p, :rows, :] = lo[i]
            both[p, rows:, :] = hi[i]
        return 0

    lax.fori_loop(0, n // 16, turn, 0)
    keep_ref[:, 0] = both[: n // 2]
    send_ref[:, 0] = both[n // 2 :]


def last(at, x3, s, dl, dfm, wt, rows=32):
    count, n, _ = x3.shape
    nl = dl.shape[1]
    out = pl.BlockSpec((n // 2, 1, rows + rows // 2, 128), lambda i, o: (0, i, 0, 0))
    grid = pltpu.PrefetchScalarGridSpec(
        num_scalar_prefetch=1,
        grid=(count // rows,),
        in_specs=[
            pl.BlockSpec((rows, n, DP), lambda i, o: (i, 0, 0)),
            pl.BlockSpec((rows, 2 * K, DP), lambda i, o: (i, 0, 0)),
            pl.BlockSpec((rows, nl, DP), lambda i, o: (i, 0, 0)),
            pl.BlockSpec((K, rows, n), lambda i, o: (0, i, 0)),
            pl.BlockSpec(wt.shape, lambda i, o: (0, 0)),
        ],
        out_specs=[out, out, pl.BlockSpec((2 * K + nl, n), lambda i, o: (0, 0))],
        scratch_shapes=[pltpu.VMEM((K * rows, 128), F32)] * 2
        + [pltpu.VMEM((rows, n, DP), F32), pltpu.VMEM((n, rows + rows // 2, 128), BF16)],
    )
    half = jax.ShapeDtypeStruct((n // 2, count // rows, rows + rows // 2, 128), BF16)
    return pl.pallas_call(
        last_kernel,
        grid_spec=grid,
        out_shape=[half, half, jax.ShapeDtypeStruct((2 * K + nl, n), F32)],
        compiler_params=params(),
        cost_estimate=cost(2e10, count * n * DP * 4),
        name="last",
    )(at, x3, s, dl, dfm, wt)


def sums_kernel(at_ref, mine_ref, other_ref, ids_ref, oid_ref, a_ref, b_ref, c_ref):
    nx = b_ref.shape[0]
    ny = c_ref.shape[0]
    _, steps, height, _ = mine_ref.shape
    part = height // 3
    count = ids_ref.shape[2]
    rows = 2 * count
    iota = lax.broadcasted_iota(jnp.int32, (rows, count), 0).astype(F32).astype(BF16)
    one, none = jnp.ones((rows, count), BF16), jnp.zeros((rows, count), BF16)
    low = lax.broadcasted_iota(jnp.int32, (1, 128), 1) < 64
    zero = jnp.zeros((part, 128), BF16)

    def column(x, _):
        ahead = lax.rem(x + nx - at_ref[1], nx)
        for y in range(ny):
            pair = x * ny + y
            for t in range(2):
                hot = [
                    jnp.where(iota == r[pair, t : t + 1, :].astype(F32).astype(BF16), one, none)
                    for r in (ids_ref, oid_ref)
                ]
                main, rest = [], []
                for r in (mine_ref, other_ref):
                    for s in range(steps):
                        tail = r[2 * pair + t, s, 2 * part :, :]
                        main.append(r[2 * pair + t, s, : 2 * part, :])
                        rest += [jnp.where(low, tail, zero), jnp.where(low, zero, tail)]
                block = jnp.concatenate(
                    [jnp.concatenate(main, axis=0), jnp.concatenate(rest, axis=0)], axis=1
                )
                out = dot(jnp.concatenate(hot, axis=1), block)
                tail = out[:, 128:] + pltpu.roll(out[:, 128:], 64, 1)
                main = out[:, :128].astype(BF16)
                tail = jnp.where(low, tail[:count], tail[count:]).astype(BF16)
                if t == 0:
                    a_ref[0, ahead, y, :256, :] = main
                    a_ref[0, ahead, y, 256:, :] = tail[:32]
                    b_ref[ahead, 0, y, :96, :] = tail[32:]
                else:
                    b_ref[ahead, 0, y, 96:, :] = main[:160]
                    c_ref[y, 0, x, :96, :] = main[160:]
                    c_ref[y, 0, x, 96:, :] = tail
        return 0

    lax.fori_loop(0, nx, column, 0)


def sums(at, mine, other, ids, oids, nz=4, nx=4):
    tables, steps, height, _ = mine.shape
    count = ids.shape[2]
    ny = tables // (2 * nz * nx)
    data = pl.BlockSpec((2 * nx * ny, steps, height, 128), lambda z, at: (z, 0, 0, 0))
    index = pl.BlockSpec((nx * ny, 2, count), lambda z, at: (z, 0, 0))
    grid = pltpu.PrefetchScalarGridSpec(
        num_scalar_prefetch=1,
        grid=(nz,),
        in_specs=[data, data, index, index],
        out_specs=[
            pl.BlockSpec(
                (1, nx, ny, 288, 128), lambda z, at: (lax.rem(z + nz - at[0], nz), 0, 0, 0, 0)
            ),
            pl.BlockSpec(
                (nx, 1, ny, 256, 128), lambda z, at: (0, lax.rem(z + nz - at[0], nz), 0, 0, 0)
            ),
            pl.BlockSpec((ny, 1, nx, 224, 128), lambda z, at: (0, z, 0, 0, 0)),
        ],
    )
    return pl.pallas_call(
        sums_kernel,
        grid_spec=grid,
        out_shape=[
            jax.ShapeDtypeStruct((nz, nx, ny, 288, 128), BF16),
            jax.ShapeDtypeStruct((nx, nz, ny, 256, 128), BF16),
            jax.ShapeDtypeStruct((ny, nz, nx, 224, 128), BF16),
        ],
        compiler_params=params(),
        cost_estimate=cost(1e10, mine.size * 8),
        name="sums",
    )(at, mine, other, ids, oids)


def update_kernel(slot_ref, sum_ref, rows_ref, accum_ref, new_rows_ref, new_accum_ref, acc):
    cores, runs, height, _ = sum_ref.shape
    tables = 2 * cores * runs
    state = rows_ref.shape[1]
    rows = state // tables
    half = rows // 2
    for t in range(tables):
        where = t // 2 // runs, t // 2 % runs
        base = (t % 2) * (height - 384)
        first = slice(t * rows, t * rows + half)
        second = slice(t * rows + half, (t + 1) * rows)
        main = sum_ref[where + (slice(base, base + rows),)].astype(F32).T.astype(BF16)
        tail = sum_ref[where + (slice(base + rows, base + 384),)].astype(F32).T.astype(BF16)
        acc[:128, t * rows : (t + 1) * rows] = main
        acc[128:, first] = tail[:64]
        acc[128:, second] = tail[64:]
    size = 256
    iota = lax.broadcasted_iota(jnp.int32, (size, state), 0)
    slots = slot_ref[...]
    for i in range(state // size):
        at = slice(i * size, (i + 1) * size)
        hot = jnp.where(iota == slots - i * size, 1.0, 0.0).astype(BF16)
        total = dot(acc[...], hot, NT)
        accum = accum_ref[:, at] + jnp.sum(total * total, axis=0, keepdims=True) * (1.0 / D)
        new_accum_ref[:, at] = accum
        new_rows_ref[:, at] = rows_ref[:, at] - LEARN * total / jnp.sqrt(accum)


def update(slots, sums, table_rows, row_accum):
    state = slots.shape[1]
    return pl.pallas_call(
        update_kernel,
        out_shape=[
            jax.ShapeDtypeStruct((D, state), F32),
            jax.ShapeDtypeStruct((1, state), F32),
        ],
        scratch_shapes=[pltpu.VMEM((D, state), BF16)],
        compiler_params=params(),
        cost_estimate=cost(4e9, state * D * 12),
        name="update",
    )(slots, sums, table_rows, row_accum)


def forward(x3, g2, proj, w_lcb):
    wt = jnp.concatenate([proj.T, w_lcb.T], axis=0)
    return (wt,) + tuple(first(x3, g2, wt))


SWAP = [(0, 1), (1, 0)]
WIDE = ("z", "x", "yl")


def gather(a):
    n = 32
    return lax.all_to_all(jnp.broadcast_to(a[None], (n,) + a.shape), WIDE, 0, 0, tiled=True)


def ring_step(axis, by, v):
    n = 4
    return lax.ppermute(v, axis, [(i, (i + by) % n) for i in range(n)])


def add(*terms):
    total = terms[0].astype(F32)
    for term in terms[1:]:
        total = total + term.astype(F32)
    return total.astype(BF16)


def ring_sums(parts):
    fore = [ring_step(axis, 1, v[2, :2]) for axis, v in parts]
    back = [ring_step(axis, -1, v[2, 2:]) for axis, v in parts]
    fore = [
        ring_step(axis, 1, add(v[1], jnp.pad(f, ((0, 2),) + ((0, 0),) * (f.ndim - 1))))
        for (axis, v), f in zip(parts, fore)
    ]
    back = [
        ring_step(axis, -1, add(v[3], jnp.pad(b, ((2, 0),) + ((0, 0),) * (b.ndim - 1))))
        for (axis, v), b in zip(parts, back)
    ]
    return [add(v[0], f, b) for (_, v), f, b in zip(parts, fore, back)]


def body(
    samples, out_grad, row_ids, table_owner, slot_map, proj, gain_flat, w_in, w_out, w_lcb,
    table_rows, row_accum,
):
    owners = 32
    count = samples.shape[0]
    per = proj.shape[0]
    n = per * owners
    nl = w_lcb.shape[1]
    core = lax.axis_index("c")
    small = jnp.concatenate([proj, gain_flat.reshape(per, K), w_lcb], axis=1)
    small = jnp.pad(small, ((0, 8), (0, 128 - small.shape[1])))
    shard = jnp.concatenate([w_in, w_out], axis=0)
    rows = shard.shape[0] // 2
    near = jnp.concatenate([lax.dynamic_slice_in_dim(shard, core * rows, rows, 0), small], axis=0)
    x3 = unfold(samples, n, 0)
    g2 = unfold(out_grad, nl, out_grad.shape[1] // D // nl - 1)
    near, x3, g2 = lax.optimization_barrier((gather(near), x3, g2))
    small = near[:, rows : rows + per].reshape(n, 128)
    proj_f = small[:, :K]
    gain_t = small[:, K : 2 * K].T.astype(F32)
    w_lcb_f = small[:, 2 * K : 2 * K + nl]
    far = lax.ppermute(near, "c", SWAP)

    quad = per // 2
    spot = table_owner // per * quad + table_owner % quad
    spot = jnp.where((table_owner % per) // quad == core, spot, spot + n // 2)
    order = jnp.zeros((n,), jnp.int32).at[spot].set(jnp.arange(n, dtype=jnp.int32))
    ids = jnp.take(row_ids.T, order, axis=0).reshape(2, n // 4, 2, count)
    other_ids = lax.ppermute(ids[1], "c", SWAP)

    wt, score, dl, xh, inv = forward(x3, g2, proj_f, w_lcb_f)
    g_out, g_in, g_gain, dfm = batch(
        core.reshape(1), xh, inv, gain_t, near, far, rows, out_grad
    )
    w_grads = jnp.concatenate(
        [
            g_out.reshape(owners, -1, 128),
            g_in,
        ],
        axis=1,
    )
    top, bottom = w_grads[:, :rows], w_grads[:, rows:]
    theirs = lax.ppermute(jnp.where(core == 0, bottom, top), "c", SWAP)
    w_grads = add(jnp.where(core == 0, top, bottom), theirs)
    w_grads, dfm = lax.optimization_barrier((w_grads, dfm))
    w_grads = lax.all_to_all(w_grads, WIDE, 0, 0, tiled=True)
    keep, send, acc = last(spot, x3, score, dl, dfm, wt)
    w_grads, send = lax.optimization_barrier((w_grads, send))
    g_proj, g_lcb = acc[:K] + acc[K : 2 * K], acc[2 * K :]
    little = jnp.concatenate([g_proj, g_gain, g_lcb], axis=0).T.reshape(owners, per, -1)
    little = jnp.pad(little, ((0, 0), (0, 0), (0, 128 - little.shape[2])))
    little = lax.all_to_all(little, WIDE, 0, 0, tiled=True)

    other = lax.ppermute(send, "c", SWAP)
    at = jnp.stack([lax.axis_index("z"), lax.axis_index("x")]).astype(jnp.int32)
    a, b, c = sums(at, keep, other, ids[0], other_ids)
    a, b, c, little = lax.optimization_barrier((a, b, c, little))
    c = lax.all_to_all(c, ("yl", "yh"), 0, 0, tiled=True)
    a, b = ring_sums([("z", a), ("x", b)])
    c = jnp.sum(c.astype(F32), axis=0).astype(BF16)
    mixed = jnp.concatenate([jnp.sum(w_grads.astype(F32), axis=0), jnp.sum(little, axis=0)], axis=0)
    a, b, c, mixed = lax.optimization_barrier((a, b, c, mixed))
    c = lax.all_to_all(c.reshape((16,) + c.shape[2:]), ("z", "x"), 0, 0, tiled=True)
    a, b = ring_sums([("x", a), ("z", b)])
    c = jnp.sum(c.astype(F32), axis=0).astype(BF16)
    mixed = mixed + lax.ppermute(mixed, "yh", SWAP)
    swapped = lax.ppermute(mixed, "c", SWAP)
    little = (mixed[rows:] + swapped[rows:])[:, : 2 * K + nl]
    low, high = jnp.where(core == 0, mixed, swapped), jnp.where(core == 0, swapped, mixed)
    big = jnp.concatenate([low[:rows], high[:rows]], axis=0)
    a, b, c, big, little = lax.optimization_barrier((a, b, c, big, little))
    ab = jnp.concatenate([a, b], axis=1)
    ab = ab.reshape((2, 1, 2) + ab.shape[1:])
    here = (jnp.arange(2)[:, None] == lax.axis_index("yl")) & (
        jnp.arange(2)[None, :] == lax.axis_index("yh")
    )
    c = jnp.where(here.reshape(2, 1, 2, 1, 1), c, jnp.zeros_like(c))
    both = jnp.concatenate(
        [jnp.broadcast_to(v, (2, 2, 2) + v.shape[3:]) for v in (ab, c)], axis=3
    )
    both = both.reshape((4, 2) + both.shape[3:])
    both = lax.all_to_all(both, ("yl", "yh"), 0, 0, tiled=True)
    mine = jnp.sum(both.astype(F32), axis=0).astype(BF16)
    others = lax.ppermute(mine, "c", SWAP)
    owned = jnp.where(core == 0, jnp.stack([mine, others]), jnp.stack([others, mine]))
    new_rows, new_accum = update(
        slot_map.reshape(1, -1), owned, table_rows.T, row_accum.reshape(1, -1)
    )
    split_at = w_out.shape[0]
    return (
        little[:, :K],
        little[:, K : 2 * K].reshape(-1),
        big[split_at:],
        big[:split_at],
        little[:, 2 * K :],
        new_rows.T,
        new_accum.reshape(-1),
    )


def solution(mesh):
    cube = Mesh(mesh.devices.reshape(4, 4, 2, 2, 2), ("z", "x", "yl", "yh", "c"))
    batch_spec = P(("z", "x", "yl", "yh", "c"), None)
    two, one = P(WIDE, None), P(WIDE)
    in_specs = (batch_spec,) * 3 + (P(), two, two, one, two, two, two, two, one)
    out_specs = (two, one, two, two, two, two, one)
    return jax.shard_map(body, mesh=cube, in_specs=in_specs, out_specs=out_specs, check_vma=False)
```

```python
import functools

import jax
import jax.numpy as jnp
from jax import lax
from jax.experimental import pallas as pl
from jax.experimental.pallas import tpu as pltpu
from jax.sharding import Mesh, PartitionSpec as P

LEARN = 0.1
EPS = 1e-05
F32 = jnp.float32
BF16 = jnp.bfloat16
D = 192
DP = 256
K = 16
NN = (((1,), (0,)), ((), ()))
NT = (((1,), (1,)), ((), ()))
TN = (((0,), (0,)), ((), ()))


def dot(a, b, dims=NN):
    return lax.dot_general(a, b, dims, preferred_element_type=F32)


def params(mib=56):
    return pltpu.CompilerParams(vmem_limit_bytes=mib * 1024 * 1024)


def cost(flops, nbytes):
    return pl.CostEstimate(flops=int(flops), bytes_accessed=int(nbytes), transcendentals=0)


def split(v):
    hi = v.astype(BF16)
    return hi, (v - hi.astype(F32)).astype(BF16)


def unfold_kernel(x_ref, o_ref):
    tables = o_ref.shape[1]
    low = lax.broadcasted_iota(jnp.int32, (1, 1, 128), 2) < 64

    def group(j, _):
        at = pl.ds(pl.multiple_of(j * 16, 16), 16)
        for h in range(2):
            lo, hi = [], []
            part = slice(16 * h, 16 * h + 16)
            for p in range(8):
                v = x_ref[part, pl.ds(pl.multiple_of(j * 3072 + 384 * p, 128), 384)].astype(F32)
                w = pltpu.roll(v, 192, 1)
                lo += [v[:, :128], w[:, :128]]
                if h == 0:
                    hi += [v[:, 128:256], w[:, 128:256]]
                else:
                    hi += [pltpu.roll(v[:, 128:256], 64, 1), v[:, 256:]]
            hi = jnp.swapaxes(jnp.stack(hi), 0, 1)
            hi = jnp.where(low, hi, 0.0) if h == 0 else jnp.where(low, 0.0, hi)
            o_ref[part, at, :128] = jnp.swapaxes(jnp.stack(lo), 0, 1).astype(BF16)
            o_ref[part, at, 128:] = hi.astype(BF16)
        return 0

    lax.fori_loop(0, tables // 16, group, 0)


def unfold(x, tables, first, rows=32):
    count = x.shape[0]
    return pl.pallas_call(
        unfold_kernel,
        grid=(count // rows,),
        in_specs=[pl.BlockSpec((rows, tables * D), lambda i: (i, first))],
        out_specs=pl.BlockSpec((rows, tables, DP), lambda i: (i, 0, 0)),
        out_shape=jax.ShapeDtypeStruct((count, tables, DP), BF16),
        compiler_params=params(),
        cost_estimate=cost(1e9, count * tables * 900),
        name="unfold",
    )(x)


def first_kernel(x_ref, g_ref, w_ref, s_ref, dl_ref, xh_ref, inv_ref, lo, hi):
    rows = x_ref.shape[0]
    n = x_ref.shape[1]
    w = w_ref[...]
    lane = lax.broadcasted_iota(jnp.int32, (1, DP), 1)
    half = (pl.program_id(0) * rows // 16) % 2
    keep = (lane < 128) | ((lane >= 128 + 64 * half) & (lane < 192 + 64 * half))
    total = lambda v: jnp.sum(jnp.sum(v, axis=0, keepdims=True), axis=1, keepdims=True)
    for b in range(rows):
        xb = x_ref[b]
        r = dot(w, xb)
        shi, slo = split(r[:K])
        s_ref[b, :K, :] = shi
        s_ref[b, K:, :] = slo
        f2 = dot(jnp.concatenate([shi, slo], axis=0), xb, NT)
        fm = f2[:K] + f2[K:]
        c = fm - total(fm) * (1.0 / (K * n))
        inv = 1.0 / jnp.sqrt(total(c * c) * (1.0 / (K * n)) + EPS)
        inv_ref[b : b + 1, :] = jnp.broadcast_to(inv, (1, 128))
        xh = c * inv
        lo[pl.ds(b, K, stride=rows), :] = xh[:, :128]
        hi[pl.ds(b, K, stride=rows), :] = xh[:, 128:]
        lout = r[K:]
        grad = g_ref[b].astype(F32)
        mid = jnp.where(keep, lout - jnp.sum(lout, axis=1, keepdims=True) * (1.0 / D), 0.0)
        oinv = 1.0 / jnp.sqrt(jnp.sum(mid * mid, axis=1, keepdims=True) * (1.0 / D) + EPS)
        chat = mid * oinv
        gm = jnp.sum(grad, axis=1, keepdims=True) * (1.0 / D)
        gc = jnp.sum(grad * chat, axis=1, keepdims=True) * (1.0 / D)
        dl_ref[b] = jnp.where(keep, oinv * (grad - gm - chat * gc), 0.0).astype(BF16)
    xh_ref[:, :, :128] = lo[...].reshape(K, rows, 128)
    xh_ref[:, :, 128:] = hi[...].reshape(K, rows, 128)


def first(x3, g2, wt, rows=16):
    count, n, _ = x3.shape
    nl = g2.shape[1]
    return pl.pallas_call(
        first_kernel,
        grid=(count // rows,),
        in_specs=[
            pl.BlockSpec((rows, n, DP), lambda i: (i, 0, 0)),
            pl.BlockSpec((rows, nl, DP), lambda i: (i, 0, 0)),
            pl.BlockSpec(wt.shape, lambda i: (0, 0)),
        ],
        out_specs=[
            pl.BlockSpec((rows, 2 * K, DP), lambda i: (i, 0, 0)),
            pl.BlockSpec((rows, nl, DP), lambda i: (i, 0, 0)),
            pl.BlockSpec((K, rows, n), lambda i: (0, i, 0)),
            pl.BlockSpec((rows, 128), lambda i: (i, 0)),
        ],
        out_shape=[
            jax.ShapeDtypeStruct((count, 2 * K, DP), BF16),
            jax.ShapeDtypeStruct((count, nl, DP), BF16),
            jax.ShapeDtypeStruct((K, count, n), F32),
            jax.ShapeDtypeStruct((count, 128), F32),
        ],
        scratch_shapes=[pltpu.VMEM((K * rows, 128), F32)] * 2,
        compiler_params=params(),
        cost_estimate=cost(2e10, count * n * DP * 2),
        name="first",
    )(x3, g2, wt)


def batch_kernel(
    core_ref, xh_ref, inv_ref, gain_ref, nraw_ref, fraw_ref, near_ref, far_ref, g_ref,
    gout_ref, gin_ref, ggain_ref, dfm_ref, pre_s, hid_s, dhid_s, norm_s, e_s, win_ref, gin_s,
):
    step = pl.program_id(0)
    count, n = xh_ref.shape[1], xh_ref.shape[2]
    owners = nraw_ref.shape[0]
    per = n // owners
    first_core = core_ref[0] == 0

    @pl.when(step == 0)
    def _():
        for o in range(owners):
            v = jnp.where(first_core, nraw_ref[o], fraw_ref[o]).astype(F32)
            v = jnp.swapaxes(v.reshape(per, K, 128), 0, 1)
            win_ref[:, o * per : (o + 1) * per, :] = v
        pre = jnp.zeros((count, 128), F32)
        for k in range(K):
            normed = (xh_ref[k] * gain_ref[k : k + 1, :]).astype(BF16)
            norm_s[k] = normed
            pre = pre + dot(normed, win_ref[k].astype(BF16))
        pre_s[...] = pre
        hid_s[...] = (pre / (1.0 + jnp.exp(-pre))).astype(BF16)
        dhid_s[...] = jnp.zeros_like(dhid_s)

    hid = hid_s[...]
    near, far = near_ref[...], far_ref[...]
    lower = jnp.where(first_core, near[:, per * K :], far[:, per * K :])
    w = jnp.concatenate([lower, jnp.where(first_core, far, near)], axis=1).reshape(-1, 128)
    rows = w.shape[0]
    fout = dot(w, hid, NT).reshape(rows // D, D, count)
    grad = g_ref[...].astype(F32).T.reshape(rows // D, D, count)
    mid = fout - jnp.sum(fout, axis=1, keepdims=True) * (1.0 / D)
    oinv = 1.0 / jnp.sqrt(jnp.sum(mid * mid, axis=1, keepdims=True) * (1.0 / D) + EPS)
    chat = mid * oinv
    gm = jnp.sum(grad, axis=1, keepdims=True) * (1.0 / D)
    gc = jnp.sum(grad * chat, axis=1, keepdims=True) * (1.0 / D)
    df = (oinv * (grad - gm - chat * gc)).reshape(rows, count).astype(BF16)
    gout_ref[...] = dot(df, hid).astype(BF16)
    dhid_s[...] += dot(w, df, TN)

    @pl.when(step == pl.num_programs(0) - 1)
    def _():
        pre = pre_s[...]
        sig = 1.0 / (1.0 + jnp.exp(-pre))
        dpre = (dhid_s[...].T * sig * (1.0 + pre * (1.0 - sig))).astype(BF16)
        m1 = jnp.zeros((count, n), F32)
        m2 = jnp.zeros((count, n), F32)
        for k in range(K):
            gin_s[k] = dot(norm_s[k], dpre, TN)
            dn = dot(dpre, win_ref[k].astype(BF16), NT)
            xh = xh_ref[k]
            ggain_ref[k : k + 1, :] = jnp.sum(dn * xh, axis=0, keepdims=True)
            e = dn * gain_ref[k : k + 1, :]
            e_s[k] = e
            m1 = m1 + e
            m2 = m2 + e * xh
        a1 = jnp.sum(m1, axis=1, keepdims=True) * (1.0 / (K * n))
        a2 = jnp.sum(m2, axis=1, keepdims=True) * (1.0 / (K * n))
        inv = inv_ref[:, :1]
        for k in range(K):
            dfm_ref[k] = inv * (e_s[k] - a1 - xh_ref[k] * a2)
        for o in range(owners):
            v = jnp.swapaxes(gin_s[:, o * per : (o + 1) * per, :], 0, 1)
            gin_ref[o] = v.reshape(per * K, 128).astype(BF16)


def batch(core, xh, inv, gain, near, far, half, out_grad, feats=16):
    k, count, n = xh.shape
    owners = near.shape[0]
    per = n // owners * k
    total = owners * (2 * half - per)
    rows = feats * D
    some = rows * owners // total
    whole = lambda shape: pl.BlockSpec(shape, lambda i: (0,) * len(shape))
    return pl.pallas_call(
        batch_kernel,
        grid=(total // rows,),
        in_specs=[
            pl.BlockSpec(memory_space=pltpu.SMEM),
            whole((k, count, n)),
            whole((count, 128)),
            whole((k, n)),
            pl.BlockSpec((owners, per, 128), lambda i: (0, 0, 0)),
            pl.BlockSpec((owners, per, 128), lambda i: (0, 0, 0)),
            pl.BlockSpec((some, half, 128), lambda i: (i, 0, 0)),
            pl.BlockSpec((some, half, 128), lambda i: (i, 0, 0)),
            pl.BlockSpec((count, rows), lambda i: (0, i)),
        ],
        out_specs=[
            pl.BlockSpec((rows, 128), lambda i: (i, 0)),
            whole((owners, per, 128)),
            whole((k, n)),
            whole((k, count, n)),
        ],
        out_shape=[
            jax.ShapeDtypeStruct((total, 128), BF16),
            jax.ShapeDtypeStruct((owners, per, 128), BF16),
            jax.ShapeDtypeStruct((k, n), F32),
            jax.ShapeDtypeStruct((k, count, n), F32),
        ],
        scratch_shapes=[
            pltpu.VMEM((count, 128), F32),
            pltpu.VMEM((count, 128), BF16),
            pltpu.VMEM((128, count), F32),
            pltpu.VMEM((k, count, n), BF16),
            pltpu.VMEM((k, count, n), F32),
            pltpu.VMEM((k, n, 128), F32),
            pltpu.VMEM((k, n, 128), F32),
        ],
        compiler_params=params(),
        cost_estimate=cost(2e10, 2e7),
        name="batch",
    )(core, xh, inv, gain, near, far, near, far, out_grad)


def last_kernel(
    at_ref, x_ref, s_ref, dl_ref, dfm_ref, wt_ref, keep_ref, send_ref, acc_ref, flo, fhi, dx, both
):
    rows, n = x_ref.shape[0], x_ref.shape[1]

    @pl.when(pl.program_id(0) == 0)
    def _():
        acc_ref[...] = jnp.zeros_like(acc_ref)

    flo[...] = dfm_ref[:, :, :128].reshape(K * rows, 128)
    fhi[...] = dfm_ref[:, :, 128:].reshape(K * rows, 128)
    proj = wt_ref[:K, :]
    shared = wt_ref[...]

    def sample(b, _):
        dfm = jnp.concatenate(
            [flo[pl.ds(b, K, stride=rows), :], fhi[pl.ds(b, K, stride=rows), :]], axis=1
        ).astype(BF16)
        xb = x_ref[b]
        dhi, dlo = split(dot(dfm, xb))
        dl = dl_ref[b]
        low = jnp.concatenate([dhi, dlo, dl], axis=0)
        acc_ref[...] += dot(low, xb, NT)
        left = jnp.concatenate([dfm, dfm, proj, shared], axis=0)
        right = jnp.concatenate([s_ref[b], dlo, dhi, dl], axis=0)
        dx[b] = dot(left, right, TN)
        return 0

    lax.fori_loop(0, rows, sample, 0, unroll=8)

    def turn(j, _):
        at = pl.ds(pl.multiple_of(j * 16, 16), 16)
        lo = jnp.swapaxes(dx[:, at, :128], 0, 1).astype(BF16)
        hi = jnp.swapaxes(dx[:16, at, 128:] + dx[16:, at, 128:], 0, 1).astype(BF16)
        for i in range(16):
            p = at_ref[j * 16 + i]
            both[p, :rows, :] = lo[i]
            both[p, rows:, :] = hi[i]
        return 0

    lax.fori_loop(0, n // 16, turn, 0)
    keep_ref[:, 0] = both[: n // 2]
    send_ref[:, 0] = both[n // 2 :]


def last(at, x3, s, dl, dfm, wt, rows=32):
    count, n, _ = x3.shape
    nl = dl.shape[1]
    out = pl.BlockSpec((n // 2, 1, rows + rows // 2, 128), lambda i, o: (0, i, 0, 0))
    grid = pltpu.PrefetchScalarGridSpec(
        num_scalar_prefetch=1,
        grid=(count // rows,),
        in_specs=[
            pl.BlockSpec((rows, n, DP), lambda i, o: (i, 0, 0)),
            pl.BlockSpec((rows, 2 * K, DP), lambda i, o: (i, 0, 0)),
            pl.BlockSpec((rows, nl, DP), lambda i, o: (i, 0, 0)),
            pl.BlockSpec((K, rows, n), lambda i, o: (0, i, 0)),
            pl.BlockSpec(wt.shape, lambda i, o: (0, 0)),
        ],
        out_specs=[out, out, pl.BlockSpec((2 * K + nl, n), lambda i, o: (0, 0))],
        scratch_shapes=[pltpu.VMEM((K * rows, 128), F32)] * 2
        + [pltpu.VMEM((rows, n, DP), F32), pltpu.VMEM((n, rows + rows // 2, 128), BF16)],
    )
    half = jax.ShapeDtypeStruct((n // 2, count // rows, rows + rows // 2, 128), BF16)
    return pl.pallas_call(
        last_kernel,
        grid_spec=grid,
        out_shape=[half, half, jax.ShapeDtypeStruct((2 * K + nl, n), F32)],
        compiler_params=params(),
        cost_estimate=cost(2e10, count * n * DP * 4),
        name="last",
    )(at, x3, s, dl, dfm, wt)


def sums_kernel(at_ref, mine_ref, other_ref, ids_ref, oid_ref, a_ref, b_ref, c_ref, af_ref, ab_ref, bf_ref, bb_ref):
    nx = b_ref.shape[0]
    ny = c_ref.shape[0]
    _, steps, height, _ = mine_ref.shape
    part = height // 3
    count = ids_ref.shape[2]
    rows = 2 * count
    iota = lax.broadcasted_iota(jnp.int32, (rows, count), 0).astype(F32).astype(BF16)
    one, none = jnp.ones((rows, count), BF16), jnp.zeros((rows, count), BF16)
    low = lax.broadcasted_iota(jnp.int32, (1, 128), 1) < 64
    zero = jnp.zeros((part, 128), BF16)

    def column(x, _):
        ahead = lax.rem(x + nx - at_ref[1], nx)
        for y in range(ny):
            pair = x * ny + y
            for t in range(2):
                hot = [
                    jnp.where(iota == r[pair, t : t + 1, :].astype(F32).astype(BF16), one, none)
                    for r in (ids_ref, oid_ref)
                ]
                main, rest = [], []
                for r in (mine_ref, other_ref):
                    for s in range(steps):
                        tail = r[2 * pair + t, s, 2 * part :, :]
                        main.append(r[2 * pair + t, s, : 2 * part, :])
                        rest += [jnp.where(low, tail, zero), jnp.where(low, zero, tail)]
                block = jnp.concatenate(
                    [jnp.concatenate(main, axis=0), jnp.concatenate(rest, axis=0)], axis=1
                )
                out = dot(jnp.concatenate(hot, axis=1), block)
                tail = out[:, 128:] + pltpu.roll(out[:, 128:], 64, 1)
                main = out[:, :128].astype(BF16)
                tail = jnp.where(low, tail[:count], tail[count:]).astype(BF16)
                if t == 0:
                    a_ref[0, ahead, y, :256, :] = main
                    a_ref[0, ahead, y, 256:, :] = tail[:48]
                    b_ref[ahead, 0, y, :80, :] = tail[48:]
                else:
                    b_ref[ahead, 0, y, 80:, :] = main[:192]
                    c_ref[y, 0, x, :64, :] = main[192:]
                    c_ref[y, 0, x, 64:, :] = tail
        return 0

    lax.fori_loop(0, nx, column, 0)
    nz = pl.num_programs(0)
    ahead = lax.rem(pl.program_id(0) + nz - at_ref[0], nz)

    @pl.when(ahead == 2)
    def _():
        af_ref[...] = a_ref[0, :2]
        ab_ref[...] = a_ref[0, 2:]

    @pl.when(ahead < 2)
    def _():
        bf_ref[ahead] = b_ref[2, 0]

    @pl.when(ahead >= 2)
    def _():
        bb_ref[ahead - 2] = b_ref[2, 0]


def sums(at, mine, other, ids, oids, nz=4, nx=4):
    tables, steps, height, _ = mine.shape
    count = ids.shape[2]
    ny = tables // (2 * nz * nx)
    data = pl.BlockSpec((2 * nx * ny, steps, height, 128), lambda z, at: (z, 0, 0, 0))
    index = pl.BlockSpec((nx * ny, 2, count), lambda z, at: (z, 0, 0))
    grid = pltpu.PrefetchScalarGridSpec(
        num_scalar_prefetch=1,
        grid=(nz,),
        in_specs=[data, data, index, index],
        out_specs=[
            pl.BlockSpec(
                (1, nx, ny, 304, 128), lambda z, at: (lax.rem(z + nz - at[0], nz), 0, 0, 0, 0)
            ),
            pl.BlockSpec(
                (nx, 1, ny, 272, 128), lambda z, at: (0, lax.rem(z + nz - at[0], nz), 0, 0, 0)
            ),
            pl.BlockSpec((ny, 1, nx, 192, 128), lambda z, at: (0, z, 0, 0, 0)),
        ]
        + [pl.BlockSpec((2, ny, h, 128), lambda z, at: (0, 0, 0, 0)) for h in (304, 304, 272, 272)],
    )
    return pl.pallas_call(
        sums_kernel,
        grid_spec=grid,
        out_shape=[
            jax.ShapeDtypeStruct((nz, nx, ny, 304, 128), BF16),
            jax.ShapeDtypeStruct((nx, nz, ny, 272, 128), BF16),
            jax.ShapeDtypeStruct((ny, nz, nx, 192, 128), BF16),
        ]
        + [jax.ShapeDtypeStruct((2, ny, h, 128), BF16) for h in (304, 304, 272, 272)],
        compiler_params=params(),
        cost_estimate=cost(1e10, mine.size * 8),
        name="sums",
    )(at, mine, other, ids, oids)


def update_kernel(slot_ref, sum_ref, rows_ref, accum_ref, new_rows_ref, new_accum_ref, acc):
    cores, runs, height, _ = sum_ref.shape
    tables = 2 * cores * runs
    state = rows_ref.shape[1]
    rows = state // tables
    half = rows // 2
    for t in range(tables):
        where = t // 2 // runs, t // 2 % runs
        base = (t % 2) * (height - 384)
        first = slice(t * rows, t * rows + half)
        second = slice(t * rows + half, (t + 1) * rows)
        main = sum_ref[where + (slice(base, base + rows),)].astype(F32).T.astype(BF16)
        tail = sum_ref[where + (slice(base + rows, base + 384),)].astype(F32).T.astype(BF16)
        acc[:128, t * rows : (t + 1) * rows] = main
        acc[128:, first] = tail[:64]
        acc[128:, second] = tail[64:]
    size = 256
    iota = lax.broadcasted_iota(jnp.int32, (size, state), 0)
    slots = slot_ref[...]
    for i in range(state // size):
        at = slice(i * size, (i + 1) * size)
        hot = jnp.where(iota == slots - i * size, 1.0, 0.0).astype(BF16)
        total = dot(acc[...], hot, NT)
        accum = accum_ref[:, at] + jnp.sum(total * total, axis=0, keepdims=True) * (1.0 / D)
        new_accum_ref[:, at] = accum
        new_rows_ref[:, at] = rows_ref[:, at] - LEARN * total / jnp.sqrt(accum)


def update(slots, sums, table_rows, row_accum):
    state = slots.shape[1]
    return pl.pallas_call(
        update_kernel,
        out_shape=[
            jax.ShapeDtypeStruct((D, state), F32),
            jax.ShapeDtypeStruct((1, state), F32),
        ],
        scratch_shapes=[pltpu.VMEM((D, state), BF16)],
        compiler_params=params(),
        cost_estimate=cost(4e9, state * D * 12),
        name="update",
    )(slots, sums, table_rows, row_accum)


def forward(x3, g2, proj, w_lcb):
    wt = jnp.concatenate([proj.T, w_lcb.T], axis=0)
    return (wt,) + tuple(first(x3, g2, wt))


SWAP = [(0, 1), (1, 0)]
WIDE = ("z", "x", "yl")


def gather(a):
    n = 32
    return lax.all_to_all(jnp.broadcast_to(a[None], (n,) + a.shape), WIDE, 0, 0, tiled=True)


def ring_step(axis, by, v):
    n = 4
    return lax.ppermute(v, axis, [(i, (i + by) % n) for i in range(n)])


def add(*terms):
    total = terms[0].astype(F32)
    for term in terms[1:]:
        total = total + term.astype(F32)
    return total.astype(BF16)


def ring_sums(parts, sends=None):
    if sends is None:
        sends = [(v[2, :2], v[2, 2:]) for _, v in parts]
    fore = [ring_step(axis, 1, f) for (axis, _), (f, _) in zip(parts, sends)]
    back = [ring_step(axis, -1, b) for (axis, _), (_, b) in zip(parts, sends)]
    fore = [
        ring_step(axis, 1, add(v[1], jnp.pad(f, ((0, 2),) + ((0, 0),) * (f.ndim - 1))))
        for (axis, v), f in zip(parts, fore)
    ]
    back = [
        ring_step(axis, -1, add(v[3], jnp.pad(b, ((2, 0),) + ((0, 0),) * (b.ndim - 1))))
        for (axis, v), b in zip(parts, back)
    ]
    return [add(v[0], f, b) for (_, v), f, b in zip(parts, fore, back)]


def body(
    samples, out_grad, row_ids, table_owner, slot_map, proj, gain_flat, w_in, w_out, w_lcb,
    table_rows, row_accum,
):
    owners = 32
    count = samples.shape[0]
    per = proj.shape[0]
    n = per * owners
    nl = w_lcb.shape[1]
    core = lax.axis_index("c")
    small = jnp.concatenate([proj, gain_flat.reshape(per, K), w_lcb], axis=1)
    small = jnp.pad(small, ((0, 8), (0, 128 - small.shape[1])))
    shard = jnp.concatenate([w_in, w_out], axis=0)
    rows = shard.shape[0] // 2
    near = jnp.concatenate([lax.dynamic_slice_in_dim(shard, core * rows, rows, 0), small], axis=0)
    x3 = unfold(samples, n, 0)
    g2 = unfold(out_grad, nl, out_grad.shape[1] // D // nl - 1)
    near, x3, g2 = lax.optimization_barrier((gather(near), x3, g2))
    small = near[:, rows : rows + per].reshape(n, 128)
    proj_f = small[:, :K]
    gain_t = small[:, K : 2 * K].T.astype(F32)
    w_lcb_f = small[:, 2 * K : 2 * K + nl]
    far = lax.ppermute(near, "c", SWAP)

    quad = per // 2
    spot = table_owner // per * quad + table_owner % quad
    spot = jnp.where((table_owner % per) // quad == core, spot, spot + n // 2)
    order = jnp.zeros((n,), jnp.int32).at[spot].set(jnp.arange(n, dtype=jnp.int32))
    ids = jnp.take(row_ids.T, order, axis=0).reshape(2, n // 4, 2, count)
    other_ids = lax.ppermute(ids[1], "c", SWAP)

    wt, score, dl, xh, inv = forward(x3, g2, proj_f, w_lcb_f)
    g_out, g_in, g_gain, dfm = batch(
        core.reshape(1), xh, inv, gain_t, near, far, rows, out_grad
    )
    g_out = g_out.reshape(owners, -1, 128)
    w_first, dfm = lax.optimization_barrier((g_out, dfm))
    w_first = lax.all_to_all(w_first, WIDE, 0, 0, tiled=True)
    keep, send, acc = last(spot, x3, score, dl, dfm, wt)
    w_first, send = lax.optimization_barrier((w_first, send))
    little = jnp.concatenate([acc[:K] + acc[K : 2 * K], g_gain, acc[2 * K :]], axis=0)
    little = jnp.pad(little.T, ((0, 0), (0, 128 - little.shape[0]))).reshape(owners, per, 128)
    w_second = jnp.concatenate([g_in, *split(little)], axis=1)
    w_second = lax.all_to_all(w_second, WIDE, 0, 0, tiled=True)

    other = lax.ppermute(send, "c", SWAP)
    at = jnp.stack([lax.axis_index("z"), lax.axis_index("x")]).astype(jnp.int32)
    a, b, c, af, ab, bf, bb = sums(at, keep, other, ids[0], other_ids)
    c, w_second = lax.optimization_barrier((c, w_second))
    a, b = ring_sums([("z", a), ("x", b)], [(af, ab), (bf, bb)])
    c = lax.all_to_all(c, ("yl", "yh"), 0, 0, tiled=True)
    c = jnp.sum(c.astype(F32), axis=0).astype(BF16)
    mixed = jnp.concatenate(
        [jnp.sum(v.astype(F32), axis=0) for v in (w_first, w_second)], axis=0
    )
    mixed = jnp.concatenate([mixed[: 2 * rows], mixed[2 * rows : -per] + mixed[-per:]], axis=0)
    a, b, c, mixed = lax.optimization_barrier((a, b, c, mixed))
    c = lax.all_to_all(c.reshape((16,) + c.shape[2:]), ("z", "x"), 0, 0, tiled=True)
    a, b = ring_sums([("x", a), ("z", b)])
    c = jnp.sum(c.astype(F32), axis=0).astype(BF16)
    mixed = mixed + lax.ppermute(mixed, "yh", SWAP)
    mixed = mixed + lax.ppermute(mixed, "c", SWAP)
    little, big = mixed[2 * rows :, : 2 * K + nl], mixed[: 2 * rows]
    a, b, c, big, little = lax.optimization_barrier((a, b, c, big, little))
    ab = jnp.concatenate([a, b], axis=1)
    ab = ab.reshape((2, 1, 2) + ab.shape[1:])
    here = (jnp.arange(2)[:, None] == lax.axis_index("yl")) & (
        jnp.arange(2)[None, :] == lax.axis_index("yh")
    )
    c = jnp.where(here.reshape(2, 1, 2, 1, 1), c, jnp.zeros_like(c))
    both = jnp.concatenate(
        [jnp.broadcast_to(v, (2, 2, 2) + v.shape[3:]) for v in (ab, c)], axis=3
    )
    both = both.reshape((4, 2) + both.shape[3:])
    both = lax.all_to_all(both, ("yl", "yh"), 0, 0, tiled=True)
    mine = jnp.sum(both.astype(F32), axis=0).astype(BF16)
    others = lax.ppermute(mine, "c", SWAP)
    owned = jnp.where(core == 0, jnp.stack([mine, others]), jnp.stack([others, mine]))
    new_rows, new_accum = update(
        slot_map.reshape(1, -1), owned, table_rows.T, row_accum.reshape(1, -1)
    )
    split_at = w_out.shape[0]
    return (
        little[:, :K],
        little[:, K : 2 * K].reshape(-1),
        big[split_at:],
        big[:split_at],
        little[:, 2 * K :],
        new_rows.T,
        new_accum.reshape(-1),
    )


def solution(mesh):
    cube = Mesh(mesh.devices.reshape(4, 4, 2, 2, 2), ("z", "x", "yl", "yh", "c"))
    batch_spec = P(("z", "x", "yl", "yh", "c"), None)
    two, one = P(WIDE, None), P(WIDE)
    in_specs = (batch_spec,) * 3 + (P(), two, two, one, two, two, two, two, one)
    out_specs = (two, one, two, two, two, two, one)
    return jax.shard_map(body, mesh=cube, in_specs=in_specs, out_specs=out_specs, check_vma=False)
```

```python
import functools

import jax
import jax.numpy as jnp
from jax import lax
from jax.experimental import pallas as pl
from jax.experimental.pallas import tpu as pltpu
from jax.sharding import Mesh, PartitionSpec as P

LEARN = 0.1
EPS = 1e-05
F32 = jnp.float32
BF16 = jnp.bfloat16
D = 192
DP = 256
K = 16
NN = (((1,), (0,)), ((), ()))
NT = (((1,), (1,)), ((), ()))
TN = (((0,), (0,)), ((), ()))


def dot(a, b, dims=NN):
    return lax.dot_general(a, b, dims, preferred_element_type=F32)


def params(mib=56):
    return pltpu.CompilerParams(vmem_limit_bytes=mib * 1024 * 1024)


def cost(flops, nbytes):
    return pl.CostEstimate(flops=int(flops), bytes_accessed=int(nbytes), transcendentals=0)


def split(v):
    hi = v.astype(BF16)
    return hi, (v - hi.astype(F32)).astype(BF16)


def unfold_kernel(x_ref, o_ref):
    tables = o_ref.shape[1]
    low = lax.broadcasted_iota(jnp.int32, (1, 1, 128), 2) < 64

    def group(j, _):
        at = pl.ds(pl.multiple_of(j * 16, 16), 16)
        for h in range(2):
            lo, hi = [], []
            part = slice(16 * h, 16 * h + 16)
            for p in range(8):
                v = x_ref[part, pl.ds(pl.multiple_of(j * 3072 + 384 * p, 128), 384)].astype(F32)
                w = pltpu.roll(v, 192, 1)
                lo += [v[:, :128], w[:, :128]]
                if h == 0:
                    hi += [v[:, 128:256], w[:, 128:256]]
                else:
                    hi += [pltpu.roll(v[:, 128:256], 64, 1), v[:, 256:]]
            hi = jnp.swapaxes(jnp.stack(hi), 0, 1)
            hi = jnp.where(low, hi, 0.0) if h == 0 else jnp.where(low, 0.0, hi)
            o_ref[part, at, :128] = jnp.swapaxes(jnp.stack(lo), 0, 1).astype(BF16)
            o_ref[part, at, 128:] = hi.astype(BF16)
        return 0

    lax.fori_loop(0, tables // 16, group, 0)


def unfold(x, tables, first, rows=32):
    count = x.shape[0]
    return pl.pallas_call(
        unfold_kernel,
        grid=(count // rows,),
        in_specs=[pl.BlockSpec((rows, tables * D), lambda i: (i, first))],
        out_specs=pl.BlockSpec((rows, tables, DP), lambda i: (i, 0, 0)),
        out_shape=jax.ShapeDtypeStruct((count, tables, DP), BF16),
        compiler_params=params(),
        cost_estimate=cost(1e9, count * tables * 900),
        name="unfold",
    )(x)


def first_kernel(
    x_ref, g_ref, w_ref, s_ref, dl_ref, xh_ref, inv_ref, lo, hi, lout, fm
):
    rows = x_ref.shape[0]
    n = x_ref.shape[1]
    w = w_ref[...]
    lane = lax.broadcasted_iota(jnp.int32, (1, DP), 1)
    half = (pl.program_id(0) * rows // 16) % 2
    keep = (lane < 128) | ((lane >= 128 + 64 * half) & (lane < 192 + 64 * half))
    total = lambda v: jnp.sum(jnp.sum(v, axis=1, keepdims=True), axis=2, keepdims=True)
    for b in range(rows):
        r = dot(w, x_ref[b])
        shi, slo = split(r[:K])
        s_ref[b, :K, :] = shi
        s_ref[b, K:, :] = slo
        lout[b] = r[K:]
    for b in range(rows):
        f2 = dot(s_ref[b], x_ref[b], NT)
        fm[b] = f2[:K] + f2[K:]
    v = fm[...]
    c = v - total(v) * (1.0 / (K * n))
    inv = 1.0 / jnp.sqrt(total(c * c) * (1.0 / (K * n)) + EPS)
    inv_ref[...] = jnp.broadcast_to(inv.reshape(rows, 1), (rows, 128))
    xh = c * inv
    for b in range(rows):
        lo[pl.ds(b, K, stride=rows), :] = xh[b, :, :128]
        hi[pl.ds(b, K, stride=rows), :] = xh[b, :, 128:]
    for b in range(rows):
        lb = lout[b]
        grad = g_ref[b].astype(F32)
        mid = jnp.where(keep, lb - jnp.sum(lb, axis=1, keepdims=True) * (1.0 / D), 0.0)
        oinv = 1.0 / jnp.sqrt(jnp.sum(mid * mid, axis=1, keepdims=True) * (1.0 / D) + EPS)
        chat = mid * oinv
        gm = jnp.sum(grad, axis=1, keepdims=True) * (1.0 / D)
        gc = jnp.sum(grad * chat, axis=1, keepdims=True) * (1.0 / D)
        dl_ref[b] = jnp.where(keep, oinv * (grad - gm - chat * gc), 0.0).astype(BF16)
    xh_ref[:, :, :128] = lo[...].reshape(K, rows, 128)
    xh_ref[:, :, 128:] = hi[...].reshape(K, rows, 128)


def first(x3, g2, wt, rows=16):
    count, n, _ = x3.shape
    nl = g2.shape[1]
    return pl.pallas_call(
        first_kernel,
        grid=(count // rows,),
        in_specs=[
            pl.BlockSpec((rows, n, DP), lambda i: (i, 0, 0)),
            pl.BlockSpec((rows, nl, DP), lambda i: (i, 0, 0)),
            pl.BlockSpec(wt.shape, lambda i: (0, 0)),
        ],
        out_specs=[
            pl.BlockSpec((rows, 2 * K, DP), lambda i: (i, 0, 0)),
            pl.BlockSpec((rows, nl, DP), lambda i: (i, 0, 0)),
            pl.BlockSpec((K, rows, n), lambda i: (0, i, 0)),
            pl.BlockSpec((rows, 128), lambda i: (i, 0)),
        ],
        out_shape=[
            jax.ShapeDtypeStruct((count, 2 * K, DP), BF16),
            jax.ShapeDtypeStruct((count, nl, DP), BF16),
            jax.ShapeDtypeStruct((K, count, n), F32),
            jax.ShapeDtypeStruct((count, 128), F32),
        ],
        scratch_shapes=[pltpu.VMEM((K * rows, 128), F32)] * 2
        + [pltpu.VMEM((rows, nl, DP), F32), pltpu.VMEM((rows, K, n), F32)],
        compiler_params=params(),
        cost_estimate=cost(2e10, count * n * DP * 2),
        name="first",
    )(x3, g2, wt)


def batch_kernel(
    core_ref, xh_ref, inv_ref, gain_ref, nraw_ref, fraw_ref, near_ref, far_ref, g_ref,
    keep_ref, send_ref, ggain_ref, dfm_ref, pre_s, hid_s, dhid_s, norm_s, e_s, win_ref, gin_s,
):
    step = pl.program_id(0)
    count, n = xh_ref.shape[1], xh_ref.shape[2]
    owners = nraw_ref.shape[0]
    per = n // owners
    first_core = core_ref[0] == 0

    @pl.when(step == 0)
    def _():
        for o in range(owners):
            v = jnp.where(first_core, nraw_ref[o], fraw_ref[o]).astype(F32)
            v = jnp.swapaxes(v.reshape(per, K, 128), 0, 1)
            win_ref[:, o * per : (o + 1) * per, :] = v
        pre = jnp.zeros((count, 128), F32)
        for k in range(K):
            normed = (xh_ref[k] * gain_ref[k : k + 1, :]).astype(BF16)
            norm_s[k] = normed
            pre = pre + dot(normed, win_ref[k].astype(BF16))
        pre_s[...] = pre
        hid_s[...] = (pre / (1.0 + jnp.exp(-pre))).astype(BF16)
        dhid_s[...] = jnp.zeros_like(dhid_s)

    hid = hid_s[...]
    near, far = near_ref[...], far_ref[...]
    lower = jnp.where(first_core, near[:, per * K :], far[:, per * K :])
    w = jnp.concatenate([lower, jnp.where(first_core, far, near)], axis=1).reshape(-1, 128)
    rows = w.shape[0]
    fout = dot(w, hid, NT).reshape(rows // D, D, count)
    grad = g_ref[...].astype(F32).T.reshape(rows // D, D, count)
    mid = fout - jnp.sum(fout, axis=1, keepdims=True) * (1.0 / D)
    oinv = 1.0 / jnp.sqrt(jnp.sum(mid * mid, axis=1, keepdims=True) * (1.0 / D) + EPS)
    chat = mid * oinv
    gm = jnp.sum(grad, axis=1, keepdims=True) * (1.0 / D)
    gc = jnp.sum(grad * chat, axis=1, keepdims=True) * (1.0 / D)
    df = (oinv * (grad - gm - chat * gc)).reshape(rows, count).astype(BF16)
    gout = dot(df, hid).astype(BF16).reshape(near.shape[0], -1, 128)
    at = pl.ds(pl.multiple_of(step * near.shape[0], near.shape[0]), near.shape[0])
    cut = near.shape[1]

    def store(top_ref, bottom_ref):
        top_ref[at] = gout[:, :cut]
        bottom_ref[at, : gout.shape[1] - cut] = gout[:, cut:]

    pl.when(first_core)(lambda: store(keep_ref, send_ref))
    pl.when(jnp.logical_not(first_core))(lambda: store(send_ref, keep_ref))
    dhid_s[...] += dot(w, df, TN)

    @pl.when(step == pl.num_programs(0) - 1)
    def _():
        pre = pre_s[...]
        sig = 1.0 / (1.0 + jnp.exp(-pre))
        dpre = (dhid_s[...].T * sig * (1.0 + pre * (1.0 - sig))).astype(BF16)
        m1 = jnp.zeros((count, n), F32)
        m2 = jnp.zeros((count, n), F32)
        for k in range(K):
            gin_s[k] = dot(norm_s[k], dpre, TN)
            dn = dot(dpre, win_ref[k].astype(BF16), NT)
            xh = xh_ref[k]
            ggain_ref[k : k + 1, :] = jnp.sum(dn * xh, axis=0, keepdims=True)
            e = dn * gain_ref[k : k + 1, :]
            e_s[k] = e
            m1 = m1 + e
            m2 = m2 + e * xh
        a1 = jnp.sum(m1, axis=1, keepdims=True) * (1.0 / (K * n))
        a2 = jnp.sum(m2, axis=1, keepdims=True) * (1.0 / (K * n))
        inv = inv_ref[:, :1]
        for k in range(K):
            dfm_ref[k] = inv * (e_s[k] - a1 - xh_ref[k] * a2)

        def store_in(ref):
            for o in range(owners):
                v = jnp.swapaxes(gin_s[:, o * per : (o + 1) * per, :], 0, 1)
                ref[o, -per * K :] = v.reshape(per * K, 128).astype(BF16)

        pl.when(first_core)(lambda: store_in(send_ref))
        pl.when(jnp.logical_not(first_core))(lambda: store_in(keep_ref))


def batch(core, xh, inv, gain, near, far, half, out_grad, feats=16):
    k, count, n = xh.shape
    owners = near.shape[0]
    per = n // owners * k
    total = owners * (2 * half - per)
    rows = feats * D
    some = rows * owners // total
    whole = lambda shape: pl.BlockSpec(shape, lambda i: (0,) * len(shape))
    return pl.pallas_call(
        batch_kernel,
        grid=(total // rows,),
        in_specs=[
            pl.BlockSpec(memory_space=pltpu.SMEM),
            whole((k, count, n)),
            whole((count, 128)),
            whole((k, n)),
            pl.BlockSpec((owners, per, 128), lambda i: (0, 0, 0)),
            pl.BlockSpec((owners, per, 128), lambda i: (0, 0, 0)),
            pl.BlockSpec((some, half, 128), lambda i: (i, 0, 0)),
            pl.BlockSpec((some, half, 128), lambda i: (i, 0, 0)),
            pl.BlockSpec((count, rows), lambda i: (0, i)),
        ],
        out_specs=[
            whole((owners, half, 128)),
            whole((owners, half, 128)),
            whole((k, n)),
            whole((k, count, n)),
        ],
        out_shape=[
            jax.ShapeDtypeStruct((owners, half, 128), BF16),
            jax.ShapeDtypeStruct((owners, half, 128), BF16),
            jax.ShapeDtypeStruct((k, n), F32),
            jax.ShapeDtypeStruct((k, count, n), F32),
        ],
        scratch_shapes=[
            pltpu.VMEM((count, 128), F32),
            pltpu.VMEM((count, 128), BF16),
            pltpu.VMEM((128, count), F32),
            pltpu.VMEM((k, count, n), BF16),
            pltpu.VMEM((k, count, n), F32),
            pltpu.VMEM((k, n, 128), F32),
            pltpu.VMEM((k, n, 128), F32),
        ],
        compiler_params=params(),
        cost_estimate=cost(2e10, 2e7),
        name="batch",
    )(core, xh, inv, gain, near, far, near, far, out_grad)


def last_kernel(
    at_ref, x_ref, s_ref, dl_ref, dfm_ref, wt_ref, keep_ref, send_ref, acc_ref, flo, fhi, dx, both, left, low
):
    rows, n = x_ref.shape[0], x_ref.shape[1]

    @pl.when(pl.program_id(0) == 0)
    def _():
        acc_ref[...] = jnp.zeros_like(acc_ref)

    flo[...] = dfm_ref[:, :, :128].reshape(K * rows, 128)
    fhi[...] = dfm_ref[:, :, 128:].reshape(K * rows, 128)
    proj = wt_ref[:K, :]
    shared = wt_ref[...]

    def score_grad(b, _):
        dfm = jnp.concatenate(
            [flo[pl.ds(b, K, stride=rows), :], fhi[pl.ds(b, K, stride=rows), :]], axis=1
        ).astype(BF16)
        left[b] = dfm
        dhi, dlo = split(dot(dfm, x_ref[b]))
        low[b, :K] = dhi
        low[b, K:] = dlo
        return 0

    lax.fori_loop(0, rows, score_grad, 0, unroll=16)

    def samples(g, _):
        total = jnp.zeros(acc_ref.shape, F32)
        for i in range(4):
            b = g * 4 + i
            dfm, dl = left[b], dl_ref[b]
            total = total + dot(jnp.concatenate([low[b], dl], axis=0), x_ref[b], NT)
            dx[b] = dot(
                jnp.concatenate([dfm, dfm, proj, shared], axis=0),
                jnp.concatenate([s_ref[b], low[b, K:], low[b, :K], dl], axis=0),
                TN,
            )
        acc_ref[...] += total
        return 0

    lax.fori_loop(0, rows // 4, samples, 0, unroll=4)

    def turn(j, _):
        at = pl.ds(pl.multiple_of(j * 16, 16), 16)
        lo = jnp.swapaxes(dx[:, at, :128], 0, 1).astype(BF16)
        hi = jnp.swapaxes(dx[:16, at, 128:] + dx[16:, at, 128:], 0, 1).astype(BF16)
        for i in range(16):
            p = at_ref[j * 16 + i]
            both[p, :rows, :] = lo[i]
            both[p, rows:, :] = hi[i]
        return 0

    lax.fori_loop(0, n // 16, turn, 0)
    keep_ref[:, 0] = both[: n // 2]
    send_ref[:, 0] = both[n // 2 :]


def last(at, x3, s, dl, dfm, wt, rows=32):
    count, n, _ = x3.shape
    nl = dl.shape[1]
    out = pl.BlockSpec((n // 2, 1, rows + rows // 2, 128), lambda i, o: (0, i, 0, 0))
    grid = pltpu.PrefetchScalarGridSpec(
        num_scalar_prefetch=1,
        grid=(count // rows,),
        in_specs=[
            pl.BlockSpec((rows, n, DP), lambda i, o: (i, 0, 0)),
            pl.BlockSpec((rows, 2 * K, DP), lambda i, o: (i, 0, 0)),
            pl.BlockSpec((rows, nl, DP), lambda i, o: (i, 0, 0)),
            pl.BlockSpec((K, rows, n), lambda i, o: (0, i, 0)),
            pl.BlockSpec(wt.shape, lambda i, o: (0, 0)),
        ],
        out_specs=[out, out, pl.BlockSpec((2 * K + nl, n), lambda i, o: (0, 0))],
        scratch_shapes=[pltpu.VMEM((K * rows, 128), F32)] * 2
        + [pltpu.VMEM((rows, n, DP), F32), pltpu.VMEM((n, rows + rows // 2, 128), BF16)]
        + [pltpu.VMEM((rows, K, DP), BF16), pltpu.VMEM((rows, 2 * K, DP), BF16)],
    )
    half = jax.ShapeDtypeStruct((n // 2, count // rows, rows + rows // 2, 128), BF16)
    return pl.pallas_call(
        last_kernel,
        grid_spec=grid,
        out_shape=[half, half, jax.ShapeDtypeStruct((2 * K + nl, n), F32)],
        compiler_params=params(),
        cost_estimate=cost(2e10, count * n * DP * 4),
        name="last",
    )(at, x3, s, dl, dfm, wt)


def sums_kernel(at_ref, mine_ref, other_ref, ids_ref, oid_ref, a_ref, b_ref, c_ref, af_ref, ab_ref, bf_ref, bb_ref):
    nx = b_ref.shape[0]
    ny = c_ref.shape[0]
    _, steps, height, _ = mine_ref.shape
    part = height // 3
    count = ids_ref.shape[2]
    rows = 2 * count
    iota = lax.broadcasted_iota(jnp.int32, (rows, count), 0).astype(F32).astype(BF16)
    one, none = jnp.ones((rows, count), BF16), jnp.zeros((rows, count), BF16)
    low = lax.broadcasted_iota(jnp.int32, (1, 128), 1) < 64
    zero = jnp.zeros((part, 128), BF16)

    def column(x, _):
        ahead = lax.rem(x + nx - at_ref[1], nx)
        for y in range(ny):
            pair = x * ny + y
            for t in range(2):
                hot = [
                    jnp.where(iota == r[pair, t : t + 1, :].astype(F32).astype(BF16), one, none)
                    for r in (ids_ref, oid_ref)
                ]
                main, rest = [], []
                for r in (mine_ref, other_ref):
                    for s in range(steps):
                        tail = r[2 * pair + t, s, 2 * part :, :]
                        main.append(r[2 * pair + t, s, : 2 * part, :])
                        rest += [jnp.where(low, tail, zero), jnp.where(low, zero, tail)]
                block = jnp.concatenate(
                    [jnp.concatenate(main, axis=0), jnp.concatenate(rest, axis=0)], axis=1
                )
                out = dot(jnp.concatenate(hot, axis=1), block)
                tail = out[:, 128:] + pltpu.roll(out[:, 128:], 64, 1)
                main = out[:, :128].astype(BF16)
                tail = jnp.where(low, tail[:count], tail[count:]).astype(BF16)
                if t == 0:
                    a_ref[0, ahead, y, :256, :] = main
                    a_ref[0, ahead, y, 256:, :] = tail[:48]
                    b_ref[ahead, 0, y, :80, :] = tail[48:]
                else:
                    b_ref[ahead, 0, y, 80:, :] = main[:192]
                    c_ref[y, 0, x, :64, :] = main[192:]
                    c_ref[y, 0, x, 64:, :] = tail
        return 0

    lax.fori_loop(0, nx, column, 0)
    nz = pl.num_programs(0)
    ahead = lax.rem(pl.program_id(0) + nz - at_ref[0], nz)

    @pl.when(ahead == 2)
    def _():
        af_ref[...] = a_ref[0, :2]
        ab_ref[...] = a_ref[0, 2:]

    @pl.when(ahead < 2)
    def _():
        bf_ref[ahead] = b_ref[2, 0]

    @pl.when(ahead >= 2)
    def _():
        bb_ref[ahead - 2] = b_ref[2, 0]


def sums(at, mine, other, ids, oids, nz=4, nx=4):
    tables, steps, height, _ = mine.shape
    count = ids.shape[2]
    ny = tables // (2 * nz * nx)
    data = pl.BlockSpec((2 * nx * ny, steps, height, 128), lambda z, at: (z, 0, 0, 0))
    index = pl.BlockSpec((nx * ny, 2, count), lambda z, at: (z, 0, 0))
    grid = pltpu.PrefetchScalarGridSpec(
        num_scalar_prefetch=1,
        grid=(nz,),
        in_specs=[data, data, index, index],
        out_specs=[
            pl.BlockSpec(
                (1, nx, ny, 304, 128), lambda z, at: (lax.rem(z + nz - at[0], nz), 0, 0, 0, 0)
            ),
            pl.BlockSpec(
                (nx, 1, ny, 272, 128), lambda z, at: (0, lax.rem(z + nz - at[0], nz), 0, 0, 0)
            ),
            pl.BlockSpec((ny, 1, nx, 192, 128), lambda z, at: (0, z, 0, 0, 0)),
        ]
        + [pl.BlockSpec((2, ny, h, 128), lambda z, at: (0, 0, 0, 0)) for h in (304, 304, 272, 272)],
    )
    return pl.pallas_call(
        sums_kernel,
        grid_spec=grid,
        out_shape=[
            jax.ShapeDtypeStruct((nz, nx, ny, 304, 128), BF16),
            jax.ShapeDtypeStruct((nx, nz, ny, 272, 128), BF16),
            jax.ShapeDtypeStruct((ny, nz, nx, 192, 128), BF16),
        ]
        + [jax.ShapeDtypeStruct((2, ny, h, 128), BF16) for h in (304, 304, 272, 272)],
        compiler_params=params(),
        cost_estimate=cost(1e10, mine.size * 8),
        name="sums",
    )(at, mine, other, ids, oids)


def update_kernel(slot_ref, sum_ref, rows_ref, accum_ref, new_rows_ref, new_accum_ref, acc):
    cores, runs, height, _ = sum_ref.shape
    tables = 2 * cores * runs
    state = rows_ref.shape[1]
    rows = state // tables
    half = rows // 2
    for t in range(tables):
        where = t // 2 // runs, t // 2 % runs
        base = (t % 2) * (height - 384)
        first = slice(t * rows, t * rows + half)
        second = slice(t * rows + half, (t + 1) * rows)
        main = sum_ref[where + (slice(base, base + rows),)].astype(F32).T.astype(BF16)
        tail = sum_ref[where + (slice(base + rows, base + 384),)].astype(F32).T.astype(BF16)
        acc[:128, t * rows : (t + 1) * rows] = main
        acc[128:, first] = tail[:64]
        acc[128:, second] = tail[64:]
    size = 256
    iota = lax.broadcasted_iota(jnp.int32, (size, state), 0)
    slots = slot_ref[...]
    for i in range(state // size):
        at = slice(i * size, (i + 1) * size)
        hot = jnp.where(iota == slots - i * size, 1.0, 0.0).astype(BF16)
        total = dot(acc[...], hot, NT)
        accum = accum_ref[:, at] + jnp.sum(total * total, axis=0, keepdims=True) * (1.0 / D)
        new_accum_ref[:, at] = accum
        new_rows_ref[:, at] = rows_ref[:, at] - LEARN * total / jnp.sqrt(accum)


def update(slots, sums, table_rows, row_accum):
    state = slots.shape[1]
    return pl.pallas_call(
        update_kernel,
        out_shape=[
            jax.ShapeDtypeStruct((D, state), F32),
            jax.ShapeDtypeStruct((1, state), F32),
        ],
        scratch_shapes=[pltpu.VMEM((D, state), BF16)],
        compiler_params=params(),
        cost_estimate=cost(4e9, state * D * 12),
        name="update",
    )(slots, sums, table_rows, row_accum)


def forward(x3, g2, proj, w_lcb):
    wt = jnp.concatenate([proj.T, w_lcb.T], axis=0)
    return (wt,) + tuple(first(x3, g2, wt))


SWAP = [(0, 1), (1, 0)]
WIDE = ("z", "x", "yl")


def gather(a):
    n = 32
    return lax.all_to_all(jnp.broadcast_to(a[None], (n,) + a.shape), WIDE, 0, 0, tiled=True)


def ring_step(axis, by, v):
    n = 4
    return lax.ppermute(v, axis, [(i, (i + by) % n) for i in range(n)])


def add(*terms):
    total = terms[0].astype(F32)
    for term in terms[1:]:
        total = total + term.astype(F32)
    return total.astype(BF16)


def ring_sums(parts, sends=None):
    if sends is None:
        sends = [(v[2, :2], v[2, 2:]) for _, v in parts]
    fore = [ring_step(axis, 1, f) for (axis, _), (f, _) in zip(parts, sends)]
    back = [ring_step(axis, -1, b) for (axis, _), (_, b) in zip(parts, sends)]
    fore = [
        ring_step(axis, 1, add(v[1], jnp.pad(f, ((0, 2),) + ((0, 0),) * (f.ndim - 1))))
        for (axis, v), f in zip(parts, fore)
    ]
    back = [
        ring_step(axis, -1, add(v[3], jnp.pad(b, ((2, 0),) + ((0, 0),) * (b.ndim - 1))))
        for (axis, v), b in zip(parts, back)
    ]
    return [add(v[0], f, b) for (_, v), f, b in zip(parts, fore, back)]


def body(
    samples, out_grad, row_ids, table_owner, slot_map, proj, gain_flat, w_in, w_out, w_lcb,
    table_rows, row_accum,
):
    owners = 32
    count = samples.shape[0]
    per = proj.shape[0]
    n = per * owners
    nl = w_lcb.shape[1]
    core = lax.axis_index("c")
    small = jnp.concatenate([proj, gain_flat.reshape(per, K), w_lcb], axis=1)
    small = jnp.pad(small, ((0, 8), (0, 128 - small.shape[1])))
    shard = jnp.concatenate([w_in, w_out], axis=0)
    rows = shard.shape[0] // 2
    near = jnp.concatenate([lax.dynamic_slice_in_dim(shard, core * rows, rows, 0), small], axis=0)
    x3 = unfold(samples, n, 0)
    g2 = unfold(out_grad, nl, out_grad.shape[1] // D // nl - 1)
    near, x3, g2 = lax.optimization_barrier((gather(near), x3, g2))
    small = near[:, rows : rows + per].reshape(n, 128)
    proj_f = small[:, :K]
    gain_t = small[:, K : 2 * K].T.astype(F32)
    w_lcb_f = small[:, 2 * K : 2 * K + nl]
    far = lax.ppermute(near, "c", SWAP)

    quad = per // 2
    spot = table_owner // per * quad + table_owner % quad
    spot = jnp.where((table_owner % per) // quad == core, spot, spot + n // 2)
    order = jnp.zeros((n,), jnp.int32).at[spot].set(jnp.arange(n, dtype=jnp.int32))
    ids = jnp.take(row_ids.T, order, axis=0).reshape(2, n // 4, 2, count)
    other_ids = lax.ppermute(ids[1], "c", SWAP)

    wt, score, dl, xh, inv = forward(x3, g2, proj_f, w_lcb_f)
    w_keep, w_send, g_gain, dfm = batch(
        core.reshape(1), xh, inv, gain_t, near, far, rows, out_grad
    )
    w_other = lax.ppermute(w_send, "c", SWAP)
    early = 160
    w_first = add(w_keep[:, :early], w_other[:, :early])
    w_second = add(w_keep[:, early:], w_other[:, early:])
    w_first, w_second, dfm = lax.optimization_barrier((w_first, w_second, dfm))
    w_first = lax.all_to_all(w_first, WIDE, 0, 0, tiled=True)
    keep, send, acc = last(spot, x3, score, dl, dfm, wt)
    w_first, send = lax.optimization_barrier((w_first, send))
    little = jnp.concatenate([acc[:K] + acc[K : 2 * K], g_gain, acc[2 * K :]], axis=0)
    little = jnp.pad(little.T, ((0, 0), (0, 128 - little.shape[0]))).reshape(owners, per, 128)
    w_second = jnp.concatenate([w_second, *split(little)], axis=1)
    w_second = lax.all_to_all(w_second, WIDE, 0, 0, tiled=True)

    other = lax.ppermute(send, "c", SWAP)
    at = jnp.stack([lax.axis_index("z"), lax.axis_index("x")]).astype(jnp.int32)
    a, b, c, af, ab, bf, bb = sums(at, keep, other, ids[0], other_ids)
    c, w_second = lax.optimization_barrier((c, w_second))
    a, b = ring_sums([("z", a), ("x", b)], [(af, ab), (bf, bb)])
    c = lax.all_to_all(c, ("yl", "yh"), 0, 0, tiled=True)
    c = jnp.sum(c.astype(F32), axis=0).astype(BF16)
    mixed = jnp.concatenate(
        [jnp.sum(v.astype(F32), axis=0) for v in (w_first, w_second)], axis=0
    )
    mixed = jnp.concatenate([mixed[:rows], mixed[rows:-per] + mixed[-per:]], axis=0)
    a, b, c, mixed = lax.optimization_barrier((a, b, c, mixed))
    c = lax.all_to_all(c.reshape((16,) + c.shape[2:]), ("z", "x"), 0, 0, tiled=True)
    a, b = ring_sums([("x", a), ("z", b)])
    c = jnp.sum(c.astype(F32), axis=0).astype(BF16)
    mixed = mixed + lax.ppermute(mixed, "yh", SWAP)
    swapped = lax.ppermute(mixed, "c", SWAP)
    little = (mixed[rows:] + swapped[rows:])[:, : 2 * K + nl]
    big = jnp.stack([mixed[:rows], swapped[:rows]])
    big = jnp.where(core == 0, big, big[::-1]).reshape(2 * rows, 128)
    a, b, c, big, little = lax.optimization_barrier((a, b, c, big, little))
    ab = jnp.concatenate([a, b], axis=1)
    ab = ab.reshape((2, 1, 2) + ab.shape[1:])
    here = (jnp.arange(2)[:, None] == lax.axis_index("yl")) & (
        jnp.arange(2)[None, :] == lax.axis_index("yh")
    )
    c = jnp.where(here.reshape(2, 1, 2, 1, 1), c, jnp.zeros_like(c))
    both = jnp.concatenate(
        [jnp.broadcast_to(v, (2, 2, 2) + v.shape[3:]) for v in (ab, c)], axis=3
    )
    both = both.reshape((4, 2) + both.shape[3:])
    both = lax.all_to_all(both, ("yl", "yh"), 0, 0, tiled=True)
    mine = jnp.sum(both.astype(F32), axis=0).astype(BF16)
    others = lax.ppermute(mine, "c", SWAP)
    owned = jnp.where(core == 0, jnp.stack([mine, others]), jnp.stack([others, mine]))
    new_rows, new_accum = update(
        slot_map.reshape(1, -1), owned, table_rows.T, row_accum.reshape(1, -1)
    )
    split_at = w_out.shape[0]
    return (
        little[:, :K],
        little[:, K : 2 * K].reshape(-1),
        big[split_at:],
        big[:split_at],
        little[:, 2 * K :],
        new_rows.T,
        new_accum.reshape(-1),
    )


def solution(mesh):
    cube = Mesh(mesh.devices.reshape(4, 4, 2, 2, 2), ("z", "x", "yl", "yh", "c"))
    batch_spec = P(("z", "x", "yl", "yh", "c"), None)
    two, one = P(WIDE, None), P(WIDE)
    in_specs = (batch_spec,) * 3 + (P(), two, two, one, two, two, two, two, one)
    out_specs = (two, one, two, two, two, two, one)
    return jax.shard_map(body, mesh=cube, in_specs=in_specs, out_specs=out_specs, check_vma=False)
```

```python
import functools

import jax
import jax.numpy as jnp
from jax import lax
from jax.experimental import pallas as pl
from jax.experimental.pallas import tpu as pltpu
from jax.sharding import Mesh, PartitionSpec as P

LEARN = 0.1
EPS = 1e-05
F32 = jnp.float32
BF16 = jnp.bfloat16
D = 192
DP = 256
K = 16
NN = (((1,), (0,)), ((), ()))
NT = (((1,), (1,)), ((), ()))
TN = (((0,), (0,)), ((), ()))


def dot(a, b, dims=NN):
    return lax.dot_general(a, b, dims, preferred_element_type=F32)


def params(mib=56):
    return pltpu.CompilerParams(vmem_limit_bytes=mib * 1024 * 1024)


def cost(flops, nbytes):
    return pl.CostEstimate(flops=int(flops), bytes_accessed=int(nbytes), transcendentals=0)


def split(v):
    hi = v.astype(BF16)
    return hi, (v - hi.astype(F32)).astype(BF16)


def unfold_kernel(x_ref, o_ref):
    tables = o_ref.shape[1]
    low = lax.broadcasted_iota(jnp.int32, (1, 1, 128), 2) < 64

    def group(j, _):
        at = pl.ds(pl.multiple_of(j * 16, 16), 16)
        for h in range(2):
            lo, hi = [], []
            part = slice(16 * h, 16 * h + 16)
            for p in range(8):
                v = x_ref[part, pl.ds(pl.multiple_of(j * 3072 + 384 * p, 128), 384)].astype(F32)
                w = pltpu.roll(v, 192, 1)
                lo += [v[:, :128], w[:, :128]]
                if h == 0:
                    hi += [v[:, 128:256], w[:, 128:256]]
                else:
                    hi += [pltpu.roll(v[:, 128:256], 64, 1), v[:, 256:]]
            hi = jnp.swapaxes(jnp.stack(hi), 0, 1)
            hi = jnp.where(low, hi, 0.0) if h == 0 else jnp.where(low, 0.0, hi)
            o_ref[part, at, :128] = jnp.swapaxes(jnp.stack(lo), 0, 1).astype(BF16)
            o_ref[part, at, 128:] = hi.astype(BF16)
        return 0

    lax.fori_loop(0, tables // 16, group, 0)


def unfold(x, tables, first, rows=32):
    count = x.shape[0]
    return pl.pallas_call(
        unfold_kernel,
        grid=(count // rows,),
        in_specs=[pl.BlockSpec((rows, tables * D), lambda i: (i, first))],
        out_specs=pl.BlockSpec((rows, tables, DP), lambda i: (i, 0, 0)),
        out_shape=jax.ShapeDtypeStruct((count, tables, DP), BF16),
        compiler_params=params(),
        cost_estimate=cost(1e9, count * tables * 900),
        name="unfold",
    )(x)


def first_kernel(
    x_ref, g_ref, w_ref, s_ref, dl_ref, xh_ref, inv_ref, lo, hi, lout, fm
):
    rows = x_ref.shape[0]
    n = x_ref.shape[1]
    w = w_ref[...]
    lane = lax.broadcasted_iota(jnp.int32, (1, DP), 1)
    half = (pl.program_id(0) * rows // 16) % 2
    keep = (lane < 128) | ((lane >= 128 + 64 * half) & (lane < 192 + 64 * half))
    total = lambda v: jnp.sum(jnp.sum(v, axis=1, keepdims=True), axis=2, keepdims=True)
    for b in range(rows):
        r = dot(w, x_ref[b])
        shi, slo = split(r[:K])
        s_ref[b, :K, :] = shi
        s_ref[b, K:, :] = slo
        lout[b] = r[K:]
    for b in range(rows):
        f2 = dot(s_ref[b], x_ref[b], NT)
        fm[b] = f2[:K] + f2[K:]
    v = fm[...]
    c = v - total(v) * (1.0 / (K * n))
    inv = 1.0 / jnp.sqrt(total(c * c) * (1.0 / (K * n)) + EPS)
    inv_ref[...] = jnp.broadcast_to(inv.reshape(rows, 1), (rows, 128))
    xh = c * inv
    for b in range(rows):
        lo[pl.ds(b, K, stride=rows), :] = xh[b, :, :128]
        hi[pl.ds(b, K, stride=rows), :] = xh[b, :, 128:]
    for b in range(rows):
        lb = lout[b]
        grad = g_ref[b].astype(F32)
        mid = jnp.where(keep, lb - jnp.sum(lb, axis=1, keepdims=True) * (1.0 / D), 0.0)
        oinv = 1.0 / jnp.sqrt(jnp.sum(mid * mid, axis=1, keepdims=True) * (1.0 / D) + EPS)
        chat = mid * oinv
        gm = jnp.sum(grad, axis=1, keepdims=True) * (1.0 / D)
        gc = jnp.sum(grad * chat, axis=1, keepdims=True) * (1.0 / D)
        dl_ref[b] = jnp.where(keep, oinv * (grad - gm - chat * gc), 0.0).astype(BF16)
    xh_ref[:, :, :128] = lo[...].reshape(K, rows, 128)
    xh_ref[:, :, 128:] = hi[...].reshape(K, rows, 128)


def first(x3, g2, wt, rows=16):
    count, n, _ = x3.shape
    nl = g2.shape[1]
    return pl.pallas_call(
        first_kernel,
        grid=(count // rows,),
        in_specs=[
            pl.BlockSpec((rows, n, DP), lambda i: (i, 0, 0)),
            pl.BlockSpec((rows, nl, DP), lambda i: (i, 0, 0)),
            pl.BlockSpec(wt.shape, lambda i: (0, 0)),
        ],
        out_specs=[
            pl.BlockSpec((rows, 2 * K, DP), lambda i: (i, 0, 0)),
            pl.BlockSpec((rows, nl, DP), lambda i: (i, 0, 0)),
            pl.BlockSpec((K, rows, n), lambda i: (0, i, 0)),
            pl.BlockSpec((rows, 128), lambda i: (i, 0)),
        ],
        out_shape=[
            jax.ShapeDtypeStruct((count, 2 * K, DP), BF16),
            jax.ShapeDtypeStruct((count, nl, DP), BF16),
            jax.ShapeDtypeStruct((K, count, n), F32),
            jax.ShapeDtypeStruct((count, 128), F32),
        ],
        scratch_shapes=[pltpu.VMEM((K * rows, 128), F32)] * 2
        + [pltpu.VMEM((rows, nl, DP), F32), pltpu.VMEM((rows, K, n), F32)],
        compiler_params=params(),
        cost_estimate=cost(2e10, count * n * DP * 2),
        name="first",
    )(x3, g2, wt)


def batch_kernel(
    core_ref, xh_ref, inv_ref, gain_ref, nraw_ref, fraw_ref, near_ref, far_ref, g_ref,
    keep_ref, send_ref, ggain_ref, dfm_ref, pre_s, hid_s, dhid_s, norm_s, e_s, win_ref, gin_s,
):
    step = pl.program_id(0)
    count, n = xh_ref.shape[1], xh_ref.shape[2]
    owners = nraw_ref.shape[0]
    per = n // owners
    first_core = core_ref[0] == 0

    @pl.when(step == 0)
    def _():
        for o in range(owners):
            v = jnp.where(first_core, nraw_ref[o], fraw_ref[o]).astype(F32)
            v = jnp.swapaxes(v.reshape(per, K, 128), 0, 1)
            win_ref[:, o * per : (o + 1) * per, :] = v
        pre = jnp.zeros((count, 128), F32)
        for k in range(K):
            normed = (xh_ref[k] * gain_ref[k : k + 1, :]).astype(BF16)
            norm_s[k] = normed
            pre = pre + dot(normed, win_ref[k].astype(BF16))
        pre_s[...] = pre
        hid_s[...] = (pre / (1.0 + jnp.exp(-pre))).astype(BF16)
        dhid_s[...] = jnp.zeros_like(dhid_s)

    hid = hid_s[...]
    near, far = near_ref[...], far_ref[...]
    lower = jnp.where(first_core, near[:, per * K :], far[:, per * K :])
    w = jnp.concatenate([lower, jnp.where(first_core, far, near)], axis=1).reshape(-1, 128)
    rows = w.shape[0]
    fout = dot(w, hid, NT).reshape(rows // D, D, count)
    grad = g_ref[...].astype(F32).T.reshape(rows // D, D, count)
    mid = fout - jnp.sum(fout, axis=1, keepdims=True) * (1.0 / D)
    oinv = 1.0 / jnp.sqrt(jnp.sum(mid * mid, axis=1, keepdims=True) * (1.0 / D) + EPS)
    chat = mid * oinv
    gm = jnp.sum(grad, axis=1, keepdims=True) * (1.0 / D)
    gc = jnp.sum(grad * chat, axis=1, keepdims=True) * (1.0 / D)
    df = (oinv * (grad - gm - chat * gc)).reshape(rows, count).astype(BF16)
    gout = dot(df, hid).astype(BF16).reshape(near.shape[0], -1, 128)
    at = pl.ds(pl.multiple_of(step * near.shape[0], near.shape[0]), near.shape[0])
    cut = near.shape[1]

    def store(top_ref, bottom_ref):
        top_ref[at] = gout[:, :cut]
        bottom_ref[at, : gout.shape[1] - cut] = gout[:, cut:]

    pl.when(first_core)(lambda: store(keep_ref, send_ref))
    pl.when(jnp.logical_not(first_core))(lambda: store(send_ref, keep_ref))
    dhid_s[...] += dot(w, df, TN)

    @pl.when(step == pl.num_programs(0) - 1)
    def _():
        pre = pre_s[...]
        sig = 1.0 / (1.0 + jnp.exp(-pre))
        dpre = (dhid_s[...].T * sig * (1.0 + pre * (1.0 - sig))).astype(BF16)
        m1 = jnp.zeros((count, n), F32)
        m2 = jnp.zeros((count, n), F32)
        for k in range(K):
            gin_s[k] = dot(norm_s[k], dpre, TN)
            dn = dot(dpre, win_ref[k].astype(BF16), NT)
            xh = xh_ref[k]
            ggain_ref[k : k + 1, :] = jnp.sum(dn * xh, axis=0, keepdims=True)
            e = dn * gain_ref[k : k + 1, :]
            e_s[k] = e
            m1 = m1 + e
            m2 = m2 + e * xh
        a1 = jnp.sum(m1, axis=1, keepdims=True) * (1.0 / (K * n))
        a2 = jnp.sum(m2, axis=1, keepdims=True) * (1.0 / (K * n))
        inv = inv_ref[:, :1]
        for k in range(K):
            dfm_ref[k] = inv * (e_s[k] - a1 - xh_ref[k] * a2)

        def store_in(ref):
            for o in range(owners):
                v = jnp.swapaxes(gin_s[:, o * per : (o + 1) * per, :], 0, 1)
                ref[o, -per * K :] = v.reshape(per * K, 128).astype(BF16)

        pl.when(first_core)(lambda: store_in(send_ref))
        pl.when(jnp.logical_not(first_core))(lambda: store_in(keep_ref))


def batch(core, xh, inv, gain, near, far, half, out_grad, feats=16):
    k, count, n = xh.shape
    owners = near.shape[0]
    per = n // owners * k
    total = owners * (2 * half - per)
    rows = feats * D
    some = rows * owners // total
    whole = lambda shape: pl.BlockSpec(shape, lambda i: (0,) * len(shape))
    return pl.pallas_call(
        batch_kernel,
        grid=(total // rows,),
        in_specs=[
            pl.BlockSpec(memory_space=pltpu.SMEM),
            whole((k, count, n)),
            whole((count, 128)),
            whole((k, n)),
            pl.BlockSpec((owners, per, 128), lambda i: (0, 0, 0)),
            pl.BlockSpec((owners, per, 128), lambda i: (0, 0, 0)),
            pl.BlockSpec((some, half, 128), lambda i: (i, 0, 0)),
            pl.BlockSpec((some, half, 128), lambda i: (i, 0, 0)),
            pl.BlockSpec((count, rows), lambda i: (0, i)),
        ],
        out_specs=[
            whole((owners, half, 128)),
            whole((owners, half, 128)),
            whole((k, n)),
            whole((k, count, n)),
        ],
        out_shape=[
            jax.ShapeDtypeStruct((owners, half, 128), BF16),
            jax.ShapeDtypeStruct((owners, half, 128), BF16),
            jax.ShapeDtypeStruct((k, n), F32),
            jax.ShapeDtypeStruct((k, count, n), F32),
        ],
        scratch_shapes=[
            pltpu.VMEM((count, 128), F32),
            pltpu.VMEM((count, 128), BF16),
            pltpu.VMEM((128, count), F32),
            pltpu.VMEM((k, count, n), BF16),
            pltpu.VMEM((k, count, n), F32),
            pltpu.VMEM((k, n, 128), F32),
            pltpu.VMEM((k, n, 128), F32),
        ],
        compiler_params=params(),
        cost_estimate=cost(2e10, 2e7),
        name="batch",
    )(core, xh, inv, gain, near, far, near, far, out_grad)


def last_kernel(
    at_ref, x_ref, s_ref, dl_ref, dfm_ref, wt_ref, keep_ref, send_ref, acc_ref, flo, fhi, dx, both, left, low
):
    rows, n = x_ref.shape[0], x_ref.shape[1]

    @pl.when(pl.program_id(0) == 0)
    def _():
        acc_ref[...] = jnp.zeros_like(acc_ref)

    flo[...] = dfm_ref[:, :, :128].reshape(K * rows, 128)
    fhi[...] = dfm_ref[:, :, 128:].reshape(K * rows, 128)
    proj = wt_ref[:K, :]
    shared = wt_ref[...]

    def score_grad(b, _):
        dfm = jnp.concatenate(
            [flo[pl.ds(b, K, stride=rows), :], fhi[pl.ds(b, K, stride=rows), :]], axis=1
        ).astype(BF16)
        left[b] = dfm
        dhi, dlo = split(dot(dfm, x_ref[b]))
        low[b, :K] = dhi
        low[b, K:] = dlo
        return 0

    lax.fori_loop(0, rows, score_grad, 0, unroll=16)

    def samples(g, _):
        total = jnp.zeros(acc_ref.shape, F32)
        for i in range(4):
            b = g * 4 + i
            dfm, dl = left[b], dl_ref[b]
            total = total + dot(jnp.concatenate([low[b], dl], axis=0), x_ref[b], NT)
            dx[b] = dot(
                jnp.concatenate([dfm, dfm, proj, shared], axis=0),
                jnp.concatenate([s_ref[b], low[b, K:], low[b, :K], dl], axis=0),
                TN,
            )
        acc_ref[...] += total
        return 0

    lax.fori_loop(0, rows // 4, samples, 0, unroll=4)

    def turn(j, _):
        at = pl.ds(pl.multiple_of(j * 16, 16), 16)
        lo = jnp.swapaxes(dx[:, at, :128], 0, 1).astype(BF16)
        hi = jnp.swapaxes(dx[:16, at, 128:] + dx[16:, at, 128:], 0, 1).astype(BF16)
        for i in range(16):
            p = at_ref[j * 16 + i]
            both[p, :rows, :] = lo[i]
            both[p, rows:, :] = hi[i]
        return 0

    lax.fori_loop(0, n // 16, turn, 0)
    keep_ref[:, 0] = both[: n // 2]
    send_ref[:, 0] = both[n // 2 :]


def last(at, x3, s, dl, dfm, wt, rows=32):
    count, n, _ = x3.shape
    nl = dl.shape[1]
    out = pl.BlockSpec((n // 2, 1, rows + rows // 2, 128), lambda i, o: (0, i, 0, 0))
    grid = pltpu.PrefetchScalarGridSpec(
        num_scalar_prefetch=1,
        grid=(count // rows,),
        in_specs=[
            pl.BlockSpec((rows, n, DP), lambda i, o: (i, 0, 0)),
            pl.BlockSpec((rows, 2 * K, DP), lambda i, o: (i, 0, 0)),
            pl.BlockSpec((rows, nl, DP), lambda i, o: (i, 0, 0)),
            pl.BlockSpec((K, rows, n), lambda i, o: (0, i, 0)),
            pl.BlockSpec(wt.shape, lambda i, o: (0, 0)),
        ],
        out_specs=[out, out, pl.BlockSpec((2 * K + nl, n), lambda i, o: (0, 0))],
        scratch_shapes=[pltpu.VMEM((K * rows, 128), F32)] * 2
        + [pltpu.VMEM((rows, n, DP), F32), pltpu.VMEM((n, rows + rows // 2, 128), BF16)]
        + [pltpu.VMEM((rows, K, DP), BF16), pltpu.VMEM((rows, 2 * K, DP), BF16)],
    )
    half = jax.ShapeDtypeStruct((n // 2, count // rows, rows + rows // 2, 128), BF16)
    return pl.pallas_call(
        last_kernel,
        grid_spec=grid,
        out_shape=[half, half, jax.ShapeDtypeStruct((2 * K + nl, n), F32)],
        compiler_params=params(),
        cost_estimate=cost(2e10, count * n * DP * 4),
        name="last",
    )(at, x3, s, dl, dfm, wt)


def sums_kernel(at_ref, mine_ref, other_ref, ids_ref, oid_ref, a_ref, b_ref, c_ref, af_ref, ab_ref, bf_ref, bb_ref):
    nx = b_ref.shape[0]
    ny = c_ref.shape[0]
    _, steps, height, _ = mine_ref.shape
    part = height // 3
    count = ids_ref.shape[2]
    rows = 2 * count
    iota = lax.broadcasted_iota(jnp.int32, (rows, count), 0).astype(F32).astype(BF16)
    one, none = jnp.ones((rows, count), BF16), jnp.zeros((rows, count), BF16)
    low = lax.broadcasted_iota(jnp.int32, (1, 128), 1) < 64
    zero = jnp.zeros((part, 128), BF16)

    def column(x, _):
        ahead = lax.rem(x + nx - at_ref[1], nx)
        for y in range(ny):
            pair = x * ny + y
            for t in range(2):
                hot = [
                    jnp.where(iota == r[pair, t : t + 1, :].astype(F32).astype(BF16), one, none)
                    for r in (ids_ref, oid_ref)
                ]
                main, rest = [], []
                for r in (mine_ref, other_ref):
                    for s in range(steps):
                        tail = r[2 * pair + t, s, 2 * part :, :]
                        main.append(r[2 * pair + t, s, : 2 * part, :])
                        rest += [jnp.where(low, tail, zero), jnp.where(low, zero, tail)]
                block = jnp.concatenate(
                    [jnp.concatenate(main, axis=0), jnp.concatenate(rest, axis=0)], axis=1
                )
                out = dot(jnp.concatenate(hot, axis=1), block)
                tail = out[:, 128:] + pltpu.roll(out[:, 128:], 64, 1)
                main = out[:, :128].astype(BF16)
                tail = jnp.where(low, tail[:count], tail[count:]).astype(BF16)
                if t == 0:
                    a_ref[0, ahead, y, :256, :] = main
                    a_ref[0, ahead, y, 256:, :] = tail[:48]
                    b_ref[ahead, 0, y, :80, :] = tail[48:]
                else:
                    b_ref[ahead, 0, y, 80:, :] = main[:192]
                    c_ref[y, 0, x, :64, :] = main[192:]
                    c_ref[y, 0, x, 64:, :] = tail
        return 0

    lax.fori_loop(0, nx, column, 0)
    nz = pl.num_programs(0)
    ahead = lax.rem(pl.program_id(0) + nz - at_ref[0], nz)

    @pl.when(ahead == 2)
    def _():
        af_ref[...] = a_ref[0, :2]
        ab_ref[...] = a_ref[0, 2:]

    @pl.when(ahead < 2)
    def _():
        bf_ref[ahead] = b_ref[2, 0]

    @pl.when(ahead >= 2)
    def _():
        bb_ref[ahead - 2] = b_ref[2, 0]


def sums(at, mine, other, ids, oids, nz=4, nx=4):
    tables, steps, height, _ = mine.shape
    count = ids.shape[2]
    ny = tables // (2 * nz * nx)
    data = pl.BlockSpec((2 * nx * ny, steps, height, 128), lambda z, at: (z, 0, 0, 0))
    index = pl.BlockSpec((nx * ny, 2, count), lambda z, at: (z, 0, 0))
    grid = pltpu.PrefetchScalarGridSpec(
        num_scalar_prefetch=1,
        grid=(nz,),
        in_specs=[data, data, index, index],
        out_specs=[
            pl.BlockSpec(
                (1, nx, ny, 304, 128), lambda z, at: (lax.rem(z + nz - at[0], nz), 0, 0, 0, 0)
            ),
            pl.BlockSpec(
                (nx, 1, ny, 272, 128), lambda z, at: (0, lax.rem(z + nz - at[0], nz), 0, 0, 0)
            ),
            pl.BlockSpec((ny, 1, nx, 192, 128), lambda z, at: (0, z, 0, 0, 0)),
        ]
        + [pl.BlockSpec((2, ny, h, 128), lambda z, at: (0, 0, 0, 0)) for h in (304, 304, 272, 272)],
    )
    return pl.pallas_call(
        sums_kernel,
        grid_spec=grid,
        out_shape=[
            jax.ShapeDtypeStruct((nz, nx, ny, 304, 128), BF16),
            jax.ShapeDtypeStruct((nx, nz, ny, 272, 128), BF16),
            jax.ShapeDtypeStruct((ny, nz, nx, 192, 128), BF16),
        ]
        + [jax.ShapeDtypeStruct((2, ny, h, 128), BF16) for h in (304, 304, 272, 272)],
        compiler_params=params(),
        cost_estimate=cost(1e10, mine.size * 8),
        name="sums",
    )(at, mine, other, ids, oids)


def update_kernel(slot_ref, sum_ref, rows_ref, accum_ref, new_rows_ref, new_accum_ref, acc):
    cores, runs, height, _ = sum_ref.shape
    tables = 2 * cores * runs
    state = rows_ref.shape[1]
    rows = state // tables
    half = rows // 2
    for t in range(tables):
        where = t // 2 // runs, t // 2 % runs
        base = (t % 2) * (height - 384)
        first = slice(t * rows, t * rows + half)
        second = slice(t * rows + half, (t + 1) * rows)
        main = sum_ref[where + (slice(base, base + rows),)].astype(F32).T.astype(BF16)
        tail = sum_ref[where + (slice(base + rows, base + 384),)].astype(F32).T.astype(BF16)
        acc[:128, t * rows : (t + 1) * rows] = main
        acc[128:, first] = tail[:64]
        acc[128:, second] = tail[64:]
    size = 256
    iota = lax.broadcasted_iota(jnp.int32, (size, state), 0)
    slots = slot_ref[...]
    for i in range(state // size):
        at = slice(i * size, (i + 1) * size)
        hot = jnp.where(iota == slots - i * size, 1.0, 0.0).astype(BF16)
        total = dot(acc[...], hot, NT)
        accum = accum_ref[:, at] + jnp.sum(total * total, axis=0, keepdims=True) * (1.0 / D)
        new_accum_ref[:, at] = accum
        new_rows_ref[:, at] = rows_ref[:, at] - LEARN * total / jnp.sqrt(accum)


def update(slots, sums, table_rows, row_accum):
    state = slots.shape[1]
    return pl.pallas_call(
        update_kernel,
        out_shape=[
            jax.ShapeDtypeStruct((D, state), F32),
            jax.ShapeDtypeStruct((1, state), F32),
        ],
        scratch_shapes=[pltpu.VMEM((D, state), BF16)],
        compiler_params=params(),
        cost_estimate=cost(4e9, state * D * 12),
        name="update",
    )(slots, sums, table_rows, row_accum)


def forward(x3, g2, proj, w_lcb):
    wt = jnp.concatenate([proj.T, w_lcb.T], axis=0)
    return (wt,) + tuple(first(x3, g2, wt))


SWAP = [(0, 1), (1, 0)]
WIDE = ("z", "x", "yl")


def gather(a):
    n = 32
    return lax.all_to_all(jnp.broadcast_to(a[None], (n,) + a.shape), WIDE, 0, 0, tiled=True)


def ring_step(axis, by, v):
    n = 4
    return lax.ppermute(v, axis, [(i, (i + by) % n) for i in range(n)])


def add(*terms):
    total = terms[0].astype(F32)
    for term in terms[1:]:
        total = total + term.astype(F32)
    return total.astype(BF16)


def ring_sums(parts, sends=None):
    if sends is None:
        sends = [(v[2, :2], v[2, 2:]) for _, v in parts]
    fore = [ring_step(axis, 1, f) for (axis, _), (f, _) in zip(parts, sends)]
    back = [ring_step(axis, -1, b) for (axis, _), (_, b) in zip(parts, sends)]
    fore = [
        ring_step(axis, 1, add(v[1], jnp.pad(f, ((0, 2),) + ((0, 0),) * (f.ndim - 1))))
        for (axis, v), f in zip(parts, fore)
    ]
    back = [
        ring_step(axis, -1, add(v[3], jnp.pad(b, ((2, 0),) + ((0, 0),) * (b.ndim - 1))))
        for (axis, v), b in zip(parts, back)
    ]
    return [add(v[0], f, b) for (_, v), f, b in zip(parts, fore, back)]


def body(
    samples, out_grad, row_ids, table_owner, slot_map, proj, gain_flat, w_in, w_out, w_lcb,
    table_rows, row_accum,
):
    owners = 32
    count = samples.shape[0]
    per = proj.shape[0]
    n = per * owners
    nl = w_lcb.shape[1]
    core = lax.axis_index("c")
    small = jnp.concatenate([proj, gain_flat.reshape(per, K), w_lcb], axis=1)
    small = jnp.pad(small, ((0, 8), (0, 128 - small.shape[1])))
    shard = jnp.concatenate([w_in, w_out], axis=0)
    rows = shard.shape[0] // 2
    near = jnp.concatenate([lax.dynamic_slice_in_dim(shard, core * rows, rows, 0), small], axis=0)
    x3 = unfold(samples, n, 0)
    g2 = unfold(out_grad, nl, out_grad.shape[1] // D // nl - 1)
    near, x3, g2 = lax.optimization_barrier((gather(near), x3, g2))
    small = near[:, rows : rows + per].reshape(n, 128)
    proj_f = small[:, :K]
    gain_t = small[:, K : 2 * K].T.astype(F32)
    w_lcb_f = small[:, 2 * K : 2 * K + nl]
    far = lax.ppermute(near, "c", SWAP)

    quad = per // 2
    spot = table_owner // per * quad + table_owner % quad
    spot = jnp.where((table_owner % per) // quad == core, spot, spot + n // 2)
    order = jnp.zeros((n,), jnp.int32).at[spot].set(jnp.arange(n, dtype=jnp.int32))
    ids = jnp.take(row_ids.T, order, axis=0).reshape(2, n // 4, 2, count)
    other_ids = lax.ppermute(ids[1], "c", SWAP)

    wt, score, dl, xh, inv = forward(x3, g2, proj_f, w_lcb_f)
    w_keep, w_send, g_gain, dfm = batch(
        core.reshape(1), xh, inv, gain_t, near, far, rows, out_grad
    )
    w_other = lax.ppermute(w_send, "c", SWAP)
    early = 160
    w_first = add(w_keep[:, :early], w_other[:, :early])
    w_second = add(w_keep[:, early:], w_other[:, early:])
    w_first, w_second, dfm = lax.optimization_barrier((w_first, w_second, dfm))
    w_first = lax.all_to_all(w_first, WIDE, 0, 0, tiled=True)
    keep, send, acc = last(spot, x3, score, dl, dfm, wt)
    w_first, send = lax.optimization_barrier((w_first, send))
    little = jnp.concatenate([acc[:K] + acc[K : 2 * K], g_gain, acc[2 * K :]], axis=0)
    little = jnp.pad(little.T, ((0, 0), (0, 128 - little.shape[0]))).reshape(owners, per, 128)
    w_second = jnp.concatenate([w_second, *split(little)], axis=1)
    w_second = lax.all_to_all(w_second, WIDE, 0, 0, tiled=True)

    other = lax.ppermute(send, "c", SWAP)
    at = jnp.stack([lax.axis_index("z"), lax.axis_index("x")]).astype(jnp.int32)
    a, b, c, af, ab, bf, bb = sums(at, keep, other, ids[0], other_ids)
    c, w_second = lax.optimization_barrier((c, w_second))
    a, b = ring_sums([("z", a), ("x", b)], [(af, ab), (bf, bb)])
    c = lax.all_to_all(c, ("yl", "yh"), 0, 0, tiled=True)
    c = jnp.sum(c.astype(F32), axis=0).astype(BF16)
    mixed = jnp.concatenate(
        [jnp.sum(v.astype(F32), axis=0) for v in (w_first, w_second)], axis=0
    )
    mixed = jnp.concatenate([mixed[:rows], mixed[rows:-per] + mixed[-per:]], axis=0)
    a, b, c, mixed = lax.optimization_barrier((a, b, c, mixed))
    c = lax.all_to_all(c.reshape((16,) + c.shape[2:]), ("z", "x"), 0, 0, tiled=True)
    a, b = ring_sums([("x", a), ("z", b)])
    c = jnp.sum(c.astype(F32), axis=0).astype(BF16)
    mixed = mixed + lax.ppermute(mixed, "yh", SWAP)
    swapped = lax.ppermute(mixed, "c", SWAP)
    little = (mixed[rows:] + swapped[rows:])[:, : 2 * K + nl]
    big = jnp.stack([mixed[:rows], swapped[:rows]])
    big = jnp.where(core == 0, big, big[::-1]).reshape(2 * rows, 128)
    c_far = lax.ppermute(c, "yh", SWAP)
    near_first = lax.axis_index("yh") == 0
    c = jnp.stack([jnp.where(near_first, c, c_far), jnp.where(near_first, c_far, c)])
    a, b, c, big, little = lax.optimization_barrier((a, b, c, big, little))
    ab = jnp.concatenate([a, b], axis=1)
    ab = jnp.broadcast_to(ab.reshape((2, 1, 2) + ab.shape[1:]), (2, 2, 2) + ab.shape[1:])
    ab = ab.reshape((4, 2) + ab.shape[3:])
    ab = lax.all_to_all(ab, ("yl", "yh"), 0, 0, tiled=True)
    ab = jnp.sum(ab.astype(F32), axis=0).astype(BF16)
    mine = jnp.concatenate([ab, c], axis=1)
    others = lax.ppermute(mine, "c", SWAP)
    owned = jnp.where(core == 0, jnp.stack([mine, others]), jnp.stack([others, mine]))
    new_rows, new_accum = update(
        slot_map.reshape(1, -1), owned, table_rows.T, row_accum.reshape(1, -1)
    )
    split_at = w_out.shape[0]
    return (
        little[:, :K],
        little[:, K : 2 * K].reshape(-1),
        big[split_at:],
        big[:split_at],
        little[:, 2 * K :],
        new_rows.T,
        new_accum.reshape(-1),
    )


def solution(mesh):
    cube = Mesh(mesh.devices.reshape(4, 4, 2, 2, 2), ("z", "x", "yl", "yh", "c"))
    batch_spec = P(("z", "x", "yl", "yh", "c"), None)
    two, one = P(WIDE, None), P(WIDE)
    in_specs = (batch_spec,) * 3 + (P(), two, two, one, two, two, two, two, one)
    out_specs = (two, one, two, two, two, two, one)
    return jax.shard_map(body, mesh=cube, in_specs=in_specs, out_specs=out_specs, check_vma=False)
```

```python
import functools

import jax
import jax.numpy as jnp
from jax import lax
from jax.experimental import pallas as pl
from jax.experimental.pallas import tpu as pltpu
from jax.sharding import Mesh, PartitionSpec as P

LEARN = 0.1
EPS = 1e-05
F32 = jnp.float32
BF16 = jnp.bfloat16
D = 192
DP = 256
K = 16
NN = (((1,), (0,)), ((), ()))
NT = (((1,), (1,)), ((), ()))
TN = (((0,), (0,)), ((), ()))


def dot(a, b, dims=NN):
    return lax.dot_general(a, b, dims, preferred_element_type=F32)


def params(mib=56):
    return pltpu.CompilerParams(vmem_limit_bytes=mib * 1024 * 1024)


def cost(flops, nbytes):
    return pl.CostEstimate(flops=int(flops), bytes_accessed=int(nbytes), transcendentals=0)


def split(v):
    hi = v.astype(BF16)
    return hi, (v - hi.astype(F32)).astype(BF16)


def unfold_kernel(x_ref, o_ref):
    tables = o_ref.shape[1]
    low = lax.broadcasted_iota(jnp.int32, (1, 1, 128), 2) < 64

    def group(j, _):
        at = pl.ds(pl.multiple_of(j * 16, 16), 16)
        for h in range(2):
            lo, hi = [], []
            part = slice(16 * h, 16 * h + 16)
            for p in range(8):
                v = x_ref[part, pl.ds(pl.multiple_of(j * 3072 + 384 * p, 128), 384)].astype(F32)
                w = pltpu.roll(v, 192, 1)
                lo += [v[:, :128], w[:, :128]]
                if h == 0:
                    hi += [v[:, 128:256], w[:, 128:256]]
                else:
                    hi += [pltpu.roll(v[:, 128:256], 64, 1), v[:, 256:]]
            hi = jnp.swapaxes(jnp.stack(hi), 0, 1)
            hi = jnp.where(low, hi, 0.0) if h == 0 else jnp.where(low, 0.0, hi)
            o_ref[part, at, :128] = jnp.swapaxes(jnp.stack(lo), 0, 1).astype(BF16)
            o_ref[part, at, 128:] = hi.astype(BF16)
        return 0

    lax.fori_loop(0, tables // 16, group, 0)


def unfold(x, tables, first, rows=32):
    count = x.shape[0]
    return pl.pallas_call(
        unfold_kernel,
        grid=(count // rows,),
        in_specs=[pl.BlockSpec((rows, tables * D), lambda i: (i, first))],
        out_specs=pl.BlockSpec((rows, tables, DP), lambda i: (i, 0, 0)),
        out_shape=jax.ShapeDtypeStruct((count, tables, DP), BF16),
        compiler_params=params(),
        cost_estimate=cost(1e9, count * tables * 900),
        name="unfold",
    )(x)


def first_kernel(
    x_ref, g_ref, w_ref, s_ref, dl_ref, xh_ref, inv_ref, lo, hi, lout, fm
):
    rows = x_ref.shape[0]
    n = x_ref.shape[1]
    w = w_ref[...]
    lane = lax.broadcasted_iota(jnp.int32, (1, DP), 1)
    half = (pl.program_id(0) * rows // 16) % 2
    keep = (lane < 128) | ((lane >= 128 + 64 * half) & (lane < 192 + 64 * half))
    total = lambda v: jnp.sum(jnp.sum(v, axis=1, keepdims=True), axis=2, keepdims=True)
    for b in range(rows):
        r = dot(w, x_ref[b])
        shi, slo = split(r[:K])
        s_ref[b, :K, :] = shi
        s_ref[b, K:, :] = slo
        lout[b] = r[K:]
    for b in range(rows):
        f2 = dot(s_ref[b], x_ref[b], NT)
        fm[b] = f2[:K] + f2[K:]
    v = fm[...]
    c = v - total(v) * (1.0 / (K * n))
    inv = 1.0 / jnp.sqrt(total(c * c) * (1.0 / (K * n)) + EPS)
    inv_ref[...] = jnp.broadcast_to(inv.reshape(rows, 1), (rows, 128))
    xh = c * inv
    for b in range(rows):
        lo[pl.ds(b, K, stride=rows), :] = xh[b, :, :128]
        hi[pl.ds(b, K, stride=rows), :] = xh[b, :, 128:]
    for b in range(rows):
        lb = lout[b]
        grad = g_ref[b].astype(F32)
        mid = jnp.where(keep, lb - jnp.sum(lb, axis=1, keepdims=True) * (1.0 / D), 0.0)
        oinv = 1.0 / jnp.sqrt(jnp.sum(mid * mid, axis=1, keepdims=True) * (1.0 / D) + EPS)
        chat = mid * oinv
        gm = jnp.sum(grad, axis=1, keepdims=True) * (1.0 / D)
        gc = jnp.sum(grad * chat, axis=1, keepdims=True) * (1.0 / D)
        dl_ref[b] = jnp.where(keep, oinv * (grad - gm - chat * gc), 0.0).astype(BF16)
    xh_ref[:, :, :128] = lo[...].reshape(K, rows, 128)
    xh_ref[:, :, 128:] = hi[...].reshape(K, rows, 128)


def first(x3, g2, wt, rows=16):
    count, n, _ = x3.shape
    nl = g2.shape[1]
    return pl.pallas_call(
        first_kernel,
        grid=(count // rows,),
        in_specs=[
            pl.BlockSpec((rows, n, DP), lambda i: (i, 0, 0)),
            pl.BlockSpec((rows, nl, DP), lambda i: (i, 0, 0)),
            pl.BlockSpec(wt.shape, lambda i: (0, 0)),
        ],
        out_specs=[
            pl.BlockSpec((rows, 2 * K, DP), lambda i: (i, 0, 0)),
            pl.BlockSpec((rows, nl, DP), lambda i: (i, 0, 0)),
            pl.BlockSpec((K, rows, n), lambda i: (0, i, 0)),
            pl.BlockSpec((rows, 128), lambda i: (i, 0)),
        ],
        out_shape=[
            jax.ShapeDtypeStruct((count, 2 * K, DP), BF16),
            jax.ShapeDtypeStruct((count, nl, DP), BF16),
            jax.ShapeDtypeStruct((K, count, n), F32),
            jax.ShapeDtypeStruct((count, 128), F32),
        ],
        scratch_shapes=[pltpu.VMEM((K * rows, 128), F32)] * 2
        + [pltpu.VMEM((rows, nl, DP), F32), pltpu.VMEM((rows, K, n), F32)],
        compiler_params=params(),
        cost_estimate=cost(2e10, count * n * DP * 2),
        name="first",
    )(x3, g2, wt)


def batch_kernel(
    core_ref, xh_ref, inv_ref, gain_ref, nraw_ref, fraw_ref, near_ref, far_ref, g_ref,
    keep_ref, send_ref, ggain_ref, dfm_ref, pre_s, hid_s, dhid_s, norm_s, e_s, win_ref, gin_s,
):
    step = pl.program_id(0)
    count, n = xh_ref.shape[1], xh_ref.shape[2]
    owners = nraw_ref.shape[0]
    per = n // owners
    first_core = core_ref[0] == 0

    @pl.when(step == 0)
    def _():
        for o in range(owners):
            v = jnp.where(first_core, nraw_ref[o], fraw_ref[o]).astype(F32)
            v = jnp.swapaxes(v.reshape(per, K, 128), 0, 1)
            win_ref[:, o * per : (o + 1) * per, :] = v
        pre = jnp.zeros((count, 128), F32)
        for k in range(K):
            normed = (xh_ref[k] * gain_ref[k : k + 1, :]).astype(BF16)
            norm_s[k] = normed
            pre = pre + dot(normed, win_ref[k].astype(BF16))
        pre_s[...] = pre
        hid_s[...] = (pre / (1.0 + jnp.exp(-pre))).astype(BF16)
        dhid_s[...] = jnp.zeros_like(dhid_s)

    hid = hid_s[...]
    near, far = near_ref[...], far_ref[...]
    lower = jnp.where(first_core, near[:, per * K :], far[:, per * K :])
    w = jnp.concatenate([lower, jnp.where(first_core, far, near)], axis=1).reshape(-1, 128)
    rows = w.shape[0]
    fout = dot(w, hid, NT).reshape(rows // D, D, count)
    grad = g_ref[...].astype(F32).T.reshape(rows // D, D, count)
    mid = fout - jnp.sum(fout, axis=1, keepdims=True) * (1.0 / D)
    oinv = 1.0 / jnp.sqrt(jnp.sum(mid * mid, axis=1, keepdims=True) * (1.0 / D) + EPS)
    chat = mid * oinv
    gm = jnp.sum(grad, axis=1, keepdims=True) * (1.0 / D)
    gc = jnp.sum(grad * chat, axis=1, keepdims=True) * (1.0 / D)
    df = (oinv * (grad - gm - chat * gc)).reshape(rows, count).astype(BF16)
    gout = dot(df, hid).astype(BF16).reshape(near.shape[0], -1, 128)
    at = pl.ds(pl.multiple_of(step * near.shape[0], near.shape[0]), near.shape[0])
    cut = near.shape[1]

    def store(top_ref, bottom_ref):
        top_ref[at] = gout[:, :cut]
        bottom_ref[at, : gout.shape[1] - cut] = gout[:, cut:]

    pl.when(first_core)(lambda: store(keep_ref, send_ref))
    pl.when(jnp.logical_not(first_core))(lambda: store(send_ref, keep_ref))
    dhid_s[...] += dot(w, df, TN)

    @pl.when(step == pl.num_programs(0) - 1)
    def _():
        pre = pre_s[...]
        sig = 1.0 / (1.0 + jnp.exp(-pre))
        dpre = (dhid_s[...].T * sig * (1.0 + pre * (1.0 - sig))).astype(BF16)
        m1 = jnp.zeros((count, n), F32)
        m2 = jnp.zeros((count, n), F32)
        for k in range(K):
            gin_s[k] = dot(norm_s[k], dpre, TN)
            dn = dot(dpre, win_ref[k].astype(BF16), NT)
            xh = xh_ref[k]
            ggain_ref[k : k + 1, :] = jnp.sum(dn * xh, axis=0, keepdims=True)
            e = dn * gain_ref[k : k + 1, :]
            e_s[k] = e
            m1 = m1 + e
            m2 = m2 + e * xh
        a1 = jnp.sum(m1, axis=1, keepdims=True) * (1.0 / (K * n))
        a2 = jnp.sum(m2, axis=1, keepdims=True) * (1.0 / (K * n))
        inv = inv_ref[:, :1]
        for k in range(K):
            dfm_ref[k] = inv * (e_s[k] - a1 - xh_ref[k] * a2)

        def store_in(ref):
            for o in range(owners):
                v = jnp.swapaxes(gin_s[:, o * per : (o + 1) * per, :], 0, 1)
                ref[o, -per * K :] = v.reshape(per * K, 128).astype(BF16)

        pl.when(first_core)(lambda: store_in(send_ref))
        pl.when(jnp.logical_not(first_core))(lambda: store_in(keep_ref))


def batch(core, xh, inv, gain, near, far, half, out_grad, feats=16):
    k, count, n = xh.shape
    owners = near.shape[0]
    per = n // owners * k
    total = owners * (2 * half - per)
    rows = feats * D
    some = rows * owners // total
    whole = lambda shape: pl.BlockSpec(shape, lambda i: (0,) * len(shape))
    return pl.pallas_call(
        batch_kernel,
        grid=(total // rows,),
        in_specs=[
            pl.BlockSpec(memory_space=pltpu.SMEM),
            whole((k, count, n)),
            whole((count, 128)),
            whole((k, n)),
            pl.BlockSpec((owners, per, 128), lambda i: (0, 0, 0)),
            pl.BlockSpec((owners, per, 128), lambda i: (0, 0, 0)),
            pl.BlockSpec((some, half, 128), lambda i: (i, 0, 0)),
            pl.BlockSpec((some, half, 128), lambda i: (i, 0, 0)),
            pl.BlockSpec((count, rows), lambda i: (0, i)),
        ],
        out_specs=[
            whole((owners, half, 128)),
            whole((owners, half, 128)),
            whole((k, n)),
            whole((k, count, n)),
        ],
        out_shape=[
            jax.ShapeDtypeStruct((owners, half, 128), BF16),
            jax.ShapeDtypeStruct((owners, half, 128), BF16),
            jax.ShapeDtypeStruct((k, n), F32),
            jax.ShapeDtypeStruct((k, count, n), F32),
        ],
        scratch_shapes=[
            pltpu.VMEM((count, 128), F32),
            pltpu.VMEM((count, 128), BF16),
            pltpu.VMEM((128, count), F32),
            pltpu.VMEM((k, count, n), BF16),
            pltpu.VMEM((k, count, n), F32),
            pltpu.VMEM((k, n, 128), F32),
            pltpu.VMEM((k, n, 128), F32),
        ],
        compiler_params=params(),
        cost_estimate=cost(2e10, 2e7),
        name="batch",
    )(core, xh, inv, gain, near, far, near, far, out_grad)


def last_kernel(
    at_ref, x_ref, s_ref, dl_ref, dfm_ref, wt_ref, keep_ref, send_ref, acc_ref, flo, fhi, dx, both, left, low
):
    rows, n = x_ref.shape[0], x_ref.shape[1]

    @pl.when(pl.program_id(0) == 0)
    def _():
        acc_ref[...] = jnp.zeros_like(acc_ref)

    flo[...] = dfm_ref[:, :, :128].reshape(K * rows, 128)
    fhi[...] = dfm_ref[:, :, 128:].reshape(K * rows, 128)
    proj = wt_ref[:K, :]
    shared = wt_ref[...]

    def score_grad(b, _):
        dfm = jnp.concatenate(
            [flo[pl.ds(b, K, stride=rows), :], fhi[pl.ds(b, K, stride=rows), :]], axis=1
        ).astype(BF16)
        left[b] = dfm
        dhi, dlo = split(dot(dfm, x_ref[b]))
        low[b, :K] = dhi
        low[b, K:] = dlo
        return 0

    lax.fori_loop(0, rows, score_grad, 0, unroll=16)

    def samples(g, _):
        total = jnp.zeros(acc_ref.shape, F32)
        for i in range(4):
            b = g * 4 + i
            dfm, dl = left[b], dl_ref[b]
            total = total + dot(jnp.concatenate([low[b], dl], axis=0), x_ref[b], NT)
            dx[b] = dot(
                jnp.concatenate([dfm, dfm, proj, shared], axis=0),
                jnp.concatenate([s_ref[b], low[b, K:], low[b, :K], dl], axis=0),
                TN,
            )
        acc_ref[...] += total
        return 0

    lax.fori_loop(0, rows // 4, samples, 0, unroll=4)

    def turn(j, _):
        at = pl.ds(pl.multiple_of(j * 16, 16), 16)
        lo = jnp.swapaxes(dx[:, at, :128], 0, 1).astype(BF16)
        hi = jnp.swapaxes(dx[:16, at, 128:] + dx[16:, at, 128:], 0, 1).astype(BF16)
        for i in range(16):
            p = at_ref[j * 16 + i]
            both[p, :rows, :] = lo[i]
            both[p, rows:, :] = hi[i]
        return 0

    lax.fori_loop(0, n // 16, turn, 0)
    keep_ref[:, 0] = both[: n // 2]
    send_ref[:, 0] = both[n // 2 :]


def last(at, x3, s, dl, dfm, wt, rows=32):
    count, n, _ = x3.shape
    nl = dl.shape[1]
    out = pl.BlockSpec((n // 2, 1, rows + rows // 2, 128), lambda i, o: (0, i, 0, 0))
    grid = pltpu.PrefetchScalarGridSpec(
        num_scalar_prefetch=1,
        grid=(count // rows,),
        in_specs=[
            pl.BlockSpec((rows, n, DP), lambda i, o: (i, 0, 0)),
            pl.BlockSpec((rows, 2 * K, DP), lambda i, o: (i, 0, 0)),
            pl.BlockSpec((rows, nl, DP), lambda i, o: (i, 0, 0)),
            pl.BlockSpec((K, rows, n), lambda i, o: (0, i, 0)),
            pl.BlockSpec(wt.shape, lambda i, o: (0, 0)),
        ],
        out_specs=[out, out, pl.BlockSpec((2 * K + nl, n), lambda i, o: (0, 0))],
        scratch_shapes=[pltpu.VMEM((K * rows, 128), F32)] * 2
        + [pltpu.VMEM((rows, n, DP), F32), pltpu.VMEM((n, rows + rows // 2, 128), BF16)]
        + [pltpu.VMEM((rows, K, DP), BF16), pltpu.VMEM((rows, 2 * K, DP), BF16)],
    )
    half = jax.ShapeDtypeStruct((n // 2, count // rows, rows + rows // 2, 128), BF16)
    return pl.pallas_call(
        last_kernel,
        grid_spec=grid,
        out_shape=[half, half, jax.ShapeDtypeStruct((2 * K + nl, n), F32)],
        compiler_params=params(),
        cost_estimate=cost(2e10, count * n * DP * 4),
        name="last",
    )(at, x3, s, dl, dfm, wt)


def sums_kernel(at_ref, mine_ref, other_ref, ids_ref, oid_ref, a_ref, b_ref, c_ref, af_ref, ab_ref, bf_ref, bb_ref):
    nx = b_ref.shape[0]
    ny = c_ref.shape[0]
    _, steps, height, _ = mine_ref.shape
    part = height // 3
    count = ids_ref.shape[2]
    rows = 2 * count
    iota = lax.broadcasted_iota(jnp.int32, (rows, count), 0).astype(F32).astype(BF16)
    one, none = jnp.ones((rows, count), BF16), jnp.zeros((rows, count), BF16)
    low = lax.broadcasted_iota(jnp.int32, (1, 128), 1) < 64
    zero = jnp.zeros((part, 128), BF16)

    def column(x, _):
        ahead = lax.rem(x + nx - at_ref[1], nx)
        for y in range(ny):
            pair = x * ny + y
            for t in range(2):
                hot = [
                    jnp.where(iota == r[pair, t : t + 1, :].astype(F32).astype(BF16), one, none)
                    for r in (ids_ref, oid_ref)
                ]
                main, rest = [], []
                for r in (mine_ref, other_ref):
                    for s in range(steps):
                        tail = r[2 * pair + t, s, 2 * part :, :]
                        main.append(r[2 * pair + t, s, : 2 * part, :])
                        rest += [jnp.where(low, tail, zero), jnp.where(low, zero, tail)]
                block = jnp.concatenate(
                    [jnp.concatenate(main, axis=0), jnp.concatenate(rest, axis=0)], axis=1
                )
                out = dot(jnp.concatenate(hot, axis=1), block)
                tail = out[:, 128:] + pltpu.roll(out[:, 128:], 64, 1)
                main = out[:, :128].astype(BF16)
                tail = jnp.where(low, tail[:count], tail[count:]).astype(BF16)
                if t == 0:
                    a_ref[0, ahead, y, :256, :] = main
                    a_ref[0, ahead, y, 256:, :] = tail[:48]
                    b_ref[ahead, 0, y, :80, :] = tail[48:]
                else:
                    b_ref[ahead, 0, y, 80:, :] = main[:192]
                    c_ref[y, 0, x, :64, :] = main[192:]
                    c_ref[y, 0, x, 64:, :] = tail
        return 0

    lax.fori_loop(0, nx, column, 0)
    nz = pl.num_programs(0)
    ahead = lax.rem(pl.program_id(0) + nz - at_ref[0], nz)

    @pl.when(ahead == 2)
    def _():
        af_ref[...] = a_ref[0, :2]
        ab_ref[...] = a_ref[0, 2:]

    @pl.when(ahead < 2)
    def _():
        bf_ref[ahead] = b_ref[2, 0]

    @pl.when(ahead >= 2)
    def _():
        bb_ref[ahead - 2] = b_ref[2, 0]


def sums(at, mine, other, ids, oids, nz=4, nx=4):
    tables, steps, height, _ = mine.shape
    count = ids.shape[2]
    ny = tables // (2 * nz * nx)
    data = pl.BlockSpec((2 * nx * ny, steps, height, 128), lambda z, at: (z, 0, 0, 0))
    index = pl.BlockSpec((nx * ny, 2, count), lambda z, at: (z, 0, 0))
    grid = pltpu.PrefetchScalarGridSpec(
        num_scalar_prefetch=1,
        grid=(nz,),
        in_specs=[data, data, index, index],
        out_specs=[
            pl.BlockSpec(
                (1, nx, ny, 304, 128), lambda z, at: (lax.rem(z + nz - at[0], nz), 0, 0, 0, 0)
            ),
            pl.BlockSpec(
                (nx, 1, ny, 272, 128), lambda z, at: (0, lax.rem(z + nz - at[0], nz), 0, 0, 0)
            ),
            pl.BlockSpec((ny, 1, nx, 192, 128), lambda z, at: (0, z, 0, 0, 0)),
        ]
        + [pl.BlockSpec((2, ny, h, 128), lambda z, at: (0, 0, 0, 0)) for h in (304, 304, 272, 272)],
    )
    return pl.pallas_call(
        sums_kernel,
        grid_spec=grid,
        out_shape=[
            jax.ShapeDtypeStruct((nz, nx, ny, 304, 128), BF16),
            jax.ShapeDtypeStruct((nx, nz, ny, 272, 128), BF16),
            jax.ShapeDtypeStruct((ny, nz, nx, 192, 128), BF16),
        ]
        + [jax.ShapeDtypeStruct((2, ny, h, 128), BF16) for h in (304, 304, 272, 272)],
        compiler_params=params(),
        cost_estimate=cost(1e10, mine.size * 8),
        name="sums",
    )(at, mine, other, ids, oids)


def update_kernel(slot_ref, sum_ref, rows_ref, accum_ref, new_rows_ref, new_accum_ref, acc):
    cores, runs, height, _ = sum_ref.shape
    tables = 2 * cores * runs
    state = rows_ref.shape[1]
    rows = state // tables
    half = rows // 2
    for t in range(tables):
        where = t // 2 // runs, t // 2 % runs
        base = (t % 2) * (height - 384)
        first = slice(t * rows, t * rows + half)
        second = slice(t * rows + half, (t + 1) * rows)
        main = sum_ref[where + (slice(base, base + rows),)].astype(F32).T.astype(BF16)
        tail = sum_ref[where + (slice(base + rows, base + 384),)].astype(F32).T.astype(BF16)
        acc[:128, t * rows : (t + 1) * rows] = main
        acc[128:, first] = tail[:64]
        acc[128:, second] = tail[64:]
    size = 256
    iota = lax.broadcasted_iota(jnp.int32, (size, state), 0)
    slots = slot_ref[...]
    for i in range(state // size):
        at = slice(i * size, (i + 1) * size)
        hot = jnp.where(iota == slots - i * size, 1.0, 0.0).astype(BF16)
        total = dot(acc[...], hot, NT)
        accum = accum_ref[:, at] + jnp.sum(total * total, axis=0, keepdims=True) * (1.0 / D)
        new_accum_ref[:, at] = accum
        new_rows_ref[:, at] = rows_ref[:, at] - LEARN * total / jnp.sqrt(accum)


def update(slots, sums, table_rows, row_accum):
    state = slots.shape[1]
    return pl.pallas_call(
        update_kernel,
        out_shape=[
            jax.ShapeDtypeStruct((D, state), F32),
            jax.ShapeDtypeStruct((1, state), F32),
        ],
        scratch_shapes=[pltpu.VMEM((D, state), BF16)],
        compiler_params=params(),
        cost_estimate=cost(4e9, state * D * 12),
        name="update",
    )(slots, sums, table_rows, row_accum)


def forward(x3, g2, proj, w_lcb):
    wt = jnp.concatenate([proj.T, w_lcb.T], axis=0)
    return (wt,) + tuple(first(x3, g2, wt))


SWAP = [(0, 1), (1, 0)]
WIDE = ("z", "x", "yl")


def gather(a):
    n = 32
    return lax.all_to_all(jnp.broadcast_to(a[None], (n,) + a.shape), WIDE, 0, 0, tiled=True)


def ring_step(axis, by, v):
    n = 4
    return lax.ppermute(v, axis, [(i, (i + by) % n) for i in range(n)])


def add(*terms):
    total = terms[0].astype(F32)
    for term in terms[1:]:
        total = total + term.astype(F32)
    return total.astype(BF16)


def ring_sums(parts, sends=None):
    if sends is None:
        sends = [(v[2, :2], v[2, 2:]) for _, v in parts]
    fore = [ring_step(axis, 1, f) for (axis, _), (f, _) in zip(parts, sends)]
    back = [ring_step(axis, -1, b) for (axis, _), (_, b) in zip(parts, sends)]
    fore = [
        ring_step(axis, 1, add(v[1], jnp.pad(f, ((0, 2),) + ((0, 0),) * (f.ndim - 1))))
        for (axis, v), f in zip(parts, fore)
    ]
    back = [
        ring_step(axis, -1, add(v[3], jnp.pad(b, ((2, 0),) + ((0, 0),) * (b.ndim - 1))))
        for (axis, v), b in zip(parts, back)
    ]
    return [add(v[0], f, b) for (_, v), f, b in zip(parts, fore, back)]


def body(
    samples, out_grad, row_ids, table_owner, slot_map, proj, gain_flat, w_in, w_out, w_lcb,
    table_rows, row_accum,
):
    owners = 32
    count = samples.shape[0]
    per = proj.shape[0]
    n = per * owners
    nl = w_lcb.shape[1]
    core = lax.axis_index("c")
    small = jnp.concatenate([proj, gain_flat.reshape(per, K), w_lcb], axis=1)
    small = jnp.pad(small, ((0, 8), (0, 128 - small.shape[1])))
    shard = jnp.concatenate([w_in, w_out], axis=0)
    rows = shard.shape[0] // 2
    near = jnp.concatenate([lax.dynamic_slice_in_dim(shard, core * rows, rows, 0), small], axis=0)
    x3 = unfold(samples, n, 0)
    g2 = unfold(out_grad, nl, out_grad.shape[1] // D // nl - 1)
    quad = per // 2
    spot = table_owner // per * quad + table_owner % quad
    spot = jnp.where((table_owner % per) // quad == core, spot, spot + n // 2)
    order = jnp.zeros((n,), jnp.int32).at[spot].set(jnp.arange(n, dtype=jnp.int32))
    ids = jnp.take(row_ids.T, order, axis=0).reshape(2, n // 4, 2, count)
    other_ids = lax.ppermute(ids[1], "c", SWAP)
    mine_ids = ids[0]
    near, x3, g2, mine_ids, other_ids = lax.optimization_barrier(
        (gather(near), x3, g2, mine_ids, other_ids)
    )
    small = near[:, rows : rows + per].reshape(n, 128)
    proj_f = small[:, :K]
    gain_t = small[:, K : 2 * K].T.astype(F32)
    w_lcb_f = small[:, 2 * K : 2 * K + nl]
    far = lax.ppermute(near, "c", SWAP)


    wt, score, dl, xh, inv = forward(x3, g2, proj_f, w_lcb_f)
    w_keep, w_send, g_gain, dfm = batch(
        core.reshape(1), xh, inv, gain_t, near, far, rows, out_grad
    )
    w_other = lax.ppermute(w_send, "c", SWAP)
    early = 160
    w_first = add(w_keep[:, :early], w_other[:, :early])
    w_second = add(w_keep[:, early:], w_other[:, early:])
    w_first, w_second, dfm = lax.optimization_barrier((w_first, w_second, dfm))
    w_first = lax.all_to_all(w_first, WIDE, 0, 0, tiled=True)
    keep, send, acc = last(spot, x3, score, dl, dfm, wt)
    w_first, send = lax.optimization_barrier((w_first, send))
    little = jnp.concatenate([acc[:K] + acc[K : 2 * K], g_gain, acc[2 * K :]], axis=0)
    little = jnp.pad(little.T, ((0, 0), (0, 128 - little.shape[0]))).reshape(owners, per, 128)
    w_second = jnp.concatenate([w_second, *split(little)], axis=1)
    w_second = lax.all_to_all(w_second, WIDE, 0, 0, tiled=True)

    other = lax.ppermute(send, "c", SWAP)
    at = jnp.stack([lax.axis_index("z"), lax.axis_index("x")]).astype(jnp.int32)
    a, b, c, af, ab, bf, bb = sums(at, keep, other, mine_ids, other_ids)
    c, w_second = lax.optimization_barrier((c, w_second))
    a, b = ring_sums([("z", a), ("x", b)], [(af, ab), (bf, bb)])
    c = lax.all_to_all(c, ("yl", "yh"), 0, 0, tiled=True)
    c = jnp.sum(c.astype(F32), axis=0).astype(BF16)
    mixed = jnp.concatenate(
        [jnp.sum(v.astype(F32), axis=0) for v in (w_first, w_second)], axis=0
    )
    mixed = jnp.concatenate([mixed[:rows], mixed[rows:-per] + mixed[-per:]], axis=0)
    a, b, c, mixed = lax.optimization_barrier((a, b, c, mixed))
    c = lax.all_to_all(c.reshape((16,) + c.shape[2:]), ("z", "x"), 0, 0, tiled=True)
    a, b = ring_sums([("x", a), ("z", b)])
    c = jnp.sum(c.astype(F32), axis=0).astype(BF16)
    mixed = mixed + lax.ppermute(mixed, "yh", SWAP)
    swapped = lax.ppermute(mixed, "c", SWAP)
    little = (mixed[rows:] + swapped[rows:])[:, : 2 * K + nl]
    big = jnp.stack([mixed[:rows], swapped[:rows]])
    big = jnp.where(core == 0, big, big[::-1]).reshape(2 * rows, 128)
    c_far = lax.ppermute(c, "yh", SWAP)
    near_first = lax.axis_index("yh") == 0
    c = jnp.stack([jnp.where(near_first, c, c_far), jnp.where(near_first, c_far, c)])
    a, b, c, big, little = lax.optimization_barrier((a, b, c, big, little))
    ab = jnp.concatenate([a, b], axis=1)
    ab = jnp.broadcast_to(ab.reshape((2, 1, 2) + ab.shape[1:]), (2, 2, 2) + ab.shape[1:])
    ab = ab.reshape((4, 2) + ab.shape[3:])
    ab = lax.all_to_all(ab, ("yl", "yh"), 0, 0, tiled=True)
    ab = jnp.sum(ab.astype(F32), axis=0).astype(BF16)
    mine = jnp.concatenate([ab, c], axis=1)
    others = lax.ppermute(mine, "c", SWAP)
    owned = jnp.where(core == 0, jnp.stack([mine, others]), jnp.stack([others, mine]))
    new_rows, new_accum = update(
        slot_map.reshape(1, -1), owned, table_rows.T, row_accum.reshape(1, -1)
    )
    split_at = w_out.shape[0]
    return (
        little[:, :K],
        little[:, K : 2 * K].reshape(-1),
        big[split_at:],
        big[:split_at],
        little[:, 2 * K :],
        new_rows.T,
        new_accum.reshape(-1),
    )


def solution(mesh):
    cube = Mesh(mesh.devices.reshape(4, 4, 2, 2, 2), ("z", "x", "yl", "yh", "c"))
    batch_spec = P(("z", "x", "yl", "yh", "c"), None)
    two, one = P(WIDE, None), P(WIDE)
    in_specs = (batch_spec,) * 3 + (P(), two, two, one, two, two, two, two, one)
    out_specs = (two, one, two, two, two, two, one)
    return jax.shard_map(body, mesh=cube, in_specs=in_specs, out_specs=out_specs, check_vma=False)
```
